32 devices in a mesh: grp: 4 (over y, x), blk: 8 (over z, core).
Axes of the slice: x: 2, y: 2, z: 4, core: 2. Of those that a mesh axis runs over, the one named last changes fastest.
Arguments:
- queries: bfloat16 [4096, 4096], P(('grp', 'blk')), may hold values from -4 to 4
- passages: bfloat16 [4096, 4096], P(('grp', 'blk')), may hold values from -1 to 1
- hard_index: int32 [4096, 3], P(('grp', 'blk')), may hold values from 0 to 4095, as said below
- weights: float32 [4096], P(('grp', 'blk')), may hold values from 0.5 to 2
Outputs:
- loss_rows: float32 [4096], P(('grp', 'blk'))
- grad_queries: bfloat16 [4096, 4096], P(('grp', 'blk'))
- grad_passages: bfloat16 [4096, 4096], P(('grp', 'blk'))
The draws below stay inside these ranges and needn't reach their ends.
Inputs may be any that keep to these rules, and one draw needn't show every extreme that they name: `hard_index`: the three entries of query i name passages of the block at the same index of blk as query i in three different groups, none its own; among the queries of one device at most 128 entries name one group, and in every device exactly 128 entries name some group.
All inputs are finite; a program needn't handle non-finite values.
Results may differ from the reference program's by a relative error of at most 0.0065.
Values may be sent and summed in bfloat16 or wider, within the bound.
No kernel may reach another device: no remote copies, remote signals or barrier semaphores. Data moves between devices by JAX's collectives and lax.ppermute only.
A program may use at most 64 MiB of HBM per device.

```python
import math
import jax
import jax.numpy as jnp
from jax import lax

D = 4096
ROWS = 128
WINDOW = 4
GROUPS = 4
LOOP = 8
TOTAL = 4096
CAP = 128


def base_passages(key):
    total_rows = GROUPS * LOOP * ROWS
    raw_values = jax.random.normal(jax.random.fold_in(key, 11), (total_rows, D), jnp.float32) * D ** (-0.5)
    return jnp.clip(raw_values, -1.0, 1.0)


def hard_targets(key):
    blocks = GROUPS * LOOP
    others = GROUPS - 1

    def per_block(block_key, block_id):
        key_order = jax.random.fold_in(block_key, 1)
        key_rows = jax.random.fold_in(block_key, 2)
        order = jax.random.permutation(key_order, others)
        position = (jnp.arange(3)[None, :] * ROWS + jnp.arange(ROWS)[:, None]) // CAP
        offset = order[position]
        group_id = block_id // LOOP
        blk_id = block_id % LOOP
        target_group = (group_id + 1 + offset) % GROUPS
        row_pick = jax.random.randint(key_rows, (ROWS, 3), 0, ROWS)
        return ((target_group * LOOP + blk_id) * ROWS + row_pick).astype(jnp.int32)
    block_keys = jax.random.split(jax.random.fold_in(key, 7), blocks)
    return jax.vmap(per_block)(block_keys, jnp.arange(blocks)).reshape(blocks * ROWS, 3)


def draw_passages(key, part):
    return base_passages(key).astype(jnp.bfloat16)


def draw_hard_index(key, part):
    return hard_targets(key)


def draw_queries(key, part):
    total_rows = GROUPS * LOOP * ROWS
    group_rows = LOOP * ROWS
    base_rows = base_passages(key)
    targets = hard_targets(key)
    group_keys = jax.random.split(jax.random.fold_in(key, 13), GROUPS)
    partner_rows = jax.vmap(lambda group_key: jax.random.permutation(group_key, group_rows))(group_keys)
    partner_rows = (partner_rows + jnp.arange(GROUPS)[:, None] * group_rows).reshape(total_rows)
    noise_part = jax.random.normal(jax.random.fold_in(key, 15), (total_rows, D), jnp.float32) * D ** (-0.5)
    mixture = 0.12 * base_rows + 0.1 * (base_rows[targets[:, 0]] + base_rows[targets[:, 1]] + base_rows[targets[:, 2]])
    mixture = mixture + 0.1 * base_rows[partner_rows] + 0.9 * noise_part
    return jnp.clip(mixture, -4.0, 4.0).astype(jnp.bfloat16)


def block_scale(own_key, shape, cuts, smallest, top_value):
    loudness, own = 1.0, jax.random.fold_in(own_key, 6)
    for dim, blocks in cuts:
        draws = jnp.exp(jax.random.uniform(jax.random.fold_in(own, dim), (blocks,), jnp.float32, smallest / len(cuts), top_value / len(cuts)))
        loudness = loudness * jnp.repeat(draws, shape[dim] // blocks).reshape([-1 if axis == dim else 1 for axis in range(len(shape))])
    return loudness


def setup_inputs(seed: int = 0) -> dict:
    arg_keys = jax.random.split(jax.random.key(seed), 5)
    return {
        "queries": draw_queries(jax.random.fold_in(arg_keys[4], 71), 0),
        "passages": draw_passages(jax.random.fold_in(arg_keys[4], 71), 0),
        "hard_index": draw_hard_index(jax.random.fold_in(arg_keys[4], 71), 0),
        "weights": jnp.clip(jnp.exp(math.log(2.0) - 1.3862944 * jax.random.uniform(arg_keys[3], (TOTAL,), jnp.float32) ** block_scale(arg_keys[3], (TOTAL,), ((0, 32),), -0.2, 0.2)), 0.5, 2.0),
    }


def reference(queries, passages, hard_index, weights):
    block_total = GROUPS * LOOP
    q_blocks = queries.reshape(block_total, ROWS, D)
    p_blocks = passages.reshape(block_total, ROWS, D)
    index_blocks = hard_index.reshape(block_total, ROWS, 3)
    weight_blocks = weights.reshape(block_total, ROWS)

    def first(hard_extra, block_id):
        group_id = block_id // LOOP
        blk_id = block_id % LOOP
        q_here = q_blocks[block_id]
        weight_here = weight_blocks[block_id]
        index_here = index_blocks[block_id]
        window = jnp.concatenate([p_blocks[group_id * LOOP + (blk_id + s) % LOOP] for s in range(WINDOW)], axis=0)
        hard_rows = passages[index_here.reshape(-1)].reshape(ROWS, 3, D)
        scores = 50.0 * jnp.dot(q_here, window.T, preferred_element_type=jnp.float32)
        hard_scores = 50.0 * jnp.einsum("rd,rkd->rk", q_here.astype(jnp.float32), hard_rows.astype(jnp.float32))
        largest = jnp.maximum(jnp.max(scores, axis=1), jnp.max(hard_scores, axis=1))
        summed = jnp.sum(jnp.exp(scores - largest[:, None]), axis=1) + jnp.sum(jnp.exp(hard_scores - largest[:, None]), axis=1)
        log_total = largest + jnp.log(summed)
        loss_part = log_total - jnp.diagonal(scores[:, :ROWS])
        weight_col = weight_here[:, None]
        weighting = (weight_col * jnp.exp(scores - log_total[:, None])).astype(jnp.bfloat16)
        hard_weighting = (weight_col * jnp.exp(hard_scores - log_total[:, None])).astype(jnp.bfloat16)
        pulled = jnp.dot(weighting, window, preferred_element_type=jnp.float32)
        pulled = pulled + jnp.einsum("rk,rkd->rd", hard_weighting.astype(jnp.float32), hard_rows.astype(jnp.float32))
        grad_q = (50.0 * (pulled - weight_col * p_blocks[block_id].astype(jnp.float32))).astype(jnp.bfloat16)
        terms = (hard_weighting.astype(jnp.float32)[:, :, None] * q_here.astype(jnp.float32)[:, None, :]).astype(jnp.bfloat16)
        terms = lax.optimization_barrier(terms).astype(jnp.float32)
        hard_extra = hard_extra.at[index_here.reshape(-1)].add(terms.reshape(-1, D))
        return hard_extra, (loss_part, grad_q, weighting)

    start_extra = jnp.zeros((block_total * ROWS, D), jnp.float32)
    block_ids = jnp.arange(block_total).astype(jnp.int32)
    hard_extra, (loss_rows, grad_q, weighting_all) = lax.scan(first, start_extra, block_ids)

    def second(carry, block_id):
        group_id = block_id // LOOP
        blk_id = block_id % LOOP
        total = -weight_blocks[block_id][:, None] * q_blocks[block_id].astype(jnp.float32)
        for s in range(WINDOW):
            source = group_id * LOOP + (blk_id - s) % LOOP
            coef = weighting_all[source][:, s * ROWS:(s + 1) * ROWS]
            total = total + jnp.dot(coef.T, q_blocks[source], preferred_element_type=jnp.float32)
        return carry, total

    unused, in_group = lax.scan(second, jnp.zeros((), jnp.float32), block_ids)
    grad_passages = (50.0 * (in_group.reshape(-1, D) + hard_extra)).astype(jnp.bfloat16)
    return loss_rows.reshape(-1), grad_q.reshape(-1, D), grad_passages
```

```python
import jax
import jax.numpy as jnp
from jax import lax
from jax.sharding import PartitionSpec as P

INV_TEMP = 50.0
BF16 = jnp.bfloat16
F32 = jnp.float32


def dot(left, right, dims):
    return lax.dot_general(left, right, (dims, ((), ())), preferred_element_type=F32)


def per_device(queries, passages, hard_index, weights):
    rows, width = queries.shape
    groups = lax.axis_size("grp")
    loop = lax.axis_size("blk")
    cols = width // groups
    g = lax.axis_index("grp")
    odd = lax.axis_index("blk") % 2 == 1

    def shift(array, by, which=(0, 1)):
        pairs = [(i, (i + by) % loop) for i in range(loop) if i % 2 in which]
        return lax.ppermute(array, "blk", pairs)

    def swap(array):
        return lax.ppermute(array, "blk", [(i, i ^ 1) for i in range(loop)])

    def to_group(array, r):
        return lax.ppermute(array, "grp", [(i, i ^ r) for i in range(groups)])

    def slice_of(array, r):
        return lax.dynamic_slice_in_dim(array, (g ^ r) * cols, cols, 1)

    next1 = shift(passages, -1)
    next3_even = shift(passages, -3, (1,))

    index_t = hard_index.T
    pieces, indices = [], []
    for r in range(groups):
        piece = jnp.concatenate([slice_of(queries, r), slice_of(passages, r)], axis=0)
        pieces.append(piece if r == 0 else to_group(piece, r))
        indices.append(index_t if r == 0 else to_group(index_t, r))
    q_cols = jnp.concatenate([piece[:rows] for piece in pieces], axis=0)
    p_cols = jnp.concatenate([piece[rows:] for piece in pieces], axis=0)
    index_all = jnp.concatenate(indices, axis=1)
    place = ((index_all // (loop * rows)) ^ g) * rows + index_all % rows

    held = jnp.where(odd, next1, next3_even)
    next2 = swap(held)
    next3 = jnp.where(odd, shift(next1, -2, (1,)), next3_even)

    hard_dots = dot(p_cols, q_cols, ((1,), (1,)))
    passage_id = lax.broadcasted_iota(jnp.int32, hard_dots.shape, 0)
    hits = [passage_id == place[k][None, :] for k in range(3)]
    hard_part = jnp.stack([jnp.sum(jnp.where(hit, hard_dots, 0.0), axis=0) for hit in hits])
    hard_sum = hard_part[:, :rows]
    for r in range(1, groups):
        hard_sum = hard_sum + to_group(hard_part[:, r * rows : (r + 1) * rows], r)
    hard_scores = INV_TEMP * hard_sum

    window = [passages, next1, next2, next3]
    scores = [INV_TEMP * dot(block, queries, ((1,), (1,))) for block in window]
    largest = jnp.max(hard_scores, axis=0)
    for block in scores:
        largest = jnp.maximum(largest, jnp.max(block, axis=0))
    summed = jnp.sum(jnp.exp(hard_scores - largest[None, :]), axis=0)
    for block in scores:
        summed = summed + jnp.sum(jnp.exp(block - largest[None, :]), axis=0)
    log_total = largest + jnp.log(summed)
    eye = lax.broadcasted_iota(jnp.int32, (rows, rows), 0) == lax.broadcasted_iota(
        jnp.int32, (rows, rows), 1
    )
    loss_rows = log_total - jnp.sum(jnp.where(eye, scores[0], 0.0), axis=0)
    coef = [(weights[None, :] * jnp.exp(block - log_total[None, :])).astype(BF16) for block in scores]
    hard_coef = (weights[None, :] * jnp.exp(hard_scores - log_total[None, :])).astype(BF16)

    term3 = dot(coef[3], queries, ((1,), (0,)))
    got3 = shift(term3.astype(BF16), 2, (1,))
    term2 = dot(coef[2], queries, ((1,), (0,)))
    got2 = swap(term2.astype(BF16))

    hard_all = jnp.concatenate(
        [hard_coef] + [to_group(hard_coef, r) for r in range(1, groups)], axis=1
    ).astype(F32)
    hard_matrix = sum(
        jnp.where(hit, hard_all[k][None, :], 0.0) for k, hit in enumerate(hits)
    ).astype(BF16)
    hard_q = dot(hard_matrix, p_cols, ((0,), (0,))).astype(BF16)
    hard_p = dot(hard_matrix, q_cols, ((1,), (0,))).astype(BF16)

    sent3 = (term3 + got2.astype(F32)).astype(BF16)
    own3 = shift(sent3, 3, (0,))
    term1 = dot(coef[1], queries, ((1,), (0,)))
    extra = jnp.where(odd, got2.astype(F32) + got3.astype(F32), 0.0)
    own1 = shift((term1 + extra).astype(BF16), 1)

    back_q = jnp.zeros((rows, width), BF16)
    back_p = jnp.zeros((rows, width), BF16)
    for r in range(groups):
        mine = slice(r * rows, (r + 1) * rows)
        piece = jnp.concatenate([hard_q[mine], hard_p[mine]], axis=0)
        if r:
            piece = to_group(piece, r)
        back_q = lax.dynamic_update_slice_in_dim(back_q, piece[:rows], (g ^ r) * cols, 1)
        back_p = lax.dynamic_update_slice_in_dim(back_p, piece[rows:], (g ^ r) * cols, 1)

    weight_col = weights[:, None]
    pulled = dot(jnp.concatenate(coef, axis=0), jnp.concatenate(window, axis=0), ((0,), (0,)))
    grad_queries = (
        INV_TEMP * (pulled + back_q.astype(F32) - weight_col * passages.astype(F32))
    ).astype(BF16)
    in_group = dot(coef[0], queries, ((1,), (0,))) + own1.astype(F32)
    in_group = in_group + jnp.where(odd, own3.astype(F32), 0.0)
    in_group = in_group - weight_col * queries.astype(F32)
    grad_passages = (INV_TEMP * (in_group + back_p.astype(F32))).astype(BF16)
    return loss_rows, grad_queries, grad_passages


def solution(mesh):
    rows = P(("grp", "blk"))
    matrix = P(("grp", "blk"), None)
    return jax.shard_map(
        per_device,
        mesh=mesh,
        in_specs=(matrix, matrix, matrix, rows),
        out_specs=(rows, matrix, matrix),
        check_vma=False,
    )
```

```python
import functools

import jax
import jax.numpy as jnp
from jax import lax
from jax.experimental import pallas as pl
from jax.experimental.pallas import tpu as pltpu
from jax.sharding import PartitionSpec as P

INV_TEMP = 50.0
BF16 = jnp.bfloat16
F32 = jnp.float32
CHUNK = 512
SHORT, LONG = 1000, 10**11


def dot(left, right, dims):
    return lax.dot_general(left, right, (dims, ((), ())), preferred_element_type=F32)


def local_call(body, out_shape, *args, later_than=(), cost=SHORT):
    vmem = pl.BlockSpec(memory_space=pltpu.VMEM)
    anywhere = pl.BlockSpec(memory_space=pl.ANY)
    used = len(args)
    skipped = len(later_than)

    def run(*refs):
        body(*refs[:used], *refs[used + skipped :])

    return pl.pallas_call(
        run,
        out_shape=out_shape,
        in_specs=[vmem] * used + [anywhere] * skipped,
        out_specs=jax.tree.map(lambda _: vmem, out_shape),
        cost_estimate=pl.CostEstimate(flops=cost, bytes_accessed=cost, transcendentals=0),
        compiler_params=pltpu.CompilerParams(vmem_limit_bytes=20 * 2**20),
    )(*args, *later_than)


def tie(array, *others):
    anywhere = pl.BlockSpec(memory_space=pl.ANY)

    def run(*refs):
        pass

    return pl.pallas_call(
        run,
        out_shape=jax.ShapeDtypeStruct(array.shape, array.dtype),
        in_specs=[anywhere] * (1 + len(others)),
        out_specs=anywhere,
        input_output_aliases={0: 0},
        cost_estimate=pl.CostEstimate(flops=LONG, bytes_accessed=LONG, transcendentals=0),
    )(array, *others)


def cut_body(groups, q_ref, p_ref, tail_ref, *outs):
    rows = q_ref.shape[0]
    cols = outs[0].shape[1]
    g = lax.axis_index("grp")
    for r, out in enumerate(outs):
        start = pl.multiple_of((g ^ r) * cols, 128)
        out[:rows] = q_ref[:, pl.ds(start, cols)]
        out[rows : 2 * rows] = p_ref[:, pl.ds(start, cols)]
        out[2 * rows :] = tail_ref[...]


def places_of(piece_ref, rows):
    tail = piece_ref[2 * rows :, : 2 * rows].astype(F32).astype(jnp.int32)
    g = lax.axis_index("grp")
    return [(tail[k : k + 1, :rows] ^ g) * rows + tail[k : k + 1, rows:] for k in range(3)]


def hard_scores_body(groups, *refs):
    pieces, outs = refs[:groups], refs[groups:]
    rows = outs[0].shape[1]
    ids = lax.broadcasted_iota(jnp.int32, (rows, rows), 0)
    for r in range(groups):
        places = places_of(pieces[r], rows)
        sums = [jnp.zeros((1, rows), F32) for _ in range(3)]
        for other in range(groups):
            if other != r:
                dots = dot(pieces[other][rows : 2 * rows], pieces[r][:rows], ((1,), (1,)))
                for k in range(3):
                    hit = ids + other * rows == places[k]
                    sums[k] += jnp.sum(jnp.where(hit, dots, 0.0), axis=0, keepdims=True)
        outs[r][...] = jnp.concatenate(sums, axis=0)


def hard_grads_body(groups, *refs):
    pieces, coefs, outs, matrix = (
        refs[:groups], refs[groups : 2 * groups], refs[2 * groups : 3 * groups], refs[-1]
    )
    rows = coefs[0].shape[1]
    cols = outs[0].shape[1]
    ids = lax.broadcasted_iota(jnp.int32, (groups * rows, rows), 0)
    for r in range(groups):
        places = places_of(pieces[r], rows)
        total = jnp.zeros(ids.shape, F32)
        for k in range(3):
            total += jnp.where(ids == places[k], coefs[r][k : k + 1], 0.0)
        matrix[:, r * rows : (r + 1) * rows] = total.astype(BF16)
    step = min(cols, CHUNK)
    for c in range(0, cols, step):
        at = slice(c, c + step)
        q_all = jnp.concatenate([piece[:rows, at] for piece in pieces], axis=0)
        p_all = jnp.concatenate([piece[rows : 2 * rows, at] for piece in pieces], axis=0)
        for r in range(groups):
            mine = slice(r * rows, (r + 1) * rows)
            outs[r][:rows, at] = dot(matrix[:, mine], p_all, ((0,), (0,))).astype(BF16)
            outs[r][rows:, at] = dot(matrix[mine], q_all, ((1,), (0,))).astype(BF16)


def choose_body(n1_ref, e3_ref, out):
    odd = lax.axis_index("blk") % 2 == 1

    @pl.when(odd)
    def _():
        out[...] = n1_ref[...]

    @pl.when(jnp.logical_not(odd))
    def _():
        out[...] = e3_ref[...]


def scores_body(q_ref, *refs):
    half = len(refs) // 2
    for block, out in zip(refs[:half], refs[half:]):
        out[...] = dot(block[...], q_ref[...], ((1,), (1,)))


def weigh_body(groups, q_ref, s0_ref, s1_ref, s2_ref, s3_ref, last_ref, w_ref, *refs):
    hard_refs = refs[:groups]
    loss_ref, coef_ref, hard_out, term3_ref, term2_ref = refs[groups:]
    rows, width = q_ref.shape
    w = w_ref[...]
    s3 = INV_TEMP * (s3_ref[...] + dot(last_ref[...], q_ref[...], ((1,), (1,))))
    scores = [INV_TEMP * s0_ref[...], INV_TEMP * s1_ref[...], INV_TEMP * s2_ref[...], s3]
    hard = hard_refs[0][...]
    for other in hard_refs[1:]:
        hard = hard + other[...]
    hard = INV_TEMP * hard
    largest = jnp.max(hard, axis=0, keepdims=True)
    for block in scores:
        largest = jnp.maximum(largest, jnp.max(block, axis=0, keepdims=True))
    summed = jnp.sum(jnp.exp(hard - largest), axis=0, keepdims=True)
    for block in scores:
        summed = summed + jnp.sum(jnp.exp(block - largest), axis=0, keepdims=True)
    log_total = largest + jnp.log(summed)
    for s in range(4):
        coef_ref[s * rows : (s + 1) * rows] = (w * jnp.exp(scores[s] - log_total)).astype(BF16)
    for c in range(0, width, CHUNK):
        both = dot(coef_ref[2 * rows :], q_ref[:, c : c + CHUNK], ((1,), (0,))).astype(BF16)
        term2_ref[:, c : c + CHUNK] = both[:rows]
        term3_ref[:, c : c + CHUNK] = both[rows:]
    hard_out[...] = (w * jnp.exp(hard - log_total)).astype(BF16).astype(F32)
    eye = lax.broadcasted_iota(jnp.int32, (rows, rows), 0) == lax.broadcasted_iota(
        jnp.int32, (rows, rows), 1
    )
    loss_ref[...] = log_total - jnp.sum(jnp.where(eye, scores[0], 0.0), axis=0, keepdims=True)


def sums_body(q_ref, coef_ref, term3_ref, got2_ref, sent3, partial1):
    rows, width = q_ref.shape
    keep = jnp.where(lax.axis_index("blk") % 2 == 1, 1.0, 0.0)
    for c in range(0, width, CHUNK):
        at = slice(c, c + CHUNK)
        got2 = got2_ref[:, at].astype(F32)
        sent3[:, at] = (term3_ref[:, at].astype(F32) + got2).astype(BF16)
        partial1[:, at] = dot(coef_ref[rows : 2 * rows], q_ref[:, at], ((1,), (0,))) + keep * got2


def relay_body(partial1, got3_ref, out):
    out[...] = (partial1[...] + got3_ref[...].astype(F32)).astype(BF16)


def base_body(q_ref, p_ref, n1_ref, n2_ref, e3_ref, o3_ref, coef_ref, w_ref, pulled, base):
    rows, width = q_ref.shape
    w = w_ref[...]
    blocks = (p_ref, n1_ref, n2_ref, e3_ref, o3_ref)
    for c in range(0, width, CHUNK):
        at = slice(c, c + CHUNK)
        total = -w * p_ref[:, at].astype(F32)
        for s, block in enumerate(blocks):
            k = min(s, 3) * rows
            total = total + dot(coef_ref[k : k + rows], block[:, at], ((0,), (0,)))
        pulled[:, at] = total
        base[:, at] = dot(coef_ref[:rows], q_ref[:, at], ((1,), (0,))) - w * q_ref[:, at].astype(F32)


def gather_body(groups, pulled, base, own3, *refs):
    backs, (grad_q, almost) = refs[:groups], refs[groups:]
    rows, cols = pulled.shape[0], backs[0].shape[1]
    g = lax.axis_index("grp")
    for r, back in enumerate(backs):
        at = pl.ds(pl.multiple_of((g ^ r) * cols, 128), cols)
        grad_q[:, at] = (INV_TEMP * (pulled[:, at] + back[:rows].astype(F32))).astype(BF16)
        almost[:, at] = INV_TEMP * (
            base[:, at] + back[rows:].astype(F32) + own3[:, at].astype(F32)
        )


def per_device(queries, passages, hard_index, weights):
    rows, width = queries.shape
    groups = lax.axis_size("grp")
    loop = lax.axis_size("blk")
    cols = width // groups

    def shift(array, by, which=(0, 1)):
        pairs = [(i, (i + by) % loop) for i in range(loop) if i % 2 in which]
        return lax.ppermute(array, "blk", pairs)

    def swap(array):
        return lax.ppermute(array, "blk", [(i, i ^ 1) for i in range(loop)])

    def exchange(arrays):
        return [
            lax.ppermute(array, "grp", [(i, i ^ r) for i in range(groups)]) if r else array
            for r, array in enumerate(arrays)
        ]

    def like(*shape, dtype=BF16):
        return jax.ShapeDtypeStruct(shape, dtype)

    block, block32 = like(rows, width), like(rows, width, dtype=F32)
    square, triple = like(rows, rows, dtype=F32), like(3, rows, dtype=F32)

    next1 = shift(passages, -1)
    next3_even = shift(passages, -3, (1,))

    index_t = hard_index.T
    tail = jnp.concatenate([index_t // (loop * rows), index_t % rows], axis=1).astype(BF16)
    tail = jnp.pad(tail, ((0, 13), (0, cols - 2 * rows)))
    pieces = local_call(
        functools.partial(cut_body, groups),
        [like(2 * rows + 16, cols)] * groups,
        queries, passages, tail,
    )
    own_piece = pieces[0]
    pieces = exchange(pieces)

    next1 = tie(next1, own_piece)
    next3_odd = shift(next1, -2, (1,))
    next2 = swap(local_call(choose_body, block, next1, next3_even, cost=LONG))

    hard_parts = exchange(
        local_call(
            functools.partial(hard_scores_body, groups), [triple] * groups, *pieces,
            later_than=(next1,), cost=LONG,
        )
    )

    s0, s1, s3 = local_call(scores_body, [square] * 3, queries, passages, next1, next3_even)
    (s2,) = local_call(scores_body, [square], queries, next2)
    loss_rows, coef, hard_coef, term3, term2 = local_call(
        functools.partial(weigh_body, groups),
        [like(1, rows, dtype=F32), like(4 * rows, rows), triple, block, block],
        queries, s0, s1, s2, s3, next3_odd, weights[None, :], *hard_parts,
    )

    got3 = shift(term3, 2, (1,))
    got2 = swap(term2)

    hard_coefs = exchange([hard_coef] * groups)
    hard_call = pl.pallas_call(
        functools.partial(hard_grads_body, groups),
        out_shape=[like(2 * rows, cols)] * groups,
        in_specs=[pl.BlockSpec(memory_space=pltpu.VMEM)] * (2 * groups),
        out_specs=[pl.BlockSpec(memory_space=pltpu.VMEM)] * groups,
        scratch_shapes=[pltpu.VMEM((groups * rows, groups * rows), BF16)],
        cost_estimate=pl.CostEstimate(flops=SHORT, bytes_accessed=SHORT, transcendentals=0),
        compiler_params=pltpu.CompilerParams(vmem_limit_bytes=20 * 2**20),
    )
    backs = hard_call(*pieces, *hard_coefs)
    own_back = backs[0]
    backs = exchange(backs)

    sent3, partial1 = local_call(
        sums_body, [block, block32], queries, coef, term3, got2, later_than=(own_back,)
    )
    own3 = shift(sent3, 3, (0,))
    sent1 = local_call(relay_body, block, partial1, got3)
    own1 = shift(sent1, 1)

    pulled, base = local_call(
        base_body, [block32, block32],
        queries, passages, next1, next2, next3_even, next3_odd, coef, weights[:, None],
        later_than=(sent1,),
    )
    grad_queries, almost = local_call(
        functools.partial(gather_body, groups), [block, block32],
        pulled, base, own3, *backs, later_than=(sent1,), cost=LONG,
    )
    grad_passages = (almost + INV_TEMP * own1.astype(F32)).astype(BF16)
    return loss_rows.reshape(rows), grad_queries, grad_passages


def solution(mesh):
    rows = P(("grp", "blk"))
    matrix = P(("grp", "blk"), None)
    return jax.shard_map(
        per_device,
        mesh=mesh,
        in_specs=(matrix, matrix, matrix, rows),
        out_specs=(rows, matrix, matrix),
        check_vma=False,
    )
```

```python
import functools
import math

import jax
import jax.numpy as jnp
from jax import lax
from jax.experimental import pallas as pl
from jax.experimental.pallas import tpu as pltpu
from jax.sharding import PartitionSpec as P

INV_TEMP = 50.0
BF16 = jnp.bfloat16
F32 = jnp.float32
CHUNK = 512
TAIL = 16
LONG, SOME = 5 * 10**10, 16 * 10**9
VMEM = pl.BlockSpec(memory_space=pltpu.VMEM)
HBM = pl.BlockSpec(memory_space=pltpu.HBM)
TOKEN = jax.ShapeDtypeStruct((8, 128), F32)


def dot(left, right, dims):
    return lax.dot_general(left, right, (dims, ((), ())), preferred_element_type=F32)


def size_of(arrays):
    return sum(math.prod(a.shape) * jnp.dtype(a.dtype).itemsize for a in arrays)


def local_call(body, out_shape, *args, flops=0, in_specs=None, out_specs=None, scratch=()):
    return pl.pallas_call(
        body,
        out_shape=out_shape,
        in_specs=in_specs or [VMEM] * len(args),
        out_specs=out_specs or [VMEM] * len(out_shape),
        scratch_shapes=list(scratch),
        cost_estimate=pl.CostEstimate(
            flops=flops, bytes_accessed=size_of(args) + size_of(out_shape), transcendentals=0
        ),
        compiler_params=pltpu.CompilerParams(vmem_limit_bytes=20 * 2**20),
    )(*args)


def signal(token):
    token[...] = jnp.zeros(token.shape, token.dtype)


def split_index(index, rows, group_rows):
    if group_rows & (group_rows - 1) or rows & (rows - 1):
        return index // group_rows, index % rows
    return index >> (group_rows.bit_length() - 1), index & (rows - 1)


def load_body(groups, group_rows, q_hbm, p_hbm, index_ref, q_ref, p_ref, *refs):
    pieces, token, sems = refs[:groups], refs[groups], refs[groups + 1]
    rows = q_ref.shape[0]
    cols = pieces[0].shape[1]
    g = lax.axis_index("grp")
    copies = []
    for r in range(groups):
        at = pl.ds(pl.multiple_of((g ^ r) * cols, 128), cols)
        pair = [
            pltpu.make_async_copy(source.at[:, at], target.at[:, at], sems.at[2 * r + n])
            for n, (source, target) in enumerate(((q_hbm, q_ref), (p_hbm, p_ref)))
        ]
        for copy in pair:
            copy.start()
        copies.append((at, pair))
    signal(token)
    named_group, named_row = split_index(index_ref[...], rows, group_rows)
    named_group = named_group.astype(F32).astype(BF16)
    named_row = named_row.astype(F32).astype(BF16)
    for r in reversed(range(groups)):
        at, pair = copies[r]
        for copy in pair:
            copy.wait()
        pieces[r][:rows] = q_ref[:, at]
        pieces[r][rows : 2 * rows] = p_ref[:, at]
        pieces[r][2 * rows :, :rows] = named_group
        pieces[r][2 * rows :, rows : 2 * rows] = named_row


def places_of(piece_ref, rows):
    tail = piece_ref[2 * rows :, : 2 * rows].astype(F32).astype(jnp.int32)
    g = lax.axis_index("grp")
    return [(tail[k : k + 1, :rows] ^ g) * rows + tail[k : k + 1, rows:] for k in range(3)]


def hard_scores_body(groups, *refs):
    pieces, outs = refs[:groups], refs[groups + 1 :]
    rows = outs[0].shape[1]
    ids = lax.broadcasted_iota(jnp.int32, (groups * rows, rows), 0)
    p_all = jnp.concatenate([piece[rows : 2 * rows] for piece in pieces], axis=0)
    for r in range(groups):
        places = places_of(pieces[r], rows)
        dots = dot(p_all, pieces[r][:rows], ((1,), (1,)))
        for k in range(3):
            hit = jnp.where(ids == places[k], dots, 0.0)
            outs[r][k : k + 1] = jnp.sum(hit, axis=0, keepdims=True)


def hard_grads_body(groups, *refs):
    pieces, coefs, outs = refs[:groups], refs[groups : 2 * groups], refs[2 * groups : 3 * groups]
    token, matrix, matrix_t = refs[3 * groups :]
    rows = coefs[0].shape[1]
    cols = outs[0].shape[1]
    signal(token)
    ids = lax.broadcasted_iota(jnp.int32, (groups * rows, rows), 0)
    for r in range(groups):
        places = places_of(pieces[r], rows)
        total = jnp.zeros(ids.shape, F32)
        for k in range(3):
            total += jnp.where(ids == places[k], coefs[r][k : k + 1], 0.0)
        mine = slice(r * rows, (r + 1) * rows)
        matrix[:, mine] = total.astype(BF16)
        matrix_t[mine] = total.T.astype(BF16)
    step = min(cols, 256)
    for c in range(0, cols, step):
        at = slice(c, c + step)
        q_all = jnp.concatenate([piece[:rows, at] for piece in pieces], axis=0)
        p_all = jnp.concatenate([piece[rows : 2 * rows, at] for piece in pieces], axis=0)
        grad_q = dot(matrix_t[...], p_all, ((1,), (0,))).astype(BF16)
        grad_p = dot(matrix[...], q_all, ((1,), (0,))).astype(BF16)
        for r in range(groups):
            mine = slice(r * rows, (r + 1) * rows)
            outs[r][:rows, at] = grad_q[mine]
            outs[r][rows:, at] = grad_p[mine]


def pass_body(source, token, out):
    out[...] = source[...]


def choose_body(n1_ref, e3_ref, out):
    odd = lax.axis_index("blk") % 2 == 1

    @pl.when(odd)
    def _():
        out[...] = n1_ref[...]

    @pl.when(jnp.logical_not(odd))
    def _():
        out[...] = e3_ref[...]


def scores_body(q_ref, *refs):
    half = len(refs) // 2
    for block, out in zip(refs[:half], refs[half:]):
        out[...] = dot(block[...], q_ref[...], ((1,), (1,)))


def weigh_body(groups, q_ref, s0_ref, s1_ref, s2_ref, s3_ref, last_ref, w_ref, *refs):
    hard_refs = refs[:groups]
    loss_ref, coef_ref, hard_out, term3_ref, term2_ref = refs[groups:]
    rows, width = q_ref.shape
    w = w_ref[...]
    s3 = INV_TEMP * (s3_ref[...] + dot(last_ref[...], q_ref[...], ((1,), (1,))))
    scores = [INV_TEMP * s0_ref[...], INV_TEMP * s1_ref[...], INV_TEMP * s2_ref[...], s3]
    hard = hard_refs[0][...]
    for other in hard_refs[1:]:
        hard = hard + other[...]
    hard = INV_TEMP * hard
    largest = jnp.max(hard, axis=0, keepdims=True)
    for block in scores:
        largest = jnp.maximum(largest, jnp.max(block, axis=0, keepdims=True))
    summed = jnp.sum(jnp.exp(hard - largest), axis=0, keepdims=True)
    for block in scores:
        summed = summed + jnp.sum(jnp.exp(block - largest), axis=0, keepdims=True)
    log_total = largest + jnp.log(summed)
    for s in range(4):
        coef_ref[s * rows : (s + 1) * rows] = (w * jnp.exp(scores[s] - log_total)).astype(BF16)
    for c in range(0, width, CHUNK):
        at = slice(c, c + CHUNK)
        both = dot(coef_ref[2 * rows :], q_ref[:, at], ((1,), (0,))).astype(BF16)
        term2_ref[:, at] = both[:rows]
        term3_ref[:, at] = both[rows:]
    hard_out[...] = (w * jnp.exp(hard - log_total)).astype(BF16).astype(F32)
    eye = lax.broadcasted_iota(jnp.int32, (rows, rows), 0) == lax.broadcasted_iota(
        jnp.int32, (rows, rows), 1
    )
    loss_ref[...] = log_total - jnp.sum(jnp.where(eye, scores[0], 0.0), axis=0, keepdims=True)


def add_body(a_ref, b_ref, token, out, done):
    signal(done)
    out[...] = (a_ref[...].astype(F32) + b_ref[...].astype(F32)).astype(BF16)


def term1_body(q_ref, coef_ref, got2_ref, token, out):
    rows, width = q_ref.shape
    keep = jnp.where(lax.axis_index("blk") % 2 == 1, 1.0, 0.0)
    for c in range(0, width, CHUNK):
        at = slice(c, c + CHUNK)
        term1 = dot(coef_ref[rows : 2 * rows], q_ref[:, at], ((1,), (0,)))
        out[:, at] = term1 + keep * got2_ref[:, at].astype(F32)


def relay_body(partial1, got3_ref, out, done):
    signal(done)
    out[...] = (partial1[...] + got3_ref[...].astype(F32)).astype(BF16)


def base_body(
    q_ref, p_ref, n1_ref, n2_ref, e3_ref, o3_ref, coef_ref, w_ref, own3_ref, token, pulled, base
):
    rows, width = q_ref.shape
    w = w_ref[...]
    blocks = (p_ref, n1_ref, n2_ref, e3_ref, o3_ref)
    coef_t = coef_ref[...].astype(F32).T.astype(BF16)
    coef_t = jnp.concatenate([coef_t, coef_t[:, 3 * rows :]], axis=1)
    for c in range(0, width, CHUNK):
        at = slice(c, c + CHUNK)
        held = jnp.concatenate([block[:, at] for block in blocks], axis=0)
        pulled[:, at] = dot(coef_t, held, ((1,), (0,))) - w * p_ref[:, at].astype(F32)
        own = dot(coef_ref[:rows], q_ref[:, at], ((1,), (0,))) + own3_ref[:, at].astype(F32)
        base[:, at] = own - w * q_ref[:, at].astype(F32)


def finish_body(groups, pulled, base, own1, *refs):
    backs = refs[:groups]
    q_out, p_out, q_held, p_held, sems = refs[groups:]
    rows, cols = pulled.shape[0], backs[0].shape[1]
    g = lax.axis_index("grp")
    copies = []
    for r, back in enumerate(backs):
        at = pl.ds(pl.multiple_of((g ^ r) * cols, 128), cols)
        q_held[:, at] = (INV_TEMP * (pulled[:, at] + back[:rows].astype(F32))).astype(BF16)
        copies.append(pltpu.make_async_copy(q_held.at[:, at], q_out.at[:, at], sems.at[2 * r]))
        copies[-1].start()
        total = base[:, at] + back[rows:].astype(F32) + own1[:, at].astype(F32)
        p_held[:, at] = (INV_TEMP * total).astype(BF16)
        copies.append(pltpu.make_async_copy(p_held.at[:, at], p_out.at[:, at], sems.at[2 * r + 1]))
        copies[-1].start()
    for copy in copies:
        copy.wait()


def per_device(queries, passages, hard_index, weights):
    rows, width = queries.shape
    groups = lax.axis_size("grp")
    loop = lax.axis_size("blk")
    cols = width // groups

    def shift(array, by, which=(0, 1)):
        pairs = [(i, (i + by) % loop) for i in range(loop) if i % 2 in which]
        return lax.ppermute(array, "blk", pairs)

    def swap(array):
        return lax.ppermute(array, "blk", [(i, i ^ 1) for i in range(loop)])

    def exchange(arrays):
        out = list(arrays)
        for r in reversed(range(1, groups)):
            out[r] = lax.ppermute(arrays[r], "grp", [(i, i ^ r) for i in range(groups)])
        return out

    def like(*shape, dtype=BF16):
        return jax.ShapeDtypeStruct(shape, dtype)

    block, block32 = like(rows, width), like(rows, width, dtype=F32)
    square, triple = like(rows, rows, dtype=F32), like(3, rows, dtype=F32)
    piece, back = like(2 * rows + TAIL, cols), like(2 * rows, cols)

    next1 = shift(passages, -1)

    index_t = jnp.pad(hard_index.T, ((0, TAIL - 3), (0, 0)))
    held_q, held_p, *pieces, token = local_call(
        functools.partial(load_body, groups, loop * rows),
        [block, block] + [piece] * groups + [TOKEN],
        queries, passages, index_t,
        in_specs=[HBM, HBM, VMEM],
        scratch=[pltpu.SemaphoreType.DMA((2 * groups,))],
    )
    pieces = exchange(pieces)

    next3_even = shift(held_p, -3, (1,))
    (next1,) = local_call(pass_body, [block], next1, token, flops=LONG)
    next3_odd = shift(next1, -2, (1,))
    next2 = swap(local_call(choose_body, [block], next1, next3_even, flops=LONG)[0])

    s0, s1, s3 = local_call(scores_body, [square] * 3, held_q, held_p, next1, next3_even)
    hard_parts = exchange(
        local_call(
            functools.partial(hard_scores_body, groups), [triple] * groups, *pieces, s0, flops=LONG
        )
    )
    (s2,) = local_call(scores_body, [square], held_q, next2)
    loss_rows, coef, hard_coef, term3, term2 = local_call(
        functools.partial(weigh_body, groups),
        [like(1, rows, dtype=F32), like(4 * rows, rows), triple, block, block],
        held_q, s0, s1, s2, s3, next3_odd, weights[None, :], *hard_parts,
    )

    got3 = shift(term3, 2, (1,))
    got2 = swap(term2)

    hard_coefs = exchange([hard_coef] * groups)
    square_all = pltpu.VMEM((groups * rows, groups * rows), BF16)
    *backs, token = local_call(
        functools.partial(hard_grads_body, groups), [back] * groups + [TOKEN],
        *pieces, *hard_coefs, scratch=[square_all, square_all],
    )
    backs = exchange(backs)

    sent3, token = local_call(add_body, [block, TOKEN], term3, got2, token)
    own3 = shift(sent3, 3, (0,))
    (partial1,) = local_call(term1_body, [block32], held_q, coef, got2, token)
    sent1, token = local_call(relay_body, [block, TOKEN], partial1, got3, flops=SOME)
    own1 = shift(sent1, 1)

    pulled, base = local_call(
        base_body, [block32, block32],
        held_q, held_p, next1, next2, next3_even, next3_odd, coef, weights[:, None], own3, token,
        flops=LONG,
    )
    grad_queries, grad_passages = local_call(
        functools.partial(finish_body, groups), [block, block], pulled, base, own1, *backs,
        out_specs=[HBM, HBM],
        scratch=[
            pltpu.VMEM((rows, width), BF16),
            pltpu.VMEM((rows, width), BF16),
            pltpu.SemaphoreType.DMA((2 * groups,)),
        ],
    )
    return loss_rows.reshape(rows), grad_queries, grad_passages


def solution(mesh):
    rows = P(("grp", "blk"))
    matrix = P(("grp", "blk"), None)
    return jax.shard_map(
        per_device,
        mesh=mesh,
        in_specs=(matrix, matrix, matrix, rows),
        out_specs=(rows, matrix, matrix),
        check_vma=False,
    )
```

```python
import functools
import math

import jax
import jax.numpy as jnp
from jax import lax
from jax.experimental import pallas as pl
from jax.experimental.pallas import tpu as pltpu
from jax.sharding import PartitionSpec as P

INV_TEMP = 50.0
BF16 = jnp.bfloat16
F32 = jnp.float32
CHUNK = 512
TAIL = 16
LONG, SOME = 5 * 10**10, 16 * 10**9
VMEM = pl.BlockSpec(memory_space=pltpu.VMEM)
HBM = pl.BlockSpec(memory_space=pltpu.HBM)
TOKEN = jax.ShapeDtypeStruct((8, 128), F32)


def dot(left, right, dims):
    return lax.dot_general(left, right, (dims, ((), ())), preferred_element_type=F32)


def size_of(arrays):
    return sum(math.prod(a.shape) * jnp.dtype(a.dtype).itemsize for a in arrays)


def local_call(body, out_shape, *args, flops=0, in_specs=None, out_specs=None, scratch=()):
    return pl.pallas_call(
        body,
        out_shape=out_shape,
        in_specs=in_specs or [VMEM] * len(args),
        out_specs=out_specs or [VMEM] * len(out_shape),
        scratch_shapes=list(scratch),
        cost_estimate=pl.CostEstimate(
            flops=flops, bytes_accessed=size_of(args) + size_of(out_shape), transcendentals=0
        ),
        compiler_params=pltpu.CompilerParams(vmem_limit_bytes=20 * 2**20),
    )(*args)


def signal(token):
    token[...] = jnp.zeros(token.shape, token.dtype)


def split_index(index, rows, group_rows):
    if group_rows & (group_rows - 1) or rows & (rows - 1):
        return index // group_rows, index % rows
    return index >> (group_rows.bit_length() - 1), index & (rows - 1)


def load_body(groups, group_rows, q_hbm, p_hbm, index_ref, q_ref, p_ref, *refs):
    pieces, token, sems = refs[:groups], refs[groups], refs[groups + 1]
    rows = q_ref.shape[0]
    cols = pieces[0].shape[1]
    g = lax.axis_index("grp")
    copies = []
    for r in range(groups):
        at = pl.ds(pl.multiple_of((g ^ r) * cols, 128), cols)
        pair = [
            pltpu.make_async_copy(source.at[:, at], target.at[:, at], sems.at[2 * r + n])
            for n, (source, target) in enumerate(((q_hbm, q_ref), (p_hbm, p_ref)))
        ]
        for copy in pair:
            copy.start()
        copies.append((at, pair))
    signal(token)
    index = jnp.concatenate([index_ref[...], jnp.zeros((TAIL - 3, rows), jnp.int32)], axis=0)
    named_group, named_row = split_index(index, rows, group_rows)
    named_group = named_group.astype(F32).astype(BF16)
    named_row = named_row.astype(F32).astype(BF16)
    for r in reversed(range(groups)):
        at, pair = copies[r]
        for copy in pair:
            copy.wait()
        pieces[r][:rows] = q_ref[:, at]
        pieces[r][rows : 2 * rows] = p_ref[:, at]
        pieces[r][2 * rows :, :rows] = named_group
        pieces[r][2 * rows :, rows : 2 * rows] = named_row


def places_of(piece_ref, rows):
    tail = piece_ref[2 * rows :, : 2 * rows].astype(F32).astype(jnp.int32)
    g = lax.axis_index("grp")
    return [(tail[k : k + 1, :rows] ^ g) * rows + tail[k : k + 1, rows:] for k in range(3)]


def hard_scores_body(groups, *refs):
    pieces, outs = refs[:groups], refs[groups + 1 :]
    rows = outs[0].shape[1]
    ids = lax.broadcasted_iota(jnp.int32, (groups * rows, rows), 0)
    p_all = jnp.concatenate([piece[rows : 2 * rows] for piece in pieces], axis=0)
    for r in range(groups):
        places = places_of(pieces[r], rows)
        dots = dot(p_all, pieces[r][:rows], ((1,), (1,)))
        for k in range(3):
            hit = jnp.where(ids == places[k], dots, 0.0)
            outs[r][k : k + 1] = jnp.sum(hit, axis=0, keepdims=True)


def hard_grads_body(groups, *refs):
    pieces, coefs, outs = refs[:groups], refs[groups : 2 * groups], refs[2 * groups + 1 : 3 * groups + 1]
    token, matrix, matrix_t = refs[3 * groups + 1 :]
    rows = coefs[0].shape[1]
    cols = outs[0].shape[1]
    signal(token)
    ids = lax.broadcasted_iota(jnp.int32, (groups * rows, rows), 0)
    for r in range(groups):
        places = places_of(pieces[r], rows)
        total = jnp.zeros(ids.shape, F32)
        for k in range(3):
            total += jnp.where(ids == places[k], coefs[r][k : k + 1], 0.0)
        mine = slice(r * rows, (r + 1) * rows)
        matrix[:, mine] = total.astype(BF16)
        matrix_t[mine] = total.T.astype(BF16)
    step = min(cols, 256)
    for c in range(0, cols, step):
        at = slice(c, c + step)
        q_all = jnp.concatenate([piece[:rows, at] for piece in pieces], axis=0)
        p_all = jnp.concatenate([piece[rows : 2 * rows, at] for piece in pieces], axis=0)
        grad_q = dot(matrix_t[...], p_all, ((1,), (0,))).astype(BF16)
        grad_p = dot(matrix[...], q_all, ((1,), (0,))).astype(BF16)
        for r in range(groups):
            mine = slice(r * rows, (r + 1) * rows)
            outs[r][:rows, at] = grad_q[mine]
            outs[r][rows:, at] = grad_p[mine]


def pass_body(source, token, out):
    out[...] = source[...]


def choose_body(n1_ref, e3_ref, out):
    odd = lax.axis_index("blk") % 2 == 1

    @pl.when(odd)
    def _():
        out[...] = n1_ref[...]

    @pl.when(jnp.logical_not(odd))
    def _():
        out[...] = e3_ref[...]


def scores_body(q_ref, *refs):
    half = len(refs) // 2
    for block, out in zip(refs[:half], refs[half:]):
        out[...] = dot(block[...], q_ref[...], ((1,), (1,)))


def weigh_body(groups, q_ref, s0_ref, s1_ref, s2_ref, s3_ref, last_ref, w_ref, *refs):
    hard_refs = refs[:groups]
    loss_ref, coef_ref, hard_out, term3_ref, term2_ref = refs[groups:]
    rows, width = q_ref.shape
    w = w_ref[...]
    s3 = INV_TEMP * (s3_ref[...] + dot(last_ref[...], q_ref[...], ((1,), (1,))))
    scores = [INV_TEMP * s0_ref[...], INV_TEMP * s1_ref[...], INV_TEMP * s2_ref[...], s3]
    hard = hard_refs[0][...]
    for other in hard_refs[1:]:
        hard = hard + other[...]
    hard = INV_TEMP * hard
    largest = jnp.max(hard, axis=0, keepdims=True)
    for block in scores:
        largest = jnp.maximum(largest, jnp.max(block, axis=0, keepdims=True))
    summed = jnp.sum(jnp.exp(hard - largest), axis=0, keepdims=True)
    for block in scores:
        summed = summed + jnp.sum(jnp.exp(block - largest), axis=0, keepdims=True)
    log_total = largest + jnp.log(summed)
    for s in range(4):
        coef_ref[s * rows : (s + 1) * rows] = (w * jnp.exp(scores[s] - log_total)).astype(BF16)
    for c in range(0, width, CHUNK):
        at = slice(c, c + CHUNK)
        both = dot(coef_ref[2 * rows :], q_ref[:, at], ((1,), (0,))).astype(BF16)
        term2_ref[:, at] = both[:rows]
        term3_ref[:, at] = both[rows:]
    hard_out[...] = (w * jnp.exp(hard - log_total)).astype(BF16).astype(F32)
    eye = lax.broadcasted_iota(jnp.int32, (rows, rows), 0) == lax.broadcasted_iota(
        jnp.int32, (rows, rows), 1
    )
    loss_ref[...] = log_total - jnp.sum(jnp.where(eye, scores[0], 0.0), axis=0, keepdims=True)


def add_body(a_ref, b_ref, out, token):
    signal(token)
    out[...] = (a_ref[...].astype(F32) + b_ref[...].astype(F32)).astype(BF16)


def term1_body(q_ref, coef_ref, got2_ref, token, out):
    rows, width = q_ref.shape
    keep = jnp.where(lax.axis_index("blk") % 2 == 1, 1.0, 0.0)
    for c in range(0, width, CHUNK):
        at = slice(c, c + CHUNK)
        term1 = dot(coef_ref[rows : 2 * rows], q_ref[:, at], ((1,), (0,)))
        out[:, at] = term1 + keep * got2_ref[:, at].astype(F32)


def relay_body(partial1, got3_ref, out, done):
    signal(done)
    out[...] = (partial1[...] + got3_ref[...].astype(F32)).astype(BF16)


def base_body(
    q_ref, p_ref, n1_ref, n2_ref, e3_ref, o3_ref, coef_ref, w_ref, own3_ref, token, pulled, base
):
    rows, width = q_ref.shape
    w = jnp.broadcast_to(w_ref[...], (rows, rows)).T[:, :1]
    blocks = (p_ref, n1_ref, n2_ref, e3_ref, o3_ref)
    coef_t = coef_ref[...].astype(F32).T.astype(BF16)
    coef_t = jnp.concatenate([coef_t, coef_t[:, 3 * rows :]], axis=1)
    for c in range(0, width, CHUNK):
        at = slice(c, c + CHUNK)
        held = jnp.concatenate([block[:, at] for block in blocks], axis=0)
        pulled[:, at] = dot(coef_t, held, ((1,), (0,))) - w * p_ref[:, at].astype(F32)
        own = dot(coef_ref[:rows], q_ref[:, at], ((1,), (0,))) + own3_ref[:, at].astype(F32)
        base[:, at] = own - w * q_ref[:, at].astype(F32)


def finish_body(groups, pulled, base, own1, *refs):
    backs = refs[:groups]
    q_out, p_out, q_held, p_held, sems = refs[groups:]
    rows, cols = pulled.shape[0], backs[0].shape[1]
    g = lax.axis_index("grp")
    copies = []
    for r, back in enumerate(backs):
        at = pl.ds(pl.multiple_of((g ^ r) * cols, 128), cols)
        q_held[:, at] = (INV_TEMP * (pulled[:, at] + back[:rows].astype(F32))).astype(BF16)
        copies.append(pltpu.make_async_copy(q_held.at[:, at], q_out.at[:, at], sems.at[2 * r]))
        copies[-1].start()
        total = base[:, at] + back[rows:].astype(F32) + own1[:, at].astype(F32)
        p_held[:, at] = (INV_TEMP * total).astype(BF16)
        copies.append(pltpu.make_async_copy(p_held.at[:, at], p_out.at[:, at], sems.at[2 * r + 1]))
        copies[-1].start()
    for copy in copies:
        copy.wait()


def per_device(queries, passages, hard_index, weights):
    rows, width = queries.shape
    groups = lax.axis_size("grp")
    loop = lax.axis_size("blk")
    cols = width // groups

    def shift(array, by, which=(0, 1)):
        pairs = [(i, (i + by) % loop) for i in range(loop) if i % 2 in which]
        return lax.ppermute(array, "blk", pairs)

    def swap(array):
        return lax.ppermute(array, "blk", [(i, i ^ 1) for i in range(loop)])

    def exchange(arrays):
        out = list(arrays)
        for r in reversed(range(1, groups)):
            out[r] = lax.ppermute(arrays[r], "grp", [(i, i ^ r) for i in range(groups)])
        return out

    def like(*shape, dtype=BF16):
        return jax.ShapeDtypeStruct(shape, dtype)

    block, block32 = like(rows, width), like(rows, width, dtype=F32)
    square, triple = like(rows, rows, dtype=F32), like(3, rows, dtype=F32)
    piece, back = like(2 * rows + TAIL, cols), like(2 * rows, cols)

    next1 = shift(passages, -1)

    held_q, held_p, *pieces, token = local_call(
        functools.partial(load_body, groups, loop * rows),
        [block, block] + [piece] * groups + [TOKEN],
        queries, passages, hard_index.T,
        in_specs=[HBM, HBM, VMEM],
        scratch=[pltpu.SemaphoreType.DMA((2 * groups,))],
    )
    pieces = exchange(pieces)

    next3_even = shift(held_p, -3, (1,))
    (next1,) = local_call(pass_body, [block], next1, token, flops=LONG)
    next3_odd = shift(next1, -2, (1,))
    next2 = swap(local_call(choose_body, [block], next1, next3_even, flops=LONG)[0])

    s0, s1, s3 = local_call(scores_body, [square] * 3, held_q, held_p, next1, next3_even)
    hard_parts = exchange(
        local_call(
            functools.partial(hard_scores_body, groups), [triple] * groups, *pieces, s0, flops=LONG
        )
    )
    (s2,) = local_call(scores_body, [square], held_q, next2)
    loss_rows, coef, hard_coef, term3, term2 = local_call(
        functools.partial(weigh_body, groups),
        [like(1, rows, dtype=F32), like(4 * rows, rows), triple, block, block],
        held_q, s0, s1, s2, s3, next3_odd, weights[None, :], *hard_parts,
    )

    got3 = shift(term3, 2, (1,))
    got2 = swap(term2)

    sent3, token = local_call(add_body, [block, TOKEN], term3, got2)
    own3 = shift(sent3, 3, (0,))

    hard_coefs = exchange([hard_coef] * groups)
    square_all = pltpu.VMEM((groups * rows, groups * rows), BF16)
    *backs, token = local_call(
        functools.partial(hard_grads_body, groups), [back] * groups + [TOKEN],
        *pieces, *hard_coefs, token, scratch=[square_all, square_all],
    )
    backs = exchange(backs)

    (partial1,) = local_call(term1_body, [block32], held_q, coef, got2, token)
    sent1, token = local_call(relay_body, [block, TOKEN], partial1, got3, flops=SOME)
    own1 = shift(sent1, 1)

    pulled, base = local_call(
        base_body, [block32, block32],
        held_q, held_p, next1, next2, next3_even, next3_odd, coef, weights[None, :], own3, token,
        flops=LONG,
    )
    grad_queries, grad_passages = local_call(
        functools.partial(finish_body, groups), [block, block], pulled, base, own1, *backs,
        out_specs=[HBM, HBM],
        scratch=[
            pltpu.VMEM((rows, width), BF16),
            pltpu.VMEM((rows, width), BF16),
            pltpu.SemaphoreType.DMA((2 * groups,)),
        ],
    )
    return loss_rows.reshape(rows), grad_queries, grad_passages


def solution(mesh):
    rows = P(("grp", "blk"))
    matrix = P(("grp", "blk"), None)
    return jax.shard_map(
        per_device,
        mesh=mesh,
        in_specs=(matrix, matrix, matrix, rows),
        out_specs=(rows, matrix, matrix),
        check_vma=False,
    )
```

```python
import functools
import math

import jax
import jax.numpy as jnp
from jax import lax
from jax.experimental import pallas as pl
from jax.experimental.pallas import tpu as pltpu
from jax.sharding import PartitionSpec as P

INV_TEMP = 50.0
BF16 = jnp.bfloat16
F32 = jnp.float32
CHUNK = 512
TAIL = 16
LONG = 5 * 10**10
VMEM = pl.BlockSpec(memory_space=pltpu.VMEM)
HBM = pl.BlockSpec(memory_space=pltpu.HBM)
TOKEN = jax.ShapeDtypeStruct((8, 128), F32)


def dot(left, right, dims):
    return lax.dot_general(left, right, (dims, ((), ())), preferred_element_type=F32)


def size_of(arrays):
    return sum(math.prod(a.shape) * jnp.dtype(a.dtype).itemsize for a in arrays)


def local_call(body, out_shape, *args, flops=0, in_specs=None, out_specs=None, scratch=()):
    return pl.pallas_call(
        body,
        out_shape=out_shape,
        in_specs=in_specs or [VMEM] * len(args),
        out_specs=out_specs or [VMEM] * len(out_shape),
        scratch_shapes=list(scratch),
        cost_estimate=pl.CostEstimate(
            flops=flops, bytes_accessed=size_of(args) + size_of(out_shape), transcendentals=0
        ),
        compiler_params=pltpu.CompilerParams(vmem_limit_bytes=20 * 2**20),
    )(*args)


def signal(token):
    token[...] = jnp.zeros(token.shape, token.dtype)


def split_index(index, rows, group_rows):
    if group_rows & (group_rows - 1) or rows & (rows - 1):
        return index // group_rows, index % rows
    return index >> (group_rows.bit_length() - 1), index & (rows - 1)


def load_body(groups, group_rows, q_hbm, p_hbm, index_ref, q_ref, p_ref, *refs):
    pieces, token, sems = refs[:groups], refs[groups], refs[groups + 1]
    rows = q_ref.shape[0]
    cols = pieces[0].shape[1]
    g = lax.axis_index("grp")
    copies = []
    for r in range(groups):
        at = pl.ds(pl.multiple_of((g ^ r) * cols, 128), cols)
        pair = [
            pltpu.make_async_copy(source.at[:, at], target.at[:, at], sems.at[2 * r + n])
            for n, (source, target) in enumerate(((q_hbm, q_ref), (p_hbm, p_ref)))
        ]
        for copy in pair:
            copy.start()
        copies.append((at, pair))
    signal(token)
    index = jnp.concatenate([index_ref[...], jnp.zeros((TAIL - 3, rows), jnp.int32)], axis=0)
    named_group, named_row = split_index(index, rows, group_rows)
    named_group = named_group.astype(F32).astype(BF16)
    named_row = named_row.astype(F32).astype(BF16)
    for r in reversed(range(groups)):
        at, pair = copies[r]
        for copy in pair:
            copy.wait()
        pieces[r][:rows] = q_ref[:, at]
        pieces[r][rows : 2 * rows] = p_ref[:, at]
        pieces[r][2 * rows :, :rows] = named_group
        pieces[r][2 * rows :, rows : 2 * rows] = named_row


def places_of(piece_ref, rows):
    tail = piece_ref[2 * rows :, : 2 * rows].astype(F32).astype(jnp.int32)
    g = lax.axis_index("grp")
    return [(tail[k : k + 1, :rows] ^ g) * rows + tail[k : k + 1, rows:] for k in range(3)]


def hard_scores_body(groups, q_ref, *refs):
    pieces, outs, later = refs[:groups], refs[groups + 1 : -1], refs[-1]
    rows = outs[0].shape[1]
    ids = lax.broadcasted_iota(jnp.int32, (groups * rows, rows), 0)
    p_all = jnp.concatenate([piece[rows : 2 * rows] for piece in pieces], axis=0)
    for r in range(groups):
        places = places_of(pieces[r], rows)
        dots = dot(p_all, pieces[r][:rows], ((1,), (1,)))
        for k in range(3):
            hit = jnp.where(ids == places[k], dots, 0.0)
            outs[r][k : k + 1] = jnp.sum(hit, axis=0, keepdims=True)
    later[...] = q_ref[...]


def hard_grads_body(groups, *refs):
    pieces, coefs, out = refs[:groups], refs[groups : 2 * groups], refs[2 * groups]
    token, matrix, matrix_t = refs[2 * groups + 1 :]
    rows = coefs[0].shape[1]
    cols = out.shape[2]
    g = lax.axis_index("grp")
    signal(token)
    ids = lax.broadcasted_iota(jnp.int32, (groups * rows, rows), 0)
    for r in range(groups):
        places = places_of(pieces[r], rows)
        total = jnp.zeros(ids.shape, F32)
        for k in range(3):
            total += jnp.where(ids == places[k], coefs[r][k : k + 1], 0.0)
        mine = slice(r * rows, (r + 1) * rows)
        matrix[:, mine] = total.astype(BF16)
        matrix_t[mine] = total.T.astype(BF16)
    step = min(cols, 256)
    for c in range(0, cols, step):
        at = slice(c, c + step)
        q_all = jnp.concatenate([piece[:rows, at] for piece in pieces], axis=0)
        p_all = jnp.concatenate([piece[rows : 2 * rows, at] for piece in pieces], axis=0)
        grad_q = dot(matrix_t[...], p_all, ((1,), (0,))).astype(BF16)
        grad_p = dot(matrix[...], q_all, ((1,), (0,))).astype(BF16)
        for r in range(groups):
            mine = slice(r * rows, (r + 1) * rows)
            out[g ^ r, :rows, at] = grad_q[mine]
            out[g ^ r, rows:, at] = grad_p[mine]


def pass_body(source, token, out):
    out[...] = source[...]


def choose_body(parity, first_ref, second_ref, out):
    here = lax.axis_index("blk") % 2 == parity

    @pl.when(here)
    def _():
        out[...] = first_ref[...]

    @pl.when(jnp.logical_not(here))
    def _():
        out[...] = second_ref[...]


def scores_body(q_ref, *refs):
    half = len(refs) // 2
    for block, out in zip(refs[:half], refs[half:]):
        out[...] = dot(block[...], q_ref[...], ((1,), (1,)))


def weigh_body(groups, q_ref, s0_ref, s1_ref, s2_ref, s3_ref, last_ref, w_ref, *refs):
    parts = refs[:groups]
    loss_ref, hard_out, *coef_refs = refs[groups:]
    rows = q_ref.shape[0]
    w = w_ref[...]
    s3 = INV_TEMP * (s3_ref[...] + dot(last_ref[...], q_ref[...], ((1,), (1,))))
    scores = [INV_TEMP * s0_ref[...], INV_TEMP * s1_ref[...], INV_TEMP * s2_ref[...], s3]
    hard = parts[0][...]
    for other in parts[1:]:
        hard = hard + other[...]
    hard = INV_TEMP * hard
    largest = jnp.max(hard, axis=0, keepdims=True)
    for block in scores:
        largest = jnp.maximum(largest, jnp.max(block, axis=0, keepdims=True))
    summed = jnp.sum(jnp.exp(hard - largest), axis=0, keepdims=True)
    for block in scores:
        summed = summed + jnp.sum(jnp.exp(block - largest), axis=0, keepdims=True)
    log_total = largest + jnp.log(summed)
    hard_out[...] = (w * jnp.exp(hard - log_total)).astype(BF16).astype(F32)
    for block, coef_ref in zip(scores, coef_refs):
        coef_ref[...] = (w * jnp.exp(block - log_total)).astype(BF16)
    eye = lax.broadcasted_iota(jnp.int32, (rows, rows), 0) == lax.broadcasted_iota(
        jnp.int32, (rows, rows), 1
    )
    loss_ref[...] = log_total - jnp.sum(jnp.where(eye, scores[0], 0.0), axis=0, keepdims=True)


def column(row_ref, rows):
    return jnp.broadcast_to(row_ref[...], (rows, rows)).T[:, :1]


def queries_body(p_ref, n1_ref, n2_ref, e3_ref, o3_ref, w_ref, *refs):
    coefs, pulled, sent, coef_t = refs[:4], refs[5], refs[6:9], refs[9]
    for coef, out in zip(coefs[1:], sent):
        out[...] = coef[...]
    rows, width = p_ref.shape
    w = column(w_ref, rows)
    for s in range(5):
        coef_t[:, s * rows : (s + 1) * rows] = coefs[min(s, 3)][...].astype(F32).T.astype(BF16)
    blocks = (p_ref, n1_ref, n2_ref, e3_ref, o3_ref)
    for c in range(0, width, CHUNK):
        at = slice(c, c + CHUNK)
        held = jnp.concatenate([block[:, at] for block in blocks], axis=0)
        pulled[:, at] = dot(coef_t[...], held, ((1,), (0,))) - w * p_ref[:, at].astype(F32)


def passages_body(q_ref, m1_ref, m2_ref, u3_ref, w_ref, *refs):
    coefs, base = refs[:4], refs[-1]
    rows, width = q_ref.shape
    w = column(w_ref, rows)
    coef = jnp.concatenate([coef[...] for coef in coefs], axis=1)
    for c in range(0, width, CHUNK):
        at = slice(c, c + CHUNK)
        held = jnp.concatenate([ref[:, at] for ref in (q_ref, m1_ref, m2_ref, u3_ref)], axis=0)
        base[:, at] = dot(coef, held, ((1,), (0,))) - w * q_ref[:, at].astype(F32)


def finish_body(groups, pulled, base, r3_ref, coef3, *refs):
    backs, q_out, p_out, q_held, p_held, sems = refs
    rows, cols = pulled.shape[0], backs.shape[2]
    copies = []
    for r in range(groups):
        back = backs.at[r]
        at = slice(r * cols, (r + 1) * cols)
        q_held[:, at] = (INV_TEMP * (pulled[:, at] + back[:rows].astype(F32))).astype(BF16)
        copies.append(pltpu.make_async_copy(q_held.at[:, at], q_out.at[:, at], sems.at[2 * r]))
        copies[-1].start()
        total = base[:, at] + dot(coef3[...], r3_ref[:, at], ((1,), (0,)))
        p_held[:, at] = (INV_TEMP * (total + back[rows:].astype(F32))).astype(BF16)
        copies.append(pltpu.make_async_copy(p_held.at[:, at], p_out.at[:, at], sems.at[2 * r + 1]))
        copies[-1].start()
    for copy in copies:
        copy.wait()


def per_device(queries, passages, hard_index, weights):
    rows, width = queries.shape
    groups = lax.axis_size("grp")
    loop = lax.axis_size("blk")
    cols = width // groups

    def shift(array, by, which=(0, 1)):
        pairs = [(i, (i + by) % loop) for i in range(loop) if i % 2 in which]
        return lax.ppermute(array, "blk", pairs)

    def swap(array):
        return lax.ppermute(array, "blk", [(i, i ^ 1) for i in range(loop)])

    def exchange(arrays):
        out = list(arrays)
        for r in reversed(range(1, groups)):
            out[r] = lax.ppermute(arrays[r], "grp", [(i, i ^ r) for i in range(groups)])
        return out

    def like(*shape, dtype=BF16):
        return jax.ShapeDtypeStruct(shape, dtype)

    block, block32 = like(rows, width), like(rows, width, dtype=F32)
    square, square32 = like(rows, rows), like(rows, rows, dtype=F32)
    row, triple = like(1, rows, dtype=F32), like(3, rows, dtype=F32)
    piece, back = like(2 * rows + TAIL, cols), like(groups, 2 * rows, cols)

    next1 = shift(passages, -1)

    held_q, held_p, *pieces, token = local_call(
        functools.partial(load_body, groups, loop * rows),
        [block, block] + [piece] * groups + [TOKEN],
        queries, passages, hard_index.T,
        in_specs=[HBM, HBM, VMEM],
        scratch=[pltpu.SemaphoreType.DMA((2 * groups,))],
    )
    pieces = exchange(pieces)

    next3_even = shift(held_p, -3, (1,))
    (next1,) = local_call(pass_body, [block], next1, token, flops=LONG)
    next3_odd = shift(next1, -2, (1,))
    (held,) = local_call(
        functools.partial(choose_body, 1), [block], next1, next3_even, flops=LONG
    )
    next2 = swap(held)

    s0, s1, s3 = local_call(scores_body, [square32] * 3, held_q, held_p, next1, next3_even)
    (s2,) = local_call(scores_body, [square32], held_q, next2)
    *parts, later_q = local_call(
        functools.partial(hard_scores_body, groups),
        [triple] * groups + [block], held_q, *pieces, s0, flops=LONG,
    )
    parts = exchange(parts)
    prev1 = shift(later_q, 1)
    loss_rows, hard_coef, *coefs = local_call(
        functools.partial(weigh_body, groups), [row, triple] + [square] * 4,
        held_q, s0, s1, s2, s3, next3_odd, weights[None, :], *parts,
    )

    (later_q,) = local_call(pass_body, [block], held_q, hard_coef)
    prev3_odd = shift(later_q, 3, (0,))
    hard_coefs = exchange([hard_coef] * groups)
    wide = pltpu.VMEM((groups * rows, groups * rows), BF16)
    backs, token = local_call(
        functools.partial(hard_grads_body, groups), [back, TOKEN],
        *pieces, *hard_coefs, scratch=[wide, wide],
    )
    backs = lax.all_to_all(backs, "grp", split_axis=0, concat_axis=0, tiled=True)

    (prev1,) = local_call(pass_body, [block], prev1, token)
    prev3_even = shift(prev1, 2, (0,))
    (held,) = local_call(functools.partial(choose_body, 0), [block], prev1, prev3_odd)
    prev2 = swap(held)

    pulled, *sent = local_call(
        queries_body, [block32] + [square] * 3,
        held_p, next1, next2, next3_even, next3_odd, weights[None, :], *coefs, token,
        scratch=[pltpu.VMEM((rows, 5 * rows), BF16)],
    )
    came = [coefs[0]] + [shift(sent[n - 1], n) for n in range(1, 4)]
    (base,) = local_call(
        passages_body, [block32],
        held_q, prev1, prev2, prev3_odd, weights[None, :], *came,
    )
    grad_queries, grad_passages = local_call(
        functools.partial(finish_body, groups), [block, block],
        pulled, base, prev3_even, came[3], backs,
        out_specs=[HBM, HBM],
        scratch=[
            pltpu.VMEM((rows, width), BF16),
            pltpu.VMEM((rows, width), BF16),
            pltpu.SemaphoreType.DMA((2 * groups,)),
        ],
    )
    return loss_rows.reshape(rows), grad_queries, grad_passages


def solution(mesh):
    rows = P(("grp", "blk"))
    matrix = P(("grp", "blk"), None)
    return jax.shard_map(
        per_device,
        mesh=mesh,
        in_specs=(matrix, matrix, matrix, rows),
        out_specs=(rows, matrix, matrix),
        check_vma=False,
    )
```

```python
import functools
import math

import jax
import jax.numpy as jnp
from jax import lax
from jax.experimental import pallas as pl
from jax.experimental.pallas import tpu as pltpu
from jax.sharding import PartitionSpec as P

INV_TEMP = 50.0
BF16 = jnp.bfloat16
F32 = jnp.float32
CHUNK = 512
TAIL = 16
LONG, SOME, PART = 5 * 10**10, 16 * 10**9, 8 * 10**9
VMEM = pl.BlockSpec(memory_space=pltpu.VMEM)
HBM = pl.BlockSpec(memory_space=pltpu.HBM)
TOKEN = jax.ShapeDtypeStruct((8, 128), F32)


def dot(left, right, dims):
    return lax.dot_general(left, right, (dims, ((), ())), preferred_element_type=F32)


def size_of(arrays):
    return sum(math.prod(a.shape) * jnp.dtype(a.dtype).itemsize for a in arrays)


def local_call(body, out_shape, *args, flops=0, in_specs=None, out_specs=None, scratch=()):
    return pl.pallas_call(
        body,
        out_shape=out_shape,
        in_specs=in_specs or [VMEM] * len(args),
        out_specs=out_specs or [VMEM] * len(out_shape),
        scratch_shapes=list(scratch),
        cost_estimate=pl.CostEstimate(
            flops=flops, bytes_accessed=size_of(args) + size_of(out_shape), transcendentals=0
        ),
        compiler_params=pltpu.CompilerParams(vmem_limit_bytes=20 * 2**20),
    )(*args)


def signal(token):
    token[...] = jnp.zeros(token.shape, token.dtype)


def split_index(index, rows, group_rows):
    if group_rows & (group_rows - 1) or rows & (rows - 1):
        return index // group_rows, index % rows
    return index >> (group_rows.bit_length() - 1), index & (rows - 1)


def load_body(groups, group_rows, q_hbm, p_hbm, index_ref, q_ref, p_ref, *refs):
    pieces, token, sems = refs[:groups], refs[groups], refs[groups + 1]
    rows = q_ref.shape[0]
    cols = pieces[0].shape[1]
    g = lax.axis_index("grp")
    copies = []
    for r in range(groups):
        at = pl.ds(pl.multiple_of((g ^ r) * cols, 128), cols)
        pair = [
            pltpu.make_async_copy(source.at[:, at], target.at[:, at], sems.at[2 * r + n])
            for n, (source, target) in enumerate(((q_hbm, q_ref), (p_hbm, p_ref)))
        ]
        for copy in pair:
            copy.start()
        copies.append((at, pair))
    signal(token)
    index = jnp.concatenate([index_ref[...], jnp.zeros((TAIL - 3, rows), jnp.int32)], axis=0)
    named_group, named_row = split_index(index, rows, group_rows)
    named_group = named_group.astype(F32).astype(BF16)
    named_row = named_row.astype(F32).astype(BF16)
    for r in reversed(range(groups)):
        at, pair = copies[r]
        for copy in pair:
            copy.wait()
        pieces[r][:rows] = q_ref[:, at]
        pieces[r][rows : 2 * rows] = p_ref[:, at]
        pieces[r][2 * rows :, :rows] = named_group
        pieces[r][2 * rows :, rows : 2 * rows] = named_row


def places_of(piece_ref, rows):
    tail = piece_ref[2 * rows :, : 2 * rows].astype(F32).astype(jnp.int32)
    g = lax.axis_index("grp")
    return [(tail[k : k + 1, :rows] ^ g) * rows + tail[k : k + 1, rows:] for k in range(3)]


def hard_scores_body(groups, *refs):
    pieces, outs = refs[:groups], refs[groups + 1 :]
    rows = outs[0].shape[1]
    ids = lax.broadcasted_iota(jnp.int32, (groups * rows, rows), 0)
    p_all = jnp.concatenate([piece[rows : 2 * rows] for piece in pieces], axis=0)
    for r in range(groups):
        places = places_of(pieces[r], rows)
        dots = dot(p_all, pieces[r][:rows], ((1,), (1,)))
        for k in range(3):
            hit = jnp.where(ids == places[k], dots, 0.0)
            outs[r][k : k + 1] = jnp.sum(hit, axis=0, keepdims=True)


def hard_grads_body(groups, *refs):
    pieces, coefs, outs = refs[:groups], refs[groups : 2 * groups], refs[2 * groups : 3 * groups]
    token, matrix, matrix_t = refs[3 * groups :]
    rows = coefs[0].shape[1]
    cols = outs[0].shape[1]
    signal(token)
    ids = lax.broadcasted_iota(jnp.int32, (groups * rows, rows), 0)
    for r in range(groups):
        places = places_of(pieces[r], rows)
        total = jnp.zeros(ids.shape, F32)
        for k in range(3):
            total += jnp.where(ids == places[k], coefs[r][k : k + 1], 0.0)
        mine = slice(r * rows, (r + 1) * rows)
        matrix[:, mine] = total.astype(BF16)
        matrix_t[mine] = total.T.astype(BF16)
    step = min(cols, 256)
    for c in range(0, cols, step):
        at = slice(c, c + step)
        q_all = jnp.concatenate([piece[:rows, at] for piece in pieces], axis=0)
        p_all = jnp.concatenate([piece[rows : 2 * rows, at] for piece in pieces], axis=0)
        grad_q = dot(matrix_t[...], p_all, ((1,), (0,))).astype(BF16)
        grad_p = dot(matrix[...], q_all, ((1,), (0,))).astype(BF16)
        for r in range(groups):
            mine = slice(r * rows, (r + 1) * rows)
            outs[r][:rows, at] = grad_q[mine]
            outs[r][rows:, at] = grad_p[mine]


def pass_body(source, token, out):
    out[...] = source[...]


def choose_body(n1_ref, e3_ref, out):
    odd = lax.axis_index("blk") % 2 == 1

    @pl.when(odd)
    def _():
        out[...] = n1_ref[...]

    @pl.when(jnp.logical_not(odd))
    def _():
        out[...] = e3_ref[...]


def scores_body(q_ref, *refs):
    half = len(refs) // 2
    for block, out in zip(refs[:half], refs[half:]):
        out[...] = dot(block[...], q_ref[...], ((1,), (1,)))


def last_score_body(q_ref, block, token, out, later):
    out[...] = dot(block[...], q_ref[...], ((1,), (1,)))
    later[...] = q_ref[...]


def weigh_body(groups, q_ref, s0_ref, s1_ref, s2_ref, s3_ref, last_ref, w_ref, *refs):
    parts = refs[:groups]
    loss_ref, hard_out, coef_ref, sent_ref = refs[groups:]
    rows = q_ref.shape[0]
    w = w_ref[...]
    s3 = INV_TEMP * (s3_ref[...] + dot(last_ref[...], q_ref[...], ((1,), (1,))))
    scores = [INV_TEMP * s0_ref[...], INV_TEMP * s1_ref[...], INV_TEMP * s2_ref[...], s3]
    hard = parts[0][...]
    for other in parts[1:]:
        hard = hard + other[...]
    hard = INV_TEMP * hard
    largest = jnp.max(hard, axis=0, keepdims=True)
    for block in scores:
        largest = jnp.maximum(largest, jnp.max(block, axis=0, keepdims=True))
    summed = jnp.sum(jnp.exp(hard - largest), axis=0, keepdims=True)
    for block in scores:
        summed = summed + jnp.sum(jnp.exp(block - largest), axis=0, keepdims=True)
    log_total = largest + jnp.log(summed)
    hard_out[...] = (w * jnp.exp(hard - log_total)).astype(BF16).astype(F32)
    for s, block in enumerate(scores):
        coef = (w * jnp.exp(block - log_total)).astype(BF16)
        coef_ref[:, s * rows : (s + 1) * rows] = coef
        if s > 1:
            sent_ref[:, (s - 2) * rows : (s - 1) * rows] = coef
    eye = lax.broadcasted_iota(jnp.int32, (rows, rows), 0) == lax.broadcasted_iota(
        jnp.int32, (rows, rows), 1
    )
    loss_ref[...] = log_total - jnp.sum(jnp.where(eye, scores[0], 0.0), axis=0, keepdims=True)


def column(row_ref, rows):
    return jnp.broadcast_to(row_ref[...], (rows, rows)).T[:, :1]


def send_body(q_ref, coef_ref, other_ref, out):
    rows, width = q_ref.shape
    out[:, :width] = q_ref[...]
    out[:, width : width + 3 * rows] = coef_ref[:, rows:]
    out[:, width + 3 * rows :] = other_ref[...]


def relay_body(m1_ref, u3_ref, token, to_core, to_chip):
    rows, width = u3_ref.shape
    odd = lax.axis_index("blk") % 2 == 1
    part = [m1_ref[:, width + n * rows : width + (n + 1) * rows] for n in range(5)]

    @pl.when(odd)
    def _():
        to_core[:, :width] = u3_ref[...]

    @pl.when(jnp.logical_not(odd))
    def _():
        to_core[:, :width] = m1_ref[:, :width]

    to_core[:, width : width + rows] = part[1]
    to_core[:, width + rows :] = part[4]
    to_chip[:, :width] = m1_ref[:, :width]
    to_chip[:, width:] = part[2]


def queries_body(p_ref, n1_ref, n2_ref, e3_ref, o3_ref, w_ref, coef_ref, token, pulled, coef_t):
    rows, width = p_ref.shape
    w = column(w_ref, rows)
    for s in range(5):
        k = min(s, 3) * rows
        coef_t[:, s * rows : (s + 1) * rows] = coef_ref[:, k : k + rows].astype(F32).T.astype(BF16)
    blocks = (p_ref, n1_ref, n2_ref, e3_ref, o3_ref)
    for c in range(0, width, CHUNK):
        at = slice(c, c + CHUNK)
        held = jnp.concatenate([block[:, at] for block in blocks], axis=0)
        pulled[:, at] = dot(coef_t[...], held, ((1,), (0,))) - w * p_ref[:, at].astype(F32)


def passages_body(q_ref, m1_ref, w_ref, coef_ref, base):
    rows, width = q_ref.shape
    w = column(w_ref, rows)
    coef = jnp.concatenate([coef_ref[:, :rows], m1_ref[:, width : width + rows]], axis=1)
    for c in range(0, width, CHUNK):
        at = slice(c, c + CHUNK)
        held = jnp.concatenate([q_ref[:, at], m1_ref[:, at]], axis=0)
        base[:, at] = dot(coef, held, ((1,), (0,))) - w * q_ref[:, at].astype(F32)


def gather_body(groups, pulled, base, *refs):
    backs, (out, almost, held, sems) = refs[:groups], refs[groups:]
    rows, cols = pulled.shape[0], backs[0].shape[1]
    g = lax.axis_index("grp")
    copies = []
    for r, back in enumerate(backs):
        at = pl.ds(pl.multiple_of((g ^ r) * cols, 128), cols)
        held[:, at] = (INV_TEMP * (pulled[:, at] + back[:rows].astype(F32))).astype(BF16)
        copies.append(pltpu.make_async_copy(held.at[:, at], out.at[:, at], sems.at[r]))
        copies[-1].start()
        almost[:, at] = base[:, at] + back[rows:].astype(F32)
    for copy in copies:
        copy.wait()


def finish_body(almost, m1_ref, m2_ref, u3_ref, r3_ref, out, held, sems):
    rows, width = almost.shape
    odd = lax.axis_index("blk") % 2 == 1
    mine = m1_ref[:, width + 3 * rows : width + 4 * rows]
    coef = [jnp.where(odd, m2_ref[:, width : width + rows], mine)]
    coef = jnp.concatenate(coef + [m2_ref[:, width + rows :], r3_ref[:, width:]], axis=1)
    copies = []
    for n, c in enumerate(range(0, width, CHUNK)):
        at = slice(c, c + CHUNK)
        block = jnp.concatenate([m2_ref[:, at], u3_ref[:, at], r3_ref[:, at]], axis=0)
        held[:, at] = (INV_TEMP * (almost[:, at] + dot(coef, block, ((1,), (0,))))).astype(BF16)
        copies.append(pltpu.make_async_copy(held.at[:, at], out.at[:, at], sems.at[n]))
        copies[-1].start()
    for copy in copies:
        copy.wait()


def per_device(queries, passages, hard_index, weights):
    rows, width = queries.shape
    groups = lax.axis_size("grp")
    loop = lax.axis_size("blk")
    cols = width // groups

    def shift(array, by, which=(0, 1)):
        pairs = [(i, (i + by) % loop) for i in range(loop) if i % 2 in which]
        return lax.ppermute(array, "blk", pairs)

    def swap(array):
        return lax.ppermute(array, "blk", [(i, i ^ 1) for i in range(loop)])

    def exchange(arrays):
        out = list(arrays)
        for r in reversed(range(1, groups)):
            out[r] = lax.ppermute(arrays[r], "grp", [(i, i ^ r) for i in range(groups)])
        return out

    def like(*shape, dtype=BF16):
        return jax.ShapeDtypeStruct(shape, dtype)

    block, block32 = like(rows, width), like(rows, width, dtype=F32)
    square, square32 = like(rows, rows), like(rows, rows, dtype=F32)
    row, triple = like(1, rows, dtype=F32), like(3, rows, dtype=F32)
    piece, back = like(2 * rows + TAIL, cols), like(2 * rows, cols)

    next1 = shift(passages, -1)

    held_q, held_p, *pieces, token = local_call(
        functools.partial(load_body, groups, loop * rows),
        [block, block] + [piece] * groups + [TOKEN],
        queries, passages, hard_index.T,
        in_specs=[HBM, HBM, VMEM],
        scratch=[pltpu.SemaphoreType.DMA((2 * groups,))],
    )
    pieces = exchange(pieces)

    next3_even = shift(held_p, -3, (1,))
    (next1,) = local_call(pass_body, [block], next1, token, flops=LONG)
    next3_odd = shift(next1, -2, (1,))
    (held,) = local_call(choose_body, [block], next1, next3_even, flops=LONG)
    next2 = swap(held)

    s0, s1, s3 = local_call(scores_body, [square32] * 3, held_q, held_p, next1, next3_even)
    parts = exchange(
        local_call(
            functools.partial(hard_scores_body, groups), [triple] * groups, *pieces, s0, flops=LONG
        )
    )
    s2, later_q = local_call(last_score_body, [square32, block], held_q, next2, parts[0])
    prev3_odd = shift(later_q, 3, (0,))
    loss_rows, hard_coef, coef, sent = local_call(
        functools.partial(weigh_body, groups),
        [row, triple, like(rows, 4 * rows), like(rows, 2 * rows)],
        held_q, s0, s1, s2, s3, next3_odd, weights[None, :], *parts,
    )

    other = lax.ppermute(sent, "blk", [(i, i + 1) for i in range(0, loop, 2)])
    (packed,) = local_call(send_body, [like(rows, width + 5 * rows)], held_q, coef, other)
    prev1 = shift(packed, 1)

    hard_coefs = exchange([hard_coef] * groups)
    wide = pltpu.VMEM((groups * rows, groups * rows), BF16)
    *backs, token = local_call(
        functools.partial(hard_grads_body, groups), [back] * groups + [TOKEN],
        *pieces, *hard_coefs, flops=PART, scratch=[wide, wide],
    )
    backs = exchange(backs)

    (prev3_odd,) = local_call(pass_body, [block], prev3_odd, token, flops=PART)
    to_core, to_chip = local_call(
        relay_body, [like(rows, width + 2 * rows), like(rows, width + rows)], prev1, prev3_odd, token,
    )
    prev3_even = shift(to_chip, 2, (0,))
    prev2 = swap(to_core)

    (pulled,) = local_call(
        queries_body, [block32],
        held_p, next1, next2, next3_even, next3_odd, weights[None, :], coef, token,
        scratch=[pltpu.VMEM((rows, 5 * rows), BF16)],
    )
    (base,) = local_call(
        passages_body, [block32], held_q, prev1, weights[None, :], coef
    )
    held_out = pltpu.VMEM((rows, width), BF16)
    grad_queries, almost = local_call(
        functools.partial(gather_body, groups), [block, block32], pulled, base, *backs,
        flops=SOME, out_specs=[HBM, VMEM],
        scratch=[held_out, pltpu.SemaphoreType.DMA((groups,))],
    )
    (grad_passages,) = local_call(
        finish_body, [block], almost, prev1, prev2, prev3_odd, prev3_even, out_specs=[HBM],
        scratch=[held_out, pltpu.SemaphoreType.DMA((width // CHUNK,))],
    )
    return loss_rows.reshape(rows), grad_queries, grad_passages


def solution(mesh):
    rows = P(("grp", "blk"))
    matrix = P(("grp", "blk"), None)
    return jax.shard_map(
        per_device,
        mesh=mesh,
        in_specs=(matrix, matrix, matrix, rows),
        out_specs=(rows, matrix, matrix),
        check_vma=False,
    )
```

```python
import functools
import math

import jax
import jax.numpy as jnp
from jax import lax
from jax.experimental import pallas as pl
from jax.experimental.pallas import tpu as pltpu
from jax.sharding import PartitionSpec as P

INV_TEMP = 50.0
BF16 = jnp.bfloat16
F32 = jnp.float32
CHUNK = 512
TAIL = 16
SLOT = 8
LONG, SOME = 5 * 10**10, 16 * 10**9
VMEM = pl.BlockSpec(memory_space=pltpu.VMEM)
HBM = pl.BlockSpec(memory_space=pltpu.HBM)
TOKEN = jax.ShapeDtypeStruct((8, 128), F32)


def dot(left, right, dims):
    return lax.dot_general(left, right, (dims, ((), ())), preferred_element_type=F32)


def size_of(arrays):
    return sum(math.prod(a.shape) * jnp.dtype(a.dtype).itemsize for a in arrays)


def local_call(body, out_shape, *args, flops=0, in_specs=None, out_specs=None, scratch=()):
    return pl.pallas_call(
        body,
        out_shape=out_shape,
        in_specs=in_specs or [VMEM] * len(args),
        out_specs=out_specs or [VMEM] * len(out_shape),
        scratch_shapes=list(scratch),
        cost_estimate=pl.CostEstimate(
            flops=flops, bytes_accessed=size_of(args) + size_of(out_shape), transcendentals=0
        ),
        compiler_params=pltpu.CompilerParams(vmem_limit_bytes=20 * 2**20),
    )(*args)


def signal(token):
    token[...] = jnp.zeros(token.shape, token.dtype)


def split_index(index, rows, group_rows):
    if group_rows & (group_rows - 1) or rows & (rows - 1):
        return index // group_rows, index % rows
    return index >> (group_rows.bit_length() - 1), index & (rows - 1)


def load_body(groups, group_rows, q_hbm, p_hbm, index_ref, q_ref, p_ref, *refs):
    pieces, token, sems = refs[:groups], refs[groups], refs[groups + 1]
    rows = q_ref.shape[0]
    cols = pieces[0].shape[1]
    g = lax.axis_index("grp")
    copies = []
    for r in range(groups):
        at = pl.ds(pl.multiple_of((g ^ r) * cols, 128), cols)
        pair = [
            pltpu.make_async_copy(source.at[:, at], target.at[:, at], sems.at[2 * r + n])
            for n, (source, target) in enumerate(((q_hbm, q_ref), (p_hbm, p_ref)))
        ]
        for copy in pair:
            copy.start()
        copies.append((at, pair))
    signal(token)
    index = jnp.concatenate([index_ref[...], jnp.zeros((TAIL - 3, rows), jnp.int32)], axis=0)
    named_group, named_row = split_index(index, rows, group_rows)
    named_group = named_group.astype(F32).astype(BF16)
    named_row = named_row.astype(F32).astype(BF16)
    for r in reversed(range(groups)):
        at, pair = copies[r]
        for copy in pair:
            copy.wait()
        pieces[r][:rows] = q_ref[:, at]
        pieces[r][rows : 2 * rows] = p_ref[:, at]
        pieces[r][2 * rows :, :rows] = named_group
        pieces[r][2 * rows :, rows : 2 * rows] = named_row


def places_of(piece_ref, rows):
    tail = piece_ref[2 * rows :, : 2 * rows].astype(F32).astype(jnp.int32)
    g = lax.axis_index("grp")
    return [(tail[k : k + 1, :rows] ^ g) * rows + tail[k : k + 1, rows:] for k in range(3)]


def bit_order(groups):
    order = [0]
    while len(order) < groups:
        order = [2 * r for r in order] + [2 * r + 1 for r in order]
    return order


def hard_scores_body(groups, *refs):
    pieces, (keep, give) = refs[:groups], refs[groups + 1 :]
    rows = keep.shape[1]
    ids = lax.broadcasted_iota(jnp.int32, (groups * rows, rows), 0)
    p_all = jnp.concatenate([piece[rows : 2 * rows] for piece in pieces], axis=0)
    keep[...] = jnp.zeros(keep.shape, F32)
    give[...] = jnp.zeros(give.shape, F32)
    for n, r in enumerate(bit_order(groups)):
        places = places_of(pieces[r], rows)
        dots = dot(p_all, pieces[r][:rows], ((1,), (1,)))
        out, slot = (keep, n) if n < groups // 2 else (give, n - groups // 2)
        for k in range(3):
            hit = jnp.where(ids == places[k], dots, 0.0)
            at = SLOT * slot + k
            out[at : at + 1] = jnp.sum(hit, axis=0, keepdims=True)


def halve_body(mine_ref, came_ref, keep, give):
    half = mine_ref.shape[0] // 2
    keep[...] = mine_ref[:half] + came_ref[:half]
    give[...] = mine_ref[half:] + came_ref[half:]


def double_body(mine_ref, came_ref, out):
    half = mine_ref.shape[0]
    out[:half] = mine_ref[...]
    out[half:] = came_ref[...]


def hard_grads_body(groups, *refs):
    pieces, coefs, outs = refs[:groups], refs[groups], refs[groups + 2 : 2 * groups + 2]
    token, matrix, matrix_t = refs[2 * groups + 2 :]
    rows = coefs.shape[1]
    cols = outs[0].shape[1]
    signal(token)
    ids = lax.broadcasted_iota(jnp.int32, (groups * rows, rows), 0)
    for r in range(groups):
        places = places_of(pieces[r], rows)
        total = jnp.zeros(ids.shape, F32)
        for k in range(3):
            total += jnp.where(ids == places[k], coefs[SLOT * r + k : SLOT * r + k + 1], 0.0)
        mine = slice(r * rows, (r + 1) * rows)
        matrix[:, mine] = total.astype(BF16)
        matrix_t[mine] = total.T.astype(BF16)
    step = min(cols, 256)
    for c in range(0, cols, step):
        at = slice(c, c + step)
        q_all = jnp.concatenate([piece[:rows, at] for piece in pieces], axis=0)
        p_all = jnp.concatenate([piece[rows : 2 * rows, at] for piece in pieces], axis=0)
        grad_q = dot(matrix_t[...], p_all, ((1,), (0,))).astype(BF16)
        grad_p = dot(matrix[...], q_all, ((1,), (0,))).astype(BF16)
        for r in range(groups):
            mine = slice(r * rows, (r + 1) * rows)
            outs[r][:rows, at] = grad_q[mine]
            outs[r][rows:, at] = grad_p[mine]


def pass_body(source, token, out):
    out[...] = source[...]


def choose_body(n1_ref, e3_ref, out):
    odd = lax.axis_index("blk") % 2 == 1

    @pl.when(odd)
    def _():
        out[...] = n1_ref[...]

    @pl.when(jnp.logical_not(odd))
    def _():
        out[...] = e3_ref[...]


def scores_body(q_ref, *refs):
    half = len(refs) // 2
    for block, out in zip(refs[:half], refs[half:]):
        out[...] = dot(block[...], q_ref[...], ((1,), (1,)))


def weigh_body(
    q_ref, s0_ref, s1_ref, s2_ref, s3_ref, last_ref, w_ref, hard_mine, hard_came, other_ref,
    loss_ref, coef_ref, hard_out, swap_ref, term3_ref,
):
    rows, width = q_ref.shape
    w = w_ref[...]
    s3 = INV_TEMP * (s3_ref[...] + dot(last_ref[...], q_ref[...], ((1,), (1,))))
    scores = [INV_TEMP * s0_ref[...], INV_TEMP * s1_ref[...], INV_TEMP * s2_ref[...], s3]
    hard = INV_TEMP * (hard_mine[:3] + hard_came[:3])
    largest = jnp.max(hard, axis=0, keepdims=True)
    for block in scores:
        largest = jnp.maximum(largest, jnp.max(block, axis=0, keepdims=True))
    summed = jnp.sum(jnp.exp(hard - largest), axis=0, keepdims=True)
    for block in scores:
        summed = summed + jnp.sum(jnp.exp(block - largest), axis=0, keepdims=True)
    log_total = largest + jnp.log(summed)
    for s, block in enumerate(scores):
        coef = (w * jnp.exp(block - log_total)).astype(BF16)
        coef_ref[:, s * rows : (s + 1) * rows] = coef
        if s in (1, 2):
            swap_ref[:, (s - 1) * rows : s * rows] = coef
    coef3 = coef_ref[:, 3 * rows :]
    for c in range(0, width, CHUNK):
        at = slice(c, c + CHUNK)
        term3_ref[:, at] = dot(coef3, q_ref[:, at], ((1,), (0,))).astype(BF16)
    hard_out[...] = jnp.zeros(hard_out.shape, F32)
    hard_out[:3] = (w * jnp.exp(hard - log_total)).astype(BF16).astype(F32)
    eye = lax.broadcasted_iota(jnp.int32, (rows, rows), 0) == lax.broadcasted_iota(
        jnp.int32, (rows, rows), 1
    )
    loss_ref[...] = log_total - jnp.sum(jnp.where(eye, scores[0], 0.0), axis=0, keepdims=True)


def sums_body(q_ref, other_ref, coef_ref, swap_ref, sent3, partial1, token):
    signal(token)
    rows, width = q_ref.shape
    odd = lax.axis_index("blk") % 2 == 1
    mine = jnp.where(odd, coef_ref[:, rows : 2 * rows], coef_ref[:, 3 * rows :])
    coef = jnp.concatenate([mine, swap_ref[:, rows:]], axis=1)
    for c in range(0, width, CHUNK):
        at = slice(c, c + CHUNK)
        held = jnp.concatenate([q_ref[:, at], other_ref[:, at]], axis=0)
        total = dot(coef, held, ((1,), (0,)))
        sent3[:, at] = total.astype(BF16)
        partial1[:, at] = total


def relay_body(partial1, got3_ref, out, done):
    signal(done)
    out[...] = (partial1[...] + got3_ref[...].astype(F32)).astype(BF16)


def base_body(
    q_ref, other_ref, p_ref, n1_ref, n2_ref, e3_ref, o3_ref, coef_ref, swap_ref, w_ref, own3_ref,
    token, pulled, base, coef_t,
):
    rows, width = q_ref.shape
    w = jnp.broadcast_to(w_ref[...], (rows, rows)).T[:, :1]
    odd = lax.axis_index("blk") % 2 == 1
    blocks = (p_ref, n1_ref, n2_ref, e3_ref, o3_ref)
    for s in range(5):
        k = min(s, 3) * rows
        coef_t[:, s * rows : (s + 1) * rows] = coef_ref[:, k : k + rows].astype(F32).T.astype(BF16)
    coef = [coef_ref[:, :rows], jnp.where(odd, swap_ref[:, :rows], jnp.zeros((rows, rows), BF16))]
    coef = jnp.concatenate(coef, axis=1)
    for c in range(0, width, CHUNK):
        at = slice(c, c + CHUNK)
        held = jnp.concatenate([block[:, at] for block in blocks], axis=0)
        pulled[:, at] = dot(coef_t[...], held, ((1,), (0,))) - w * p_ref[:, at].astype(F32)
        held = jnp.concatenate([q_ref[:, at], other_ref[:, at]], axis=0)
        own = dot(coef, held, ((1,), (0,))) + own3_ref[:, at].astype(F32)
        base[:, at] = own - w * q_ref[:, at].astype(F32)


def finish_body(groups, pulled, base, own1, *refs):
    backs = refs[:groups]
    q_out, p_out, q_held, p_held, sems = refs[groups:]
    rows, cols = pulled.shape[0], backs[0].shape[1]
    g = lax.axis_index("grp")
    copies = []
    for r, back in enumerate(backs):
        at = pl.ds(pl.multiple_of((g ^ r) * cols, 128), cols)
        q_held[:, at] = (INV_TEMP * (pulled[:, at] + back[:rows].astype(F32))).astype(BF16)
        copies.append(pltpu.make_async_copy(q_held.at[:, at], q_out.at[:, at], sems.at[2 * r]))
        copies[-1].start()
        total = base[:, at] + back[rows:].astype(F32) + own1[:, at].astype(F32)
        p_held[:, at] = (INV_TEMP * total).astype(BF16)
        copies.append(pltpu.make_async_copy(p_held.at[:, at], p_out.at[:, at], sems.at[2 * r + 1]))
        copies[-1].start()
    for copy in copies:
        copy.wait()


def per_device(queries, passages, hard_index, weights):
    rows, width = queries.shape
    groups = lax.axis_size("grp")
    loop = lax.axis_size("blk")
    cols = width // groups

    def shift(array, by, which=(0, 1)):
        pairs = [(i, (i + by) % loop) for i in range(loop) if i % 2 in which]
        return lax.ppermute(array, "blk", pairs)

    def swap(array):
        return lax.ppermute(array, "blk", [(i, i ^ 1) for i in range(loop)])

    def over_groups(array, r):
        return lax.ppermute(array, "grp", [(i, i ^ r) for i in range(groups)])

    def exchange(arrays):
        out = list(arrays)
        for r in reversed(range(1, groups)):
            out[r] = over_groups(arrays[r], r)
        return out

    def like(*shape, dtype=BF16):
        return jax.ShapeDtypeStruct(shape, dtype)

    block, block32 = like(rows, width), like(rows, width, dtype=F32)
    square, triple = like(rows, rows, dtype=F32), like(3, rows, dtype=F32)
    piece, back = like(2 * rows + TAIL, cols), like(2 * rows, cols)

    next1 = shift(passages, -1)

    held_q, held_p, *pieces, token = local_call(
        functools.partial(load_body, groups, loop * rows),
        [block, block] + [piece] * groups + [TOKEN],
        queries, passages, hard_index.T,
        in_specs=[HBM, HBM, VMEM],
        scratch=[pltpu.SemaphoreType.DMA((2 * groups,))],
    )
    pieces = exchange(pieces)

    next3_even = shift(held_p, -3, (1,))
    (next1,) = local_call(pass_body, [block], next1, token, flops=LONG)
    next3_odd = shift(next1, -2, (1,))
    next2 = swap(local_call(choose_body, [block], next1, next3_even, flops=LONG)[0])

    s0, s1, s3 = local_call(scores_body, [square] * 3, held_q, held_p, next1, next3_even)
    half = like(SLOT * groups // 2, rows, dtype=F32)
    keep, give = local_call(
        functools.partial(hard_scores_body, groups), [half, half], *pieces, s0, flops=LONG
    )
    for bit in range(groups.bit_length() - 2):
        came = over_groups(give, 1 << bit)
        half = like(keep.shape[0] // 2, rows, dtype=F32)
        keep, give = local_call(halve_body, [half, half], keep, came)
    came = over_groups(give, groups // 2)
    other_q = swap(held_q)
    (s2,) = local_call(scores_body, [square], held_q, next2)
    loss_rows, coef, hard_coef, to_core, term3 = local_call(
        weigh_body,
        [
            like(1, rows, dtype=F32), like(rows, 4 * rows), like(SLOT, rows, dtype=F32),
            like(rows, 2 * rows), block,
        ],
        held_q, s0, s1, s2, s3, next3_odd, weights[None, :], keep, came, other_q,
    )

    got3 = shift(term3, 2, (1,))
    from_core = swap(to_core)
    sent3, partial1, token = local_call(
        sums_body, [block, block32, TOKEN], held_q, other_q, coef, from_core
    )
    own3 = shift(sent3, 3, (0,))

    for bit in range(groups.bit_length() - 1):
        came = over_groups(hard_coef, 1 << bit)
        double = like(2 * hard_coef.shape[0], rows, dtype=F32)
        (hard_coef,) = local_call(double_body, [double], hard_coef, came)
    square_all = pltpu.VMEM((groups * rows, groups * rows), BF16)
    *backs, token = local_call(
        functools.partial(hard_grads_body, groups), [back] * groups + [TOKEN],
        *pieces, hard_coef, token, scratch=[square_all, square_all],
    )
    backs = exchange(backs)

    sent1, token = local_call(relay_body, [block, TOKEN], partial1, got3, flops=SOME)
    own1 = shift(sent1, 1, (1,))

    pulled, base = local_call(
        base_body, [block32, block32],
        held_q, other_q, held_p, next1, next2, next3_even, next3_odd, coef, from_core,
        weights[None, :], own3, token, flops=LONG, scratch=[pltpu.VMEM((rows, 5 * rows), BF16)],
    )
    grad_queries, grad_passages = local_call(
        functools.partial(finish_body, groups), [block, block], pulled, base, own1, *backs,
        out_specs=[HBM, HBM],
        scratch=[
            pltpu.VMEM((rows, width), BF16),
            pltpu.VMEM((rows, width), BF16),
            pltpu.SemaphoreType.DMA((2 * groups,)),
        ],
    )
    return loss_rows.reshape(rows), grad_queries, grad_passages


def solution(mesh):
    rows = P(("grp", "blk"))
    matrix = P(("grp", "blk"), None)
    return jax.shard_map(
        per_device,
        mesh=mesh,
        in_specs=(matrix, matrix, matrix, rows),
        out_specs=(rows, matrix, matrix),
        check_vma=False,
    )
```

```python
import functools
import math

import jax
import jax.numpy as jnp
from jax import lax
from jax.experimental import pallas as pl
from jax.experimental.pallas import tpu as pltpu
from jax.sharding import PartitionSpec as P

INV_TEMP = 50.0
BF16 = jnp.bfloat16
F32 = jnp.float32
CHUNK = 512
TAIL = 16
LONG, SOME = 5 * 10**10, 16 * 10**9
VMEM = pl.BlockSpec(memory_space=pltpu.VMEM)
HBM = pl.BlockSpec(memory_space=pltpu.HBM)
TOKEN = jax.ShapeDtypeStruct((8, 128), F32)


def dot(left, right, dims):
    return lax.dot_general(left, right, (dims, ((), ())), preferred_element_type=F32)


def size_of(arrays):
    return sum(math.prod(a.shape) * jnp.dtype(a.dtype).itemsize for a in arrays)


def local_call(body, out_shape, *args, flops=0, in_specs=None, out_specs=None, scratch=()):
    return pl.pallas_call(
        body,
        out_shape=out_shape,
        in_specs=in_specs or [VMEM] * len(args),
        out_specs=out_specs or [VMEM] * len(out_shape),
        scratch_shapes=list(scratch),
        cost_estimate=pl.CostEstimate(
            flops=flops, bytes_accessed=size_of(args) + size_of(out_shape), transcendentals=0
        ),
        compiler_params=pltpu.CompilerParams(vmem_limit_bytes=20 * 2**20),
    )(*args)


def signal(token):
    token[...] = jnp.zeros(token.shape, token.dtype)


def split_index(index, rows, group_rows):
    if group_rows & (group_rows - 1) or rows & (rows - 1):
        return index // group_rows, index % rows
    return index >> (group_rows.bit_length() - 1), index & (rows - 1)


def load_body(groups, group_rows, q_hbm, p_hbm, index_ref, q_ref, p_ref, *refs):
    pieces, token, sems = refs[:groups], refs[groups], refs[groups + 1]
    rows = q_ref.shape[0]
    cols = pieces[0].shape[1]
    g = lax.axis_index("grp")
    copies = []
    for r in range(groups):
        at = pl.ds(pl.multiple_of((g ^ r) * cols, 128), cols)
        pair = [
            pltpu.make_async_copy(source.at[:, at], target.at[:, at], sems.at[2 * r + n])
            for n, (source, target) in enumerate(((q_hbm, q_ref), (p_hbm, p_ref)))
        ]
        for copy in pair:
            copy.start()
        copies.append((at, pair))
    signal(token)
    index = jnp.concatenate([index_ref[...], jnp.zeros((TAIL - 3, rows), jnp.int32)], axis=0)
    named_group, named_row = split_index(index, rows, group_rows)
    named_group = named_group.astype(F32).astype(BF16)
    named_row = named_row.astype(F32).astype(BF16)
    for r in reversed(range(groups)):
        at, pair = copies[r]
        for copy in pair:
            copy.wait()
        pieces[r][:rows] = q_ref[:, at]
        pieces[r][rows : 2 * rows] = p_ref[:, at]
        pieces[r][2 * rows :, :rows] = named_group
        pieces[r][2 * rows :, rows : 2 * rows] = named_row


def places_of(piece_ref, rows):
    tail = piece_ref[2 * rows :, : 2 * rows].astype(F32).astype(jnp.int32)
    g = lax.axis_index("grp")
    return [(tail[k : k + 1, :rows] ^ g) * rows + tail[k : k + 1, rows:] for k in range(3)]


def hard_scores_body(groups, *refs):
    pieces, outs = refs[:groups], refs[groups + 1 :]
    rows = outs[0].shape[1]
    ids = lax.broadcasted_iota(jnp.int32, (groups * rows, rows), 0)
    p_all = jnp.concatenate([piece[rows : 2 * rows] for piece in pieces], axis=0)
    for r in range(groups):
        places = places_of(pieces[r], rows)
        dots = dot(p_all, pieces[r][:rows], ((1,), (1,)))
        for k in range(3):
            hit = jnp.where(ids == places[k], dots, 0.0)
            outs[r][k : k + 1] = jnp.sum(hit, axis=0, keepdims=True)


def hard_grads_body(groups, *refs):
    pieces, coefs, outs = refs[:groups], refs[groups : 2 * groups], refs[2 * groups + 1 : 3 * groups + 1]
    token, matrix, matrix_t = refs[3 * groups + 1 :]
    rows = coefs[0].shape[1]
    cols = outs[0].shape[1]
    signal(token)
    ids = lax.broadcasted_iota(jnp.int32, (groups * rows, rows), 0)
    for r in range(groups):
        places = places_of(pieces[r], rows)
        total = jnp.zeros(ids.shape, F32)
        for k in range(3):
            total += jnp.where(ids == places[k], coefs[r][k : k + 1], 0.0)
        mine = slice(r * rows, (r + 1) * rows)
        matrix[:, mine] = total.astype(BF16)
        matrix_t[mine] = total.T.astype(BF16)
    step = min(cols, 256)
    for c in range(0, cols, step):
        at = slice(c, c + step)
        q_all = jnp.concatenate([piece[:rows, at] for piece in pieces], axis=0)
        p_all = jnp.concatenate([piece[rows : 2 * rows, at] for piece in pieces], axis=0)
        grad_q = dot(matrix_t[...], p_all, ((1,), (0,))).astype(BF16)
        grad_p = dot(matrix[...], q_all, ((1,), (0,))).astype(BF16)
        for r in range(groups):
            mine = slice(r * rows, (r + 1) * rows)
            outs[r][:rows, at] = grad_q[mine]
            outs[r][rows:, at] = grad_p[mine]


def pass_body(source, token, out):
    out[...] = source[...]


def choose_body(n1_ref, e3_ref, q_ref, out):
    width = q_ref.shape[1]
    odd = lax.axis_index("blk") % 2 == 1
    out[:, width:] = q_ref[...]

    @pl.when(odd)
    def _():
        out[:, :width] = n1_ref[...]

    @pl.when(jnp.logical_not(odd))
    def _():
        out[:, :width] = e3_ref[...]


def scores_body(q_ref, *refs):
    half = len(refs) // 2
    for block, out in zip(refs[:half], refs[half:]):
        out[...] = dot(block[...], q_ref[...], ((1,), (1,)))


def last_score_body(q_ref, pair_ref, out):
    out[...] = dot(pair_ref[:, : q_ref.shape[1]], q_ref[...], ((1,), (1,)))


def weigh_body(
    groups, q_ref, s0_ref, s1_ref, s2_ref, s3_ref, last_ref, w_ref, *refs
):
    parts, (loss_ref, coef_ref, hard_out, swap_ref, term3_ref) = refs[:groups], refs[groups:]
    rows, width = q_ref.shape
    w = w_ref[...]
    s3 = INV_TEMP * (s3_ref[...] + dot(last_ref[...], q_ref[...], ((1,), (1,))))
    scores = [INV_TEMP * s0_ref[...], INV_TEMP * s1_ref[...], INV_TEMP * s2_ref[...], s3]
    hard = parts[0][...]
    for other in parts[1:]:
        hard = hard + other[...]
    hard = INV_TEMP * hard
    largest = jnp.max(hard, axis=0, keepdims=True)
    for block in scores:
        largest = jnp.maximum(largest, jnp.max(block, axis=0, keepdims=True))
    summed = jnp.sum(jnp.exp(hard - largest), axis=0, keepdims=True)
    for block in scores:
        summed = summed + jnp.sum(jnp.exp(block - largest), axis=0, keepdims=True)
    log_total = largest + jnp.log(summed)
    for s, block in enumerate(scores):
        coef = (w * jnp.exp(block - log_total)).astype(BF16)
        coef_ref[:, s * rows : (s + 1) * rows] = coef
        if s in (1, 2):
            swap_ref[:, (s - 1) * rows : s * rows] = coef
    coef3 = coef_ref[:, 3 * rows :]
    for c in range(0, width, CHUNK):
        at = slice(c, c + CHUNK)
        term3_ref[:, at] = dot(coef3, q_ref[:, at], ((1,), (0,))).astype(BF16)
    hard_out[...] = (w * jnp.exp(hard - log_total)).astype(BF16).astype(F32)
    eye = lax.broadcasted_iota(jnp.int32, (rows, rows), 0) == lax.broadcasted_iota(
        jnp.int32, (rows, rows), 1
    )
    loss_ref[...] = log_total - jnp.sum(jnp.where(eye, scores[0], 0.0), axis=0, keepdims=True)


def sums_body(q_ref, pair_ref, coef_ref, swap_ref, sent3, partial1, token):
    signal(token)
    rows, width = q_ref.shape
    odd = lax.axis_index("blk") % 2 == 1
    mine = jnp.where(odd, coef_ref[:, rows : 2 * rows], coef_ref[:, 3 * rows :])
    coef = jnp.concatenate([mine, swap_ref[:, rows:]], axis=1)
    for c in range(0, width, CHUNK):
        at = slice(c, c + CHUNK)
        held = jnp.concatenate([q_ref[:, at], pair_ref[:, width + c : width + c + CHUNK]], axis=0)
        total = dot(coef, held, ((1,), (0,)))
        sent3[:, at] = total.astype(BF16)
        partial1[:, at] = total


def relay_body(partial1, got3_ref, out, done):
    signal(done)
    out[...] = (partial1[...] + got3_ref[...].astype(F32)).astype(BF16)


def base_body(
    q_ref, pair_ref, p_ref, n1_ref, e3_ref, o3_ref, coef_ref, swap_ref, w_ref, own3_ref,
    token, pulled, base, coef_t,
):
    rows, width = q_ref.shape
    w = jnp.broadcast_to(w_ref[...], (rows, rows)).T[:, :1]
    odd = lax.axis_index("blk") % 2 == 1
    blocks = (p_ref, n1_ref, pair_ref, e3_ref, o3_ref)
    for s in range(5):
        k = min(s, 3) * rows
        coef_t[:, s * rows : (s + 1) * rows] = coef_ref[:, k : k + rows].astype(F32).T.astype(BF16)
    coef = [coef_ref[:, :rows], jnp.where(odd, swap_ref[:, :rows], jnp.zeros((rows, rows), BF16))]
    coef = jnp.concatenate(coef, axis=1)
    for c in range(0, width, CHUNK):
        at = slice(c, c + CHUNK)
        held = jnp.concatenate([block[:, at] for block in blocks], axis=0)
        pulled[:, at] = dot(coef_t[...], held, ((1,), (0,))) - w * p_ref[:, at].astype(F32)
        held = jnp.concatenate([q_ref[:, at], pair_ref[:, width + c : width + c + CHUNK]], axis=0)
        own = dot(coef, held, ((1,), (0,))) + own3_ref[:, at].astype(F32)
        base[:, at] = own - w * q_ref[:, at].astype(F32)


def finish_body(groups, pulled, base, own1, *refs):
    backs = refs[:groups]
    q_out, p_out, q_held, p_held, sems = refs[groups:]
    rows, cols = pulled.shape[0], backs[0].shape[1]
    g = lax.axis_index("grp")
    copies = []
    for r, back in enumerate(backs):
        at = pl.ds(pl.multiple_of((g ^ r) * cols, 128), cols)
        q_held[:, at] = (INV_TEMP * (pulled[:, at] + back[:rows].astype(F32))).astype(BF16)
        copies.append(pltpu.make_async_copy(q_held.at[:, at], q_out.at[:, at], sems.at[2 * r]))
        copies[-1].start()
        total = base[:, at] + back[rows:].astype(F32) + own1[:, at].astype(F32)
        p_held[:, at] = (INV_TEMP * total).astype(BF16)
        copies.append(pltpu.make_async_copy(p_held.at[:, at], p_out.at[:, at], sems.at[2 * r + 1]))
        copies[-1].start()
    for copy in copies:
        copy.wait()


def per_device(queries, passages, hard_index, weights):
    rows, width = queries.shape
    groups = lax.axis_size("grp")
    loop = lax.axis_size("blk")
    cols = width // groups

    def shift(array, by, which=(0, 1)):
        pairs = [(i, (i + by) % loop) for i in range(loop) if i % 2 in which]
        return lax.ppermute(array, "blk", pairs)

    def swap(array):
        return lax.ppermute(array, "blk", [(i, i ^ 1) for i in range(loop)])

    def over_groups(array, r):
        return lax.ppermute(array, "grp", [(i, i ^ r) for i in range(groups)])

    def exchange(arrays):
        out = list(arrays)
        for r in reversed(range(1, groups)):
            out[r] = over_groups(arrays[r], r)
        return out

    def like(*shape, dtype=BF16):
        return jax.ShapeDtypeStruct(shape, dtype)

    block, block32 = like(rows, width), like(rows, width, dtype=F32)
    square, triple = like(rows, rows, dtype=F32), like(3, rows, dtype=F32)
    piece, back = like(2 * rows + TAIL, cols), like(2 * rows, cols)

    next1 = shift(passages, -1)

    held_q, held_p, *pieces, token = local_call(
        functools.partial(load_body, groups, loop * rows),
        [block, block] + [piece] * groups + [TOKEN],
        queries, passages, hard_index.T,
        in_specs=[HBM, HBM, VMEM],
        scratch=[pltpu.SemaphoreType.DMA((2 * groups,))],
    )
    pieces = exchange(pieces)

    next3_even = shift(held_p, -3, (1,))
    (next1,) = local_call(pass_body, [block], next1, token, flops=LONG)
    next3_odd = shift(next1, -2, (1,))
    pair = swap(
        local_call(choose_body, [like(rows, 2 * width)], next1, next3_even, held_q, flops=LONG)[0]
    )

    s0, s1, s3 = local_call(scores_body, [square] * 3, held_q, held_p, next1, next3_even)
    parts = local_call(
        functools.partial(hard_scores_body, groups), [triple] * groups, *pieces, s0, flops=LONG
    )
    (s2,) = local_call(last_score_body, [square], held_q, pair)
    parts = exchange(parts)
    loss_rows, coef, hard_coef, to_core, term3 = local_call(
        functools.partial(weigh_body, groups),
        [like(1, rows, dtype=F32), like(rows, 4 * rows), triple, like(rows, 2 * rows), block],
        held_q, s0, s1, s2, s3, next3_odd, weights[None, :], *parts,
    )

    got3 = shift(term3, 2, (1,))
    from_core = swap(to_core)
    sent3, partial1, token = local_call(
        sums_body, [block, block32, TOKEN], held_q, pair, coef, from_core
    )
    own3 = shift(sent3, 3, (0,))

    hard_coefs = exchange([hard_coef] * groups)
    square_all = pltpu.VMEM((groups * rows, groups * rows), BF16)
    *backs, token = local_call(
        functools.partial(hard_grads_body, groups), [back] * groups + [TOKEN],
        *pieces, *hard_coefs, token, scratch=[square_all, square_all],
    )
    backs = exchange(backs)

    sent1, token = local_call(relay_body, [block, TOKEN], partial1, got3, flops=SOME)
    own1 = shift(sent1, 1, (1,))

    pulled, base = local_call(
        base_body, [block32, block32],
        held_q, pair, held_p, next1, next3_even, next3_odd, coef, from_core,
        weights[None, :], own3, token, flops=LONG, scratch=[pltpu.VMEM((rows, 5 * rows), BF16)],
    )
    grad_queries, grad_passages = local_call(
        functools.partial(finish_body, groups), [block, block], pulled, base, own1, *backs,
        out_specs=[HBM, HBM],
        scratch=[
            pltpu.VMEM((rows, width), BF16),
            pltpu.VMEM((rows, width), BF16),
            pltpu.SemaphoreType.DMA((2 * groups,)),
        ],
    )
    return loss_rows.reshape(rows), grad_queries, grad_passages


def solution(mesh):
    rows = P(("grp", "blk"))
    matrix = P(("grp", "blk"), None)
    return jax.shard_map(
        per_device,
        mesh=mesh,
        in_specs=(matrix, matrix, matrix, rows),
        out_specs=(rows, matrix, matrix),
        check_vma=False,
    )
```

```python
import functools
import math

import jax
import jax.numpy as jnp
from jax import lax
from jax.experimental import pallas as pl
from jax.experimental.pallas import tpu as pltpu
from jax.sharding import PartitionSpec as P

INV_TEMP = 50.0
BF16 = jnp.bfloat16
F32 = jnp.float32
CHUNK = 512
TAIL = 16
LONG, SOME = 5 * 10**10, 16 * 10**9
VMEM = pl.BlockSpec(memory_space=pltpu.VMEM)
HBM = pl.BlockSpec(memory_space=pltpu.HBM)
TOKEN = jax.ShapeDtypeStruct((8, 128), F32)


def dot(left, right, dims):
    return lax.dot_general(left, right, (dims, ((), ())), preferred_element_type=F32)


def size_of(arrays):
    return sum(math.prod(a.shape) * jnp.dtype(a.dtype).itemsize for a in arrays)


def local_call(body, out_shape, *args, flops=0, in_specs=None, out_specs=None, scratch=(), limit=20):
    return pl.pallas_call(
        body,
        out_shape=out_shape,
        in_specs=in_specs or [VMEM] * len(args),
        out_specs=out_specs or [VMEM] * len(out_shape),
        scratch_shapes=list(scratch),
        cost_estimate=pl.CostEstimate(
            flops=flops, bytes_accessed=size_of(args) + size_of(out_shape), transcendentals=0
        ),
        compiler_params=pltpu.CompilerParams(vmem_limit_bytes=limit * 2**20),
    )(*args)


def signal(token):
    token[...] = jnp.zeros(token.shape, token.dtype)


def split_index(index, rows, group_rows):
    if group_rows & (group_rows - 1) or rows & (rows - 1):
        return index // group_rows, index % rows
    return index >> (group_rows.bit_length() - 1), index & (rows - 1)


def load_body(groups, group_rows, q_hbm, p_hbm, index_hbm, *refs):
    pieces, (token, index_ref, sems) = refs[:groups], refs[groups:]
    rows = q_hbm.shape[0]
    cols = pieces[0].shape[1]
    g = lax.axis_index("grp")
    index_copy = pltpu.make_async_copy(index_hbm, index_ref, sems.at[2 * groups])
    index_copy.start()
    copies = []
    for r, piece in enumerate(pieces):
        at = pl.ds(pl.multiple_of((g ^ r) * cols, 128), cols)
        for n, source in enumerate((q_hbm, p_hbm)):
            target = piece.at[pl.ds(n * rows, rows)]
            copies.append(pltpu.make_async_copy(source.at[:, at], target, sems.at[2 * r + n]))
            copies[-1].start()
    signal(token)
    index_copy.wait()
    index = jnp.concatenate([index_ref[...], jnp.zeros((TAIL - 3, rows), jnp.int32)], axis=0)
    named_group, named_row = split_index(index, rows, group_rows)
    named_group = named_group.astype(F32).astype(BF16)
    named_row = named_row.astype(F32).astype(BF16)
    for piece in pieces:
        piece[2 * rows :, :rows] = named_group
        piece[2 * rows :, rows : 2 * rows] = named_row
        if cols > 2 * rows:
            piece[2 * rows :, 2 * rows :] = jnp.zeros((TAIL, cols - 2 * rows), BF16)
    for copy in copies:
        copy.wait()


def places_of(piece_ref, rows):
    tail = piece_ref[2 * rows :, : 2 * rows].astype(F32).astype(jnp.int32)
    g = lax.axis_index("grp")
    return [(tail[k : k + 1, :rows] ^ g) * rows + tail[k : k + 1, rows:] for k in range(3)]


def hard_scores_body(groups, *refs):
    pieces, outs = refs[:groups], refs[groups + 1 :]
    rows = outs[0].shape[1]
    ids = lax.broadcasted_iota(jnp.int32, (groups * rows, rows), 0)
    p_all = jnp.concatenate([piece[rows : 2 * rows] for piece in pieces], axis=0)
    for r in range(groups):
        places = places_of(pieces[r], rows)
        dots = dot(p_all, pieces[r][:rows], ((1,), (1,)))
        for k in range(3):
            hit = jnp.where(ids == places[k], dots, 0.0)
            outs[r][k : k + 1] = jnp.sum(hit, axis=0, keepdims=True)


def hard_grads_body(groups, *refs):
    pieces, coefs, outs = refs[:groups], refs[groups : 2 * groups], refs[2 * groups + 1 : 3 * groups + 1]
    token, matrix, matrix_t = refs[3 * groups + 1 :]
    rows = coefs[0].shape[1]
    cols = outs[0].shape[1]
    signal(token)
    ids = lax.broadcasted_iota(jnp.int32, (groups * rows, rows), 0)
    for r in range(groups):
        places = places_of(pieces[r], rows)
        total = jnp.zeros(ids.shape, F32)
        for k in range(3):
            total += jnp.where(ids == places[k], coefs[r][k : k + 1], 0.0)
        mine = slice(r * rows, (r + 1) * rows)
        matrix[:, mine] = total.astype(BF16)
        matrix_t[mine] = total.T.astype(BF16)
    step = min(cols, 256)
    for c in range(0, cols, step):
        at = slice(c, c + step)
        q_all = jnp.concatenate([piece[:rows, at] for piece in pieces], axis=0)
        p_all = jnp.concatenate([piece[rows : 2 * rows, at] for piece in pieces], axis=0)
        grad_q = dot(matrix_t[...], p_all, ((1,), (0,))).astype(BF16)
        grad_p = dot(matrix[...], q_all, ((1,), (0,))).astype(BF16)
        for r in range(groups):
            mine = slice(r * rows, (r + 1) * rows)
            outs[r][:rows, at] = grad_q[mine]
            outs[r][rows:, at] = grad_p[mine]


def pass_body(source, token, out):
    out[...] = source[...]


def choose_body(n1_ref, e3_ref, q_ref, out):
    width = q_ref.shape[1]
    odd = lax.axis_index("blk") % 2 == 1
    out[:, width:] = q_ref[...]

    @pl.when(odd)
    def _():
        out[:, :width] = n1_ref[...]

    @pl.when(jnp.logical_not(odd))
    def _():
        out[:, :width] = e3_ref[...]


def scores_body(q_ref, *refs):
    half = len(refs) // 2
    for block, out in zip(refs[:half], refs[half:]):
        out[...] = dot(block[...], q_ref[...], ((1,), (1,)))


def last_score_body(q_ref, pair_ref, out):
    out[...] = dot(pair_ref[:, : q_ref.shape[1]], q_ref[...], ((1,), (1,)))


def weigh_body(
    groups, q_ref, s0_ref, s1_ref, s2_ref, s3_ref, last_ref, w_ref, *refs
):
    parts, (loss_ref, coef_ref, hard_out, swap_ref, term3_ref) = refs[:groups], refs[groups:]
    rows, width = q_ref.shape
    w = w_ref[...]
    s3 = INV_TEMP * (s3_ref[...] + dot(last_ref[...], q_ref[...], ((1,), (1,))))
    scores = [INV_TEMP * s0_ref[...], INV_TEMP * s1_ref[...], INV_TEMP * s2_ref[...], s3]
    hard = parts[0][...]
    for other in parts[1:]:
        hard = hard + other[...]
    hard = INV_TEMP * hard
    largest = jnp.max(hard, axis=0, keepdims=True)
    for block in scores:
        largest = jnp.maximum(largest, jnp.max(block, axis=0, keepdims=True))
    summed = jnp.sum(jnp.exp(hard - largest), axis=0, keepdims=True)
    for block in scores:
        summed = summed + jnp.sum(jnp.exp(block - largest), axis=0, keepdims=True)
    log_total = largest + jnp.log(summed)
    for s, block in enumerate(scores):
        coef = (w * jnp.exp(block - log_total)).astype(BF16)
        coef_ref[:, s * rows : (s + 1) * rows] = coef
        if s in (1, 2):
            swap_ref[:, (s - 1) * rows : s * rows] = coef
    coef3 = coef_ref[:, 3 * rows :]
    for c in range(0, width, CHUNK):
        at = slice(c, c + CHUNK)
        term3_ref[:, at] = dot(coef3, q_ref[:, at], ((1,), (0,))).astype(BF16)
    hard_out[...] = (w * jnp.exp(hard - log_total)).astype(BF16).astype(F32)
    eye = lax.broadcasted_iota(jnp.int32, (rows, rows), 0) == lax.broadcasted_iota(
        jnp.int32, (rows, rows), 1
    )
    loss_ref[...] = log_total - jnp.sum(jnp.where(eye, scores[0], 0.0), axis=0, keepdims=True)


def sums_body(q_ref, pair_ref, coef_ref, swap_ref, sent3, partial1, token):
    signal(token)
    rows, width = q_ref.shape
    odd = lax.axis_index("blk") % 2 == 1
    mine = jnp.where(odd, coef_ref[:, rows : 2 * rows], coef_ref[:, 3 * rows :])
    coef = jnp.concatenate([mine, swap_ref[:, rows:]], axis=1)
    for c in range(0, width, CHUNK):
        at = slice(c, c + CHUNK)
        held = jnp.concatenate([q_ref[:, at], pair_ref[:, width + c : width + c + CHUNK]], axis=0)
        total = dot(coef, held, ((1,), (0,)))
        sent3[:, at] = total.astype(BF16)
        partial1[:, at] = total


def relay_body(partial1, got3_ref, out, done):
    signal(done)
    out[...] = (partial1[...] + got3_ref[...].astype(F32)).astype(BF16)


def base_body(
    q_ref, pair_ref, p_ref, n1_ref, e3_ref, o3_ref, coef_ref, swap_ref, w_ref, own3_ref,
    token, pulled, base, coef_t,
):
    rows, width = q_ref.shape
    w = jnp.broadcast_to(w_ref[...], (rows, rows)).T[:, :1]
    odd = lax.axis_index("blk") % 2 == 1
    blocks = (p_ref, n1_ref, pair_ref, e3_ref, o3_ref)
    for s in range(5):
        k = min(s, 3) * rows
        coef_t[:, s * rows : (s + 1) * rows] = coef_ref[:, k : k + rows].astype(F32).T.astype(BF16)
    coef = [coef_ref[:, :rows], jnp.where(odd, swap_ref[:, :rows], jnp.zeros((rows, rows), BF16))]
    coef = jnp.concatenate(coef, axis=1)
    for c in range(0, width, CHUNK):
        at = slice(c, c + CHUNK)
        held = jnp.concatenate([block[:, at] for block in blocks], axis=0)
        pulled[:, at] = dot(coef_t[...], held, ((1,), (0,))) - w * p_ref[:, at].astype(F32)
        held = jnp.concatenate([q_ref[:, at], pair_ref[:, width + c : width + c + CHUNK]], axis=0)
        own = dot(coef, held, ((1,), (0,))) + own3_ref[:, at].astype(F32)
        base[:, at] = own - w * q_ref[:, at].astype(F32)


def finish_body(groups, pulled, base, own1, *refs):
    backs = refs[:groups]
    q_out, p_out, q_held, p_held, sems = refs[groups:]
    rows, cols = pulled.shape[0], backs[0].shape[1]
    g = lax.axis_index("grp")
    copies = []
    for r, back in enumerate(backs):
        at = pl.ds(pl.multiple_of((g ^ r) * cols, 128), cols)
        q_held[:, at] = (INV_TEMP * (pulled[:, at] + back[:rows].astype(F32))).astype(BF16)
        copies.append(pltpu.make_async_copy(q_held.at[:, at], q_out.at[:, at], sems.at[2 * r]))
        copies[-1].start()
        total = base[:, at] + back[rows:].astype(F32) + own1[:, at].astype(F32)
        p_held[:, at] = (INV_TEMP * total).astype(BF16)
        copies.append(pltpu.make_async_copy(p_held.at[:, at], p_out.at[:, at], sems.at[2 * r + 1]))
        copies[-1].start()
    for copy in copies:
        copy.wait()


def per_device(queries, passages, hard_index, weights):
    rows, width = queries.shape
    groups = lax.axis_size("grp")
    loop = lax.axis_size("blk")
    cols = width // groups

    def shift(array, by, which=(0, 1)):
        pairs = [(i, (i + by) % loop) for i in range(loop) if i % 2 in which]
        return lax.ppermute(array, "blk", pairs)

    def swap(array):
        return lax.ppermute(array, "blk", [(i, i ^ 1) for i in range(loop)])

    def over_groups(array, r):
        return lax.ppermute(array, "grp", [(i, i ^ r) for i in range(groups)])

    def exchange(arrays):
        out = list(arrays)
        for r in reversed(range(1, groups)):
            out[r] = over_groups(arrays[r], r)
        return out

    def like(*shape, dtype=BF16):
        return jax.ShapeDtypeStruct(shape, dtype)

    block, block32 = like(rows, width), like(rows, width, dtype=F32)
    square, triple = like(rows, rows, dtype=F32), like(3, rows, dtype=F32)
    piece, back = like(2 * rows + TAIL, cols), like(2 * rows, cols)

    next1 = shift(passages, -1)

    *pieces, token = local_call(
        functools.partial(load_body, groups, loop * rows), [piece] * groups + [TOKEN],
        queries, passages, hard_index.T, in_specs=[HBM, HBM, HBM],
        scratch=[pltpu.VMEM((3, rows), jnp.int32), pltpu.SemaphoreType.DMA((2 * groups + 1,))],
        limit=51,
    )
    pieces = exchange(pieces)

    next3_even = shift(passages, -3, (1,))
    (next1,) = local_call(pass_body, [block], next1, token, flops=LONG)
    next3_odd = shift(next1, -2, (1,))
    pair = swap(
        local_call(choose_body, [like(rows, 2 * width)], next1, next3_even, queries, flops=LONG)[0]
    )

    s0, s1, s3 = local_call(scores_body, [square] * 3, queries, passages, next1, next3_even)
    parts = local_call(
        functools.partial(hard_scores_body, groups), [triple] * groups, *pieces, s0, flops=LONG
    )
    (s2,) = local_call(last_score_body, [square], queries, pair)
    parts = exchange(parts)
    loss_rows, coef, hard_coef, to_core, term3 = local_call(
        functools.partial(weigh_body, groups),
        [like(1, rows, dtype=F32), like(rows, 4 * rows), triple, like(rows, 2 * rows), block],
        queries, s0, s1, s2, s3, next3_odd, weights[None, :], *parts,
    )

    got3 = shift(term3, 2, (1,))
    from_core = swap(to_core)
    sent3, partial1, token = local_call(
        sums_body, [block, block32, TOKEN], queries, pair, coef, from_core
    )
    own3 = shift(sent3, 3, (0,))

    hard_coefs = exchange([hard_coef] * groups)
    square_all = pltpu.VMEM((groups * rows, groups * rows), BF16)
    *backs, token = local_call(
        functools.partial(hard_grads_body, groups), [back] * groups + [TOKEN],
        *pieces, *hard_coefs, token, scratch=[square_all, square_all],
    )
    backs = exchange(backs)

    sent1, token = local_call(relay_body, [block, TOKEN], partial1, got3, flops=SOME)
    own1 = shift(sent1, 1, (1,))

    pulled, base = local_call(
        base_body, [block32, block32],
        queries, pair, passages, next1, next3_even, next3_odd, coef, from_core,
        weights[None, :], own3, token, flops=LONG, scratch=[pltpu.VMEM((rows, 5 * rows), BF16)],
    )
    grad_queries, grad_passages = local_call(
        functools.partial(finish_body, groups), [block, block], pulled, base, own1, *backs,
        out_specs=[HBM, HBM],
        scratch=[
            pltpu.VMEM((rows, width), BF16),
            pltpu.VMEM((rows, width), BF16),
            pltpu.SemaphoreType.DMA((2 * groups,)),
        ],
    )
    return loss_rows.reshape(rows), grad_queries, grad_passages


def solution(mesh):
    rows = P(("grp", "blk"))
    matrix = P(("grp", "blk"), None)
    return jax.shard_map(
        per_device,
        mesh=mesh,
        in_specs=(matrix, matrix, matrix, rows),
        out_specs=(rows, matrix, matrix),
        check_vma=False,
    )
```

```python
import functools
import math

import jax
import jax.numpy as jnp
from jax import lax
from jax.experimental import pallas as pl
from jax.experimental.pallas import tpu as pltpu
from jax.sharding import PartitionSpec as P

INV_TEMP = 50.0
BF16 = jnp.bfloat16
F32 = jnp.float32
CHUNK = 512
TAIL = 16
LONG, SOME = 5 * 10**10, 16 * 10**9
VMEM = pl.BlockSpec(memory_space=pltpu.VMEM)
HBM = pl.BlockSpec(memory_space=pltpu.HBM)
TOKEN = jax.ShapeDtypeStruct((8, 128), F32)


def dot(left, right, dims):
    return lax.dot_general(left, right, (dims, ((), ())), preferred_element_type=F32)


def size_of(arrays):
    return sum(math.prod(a.shape) * jnp.dtype(a.dtype).itemsize for a in arrays)


def local_call(body, out_shape, *args, flops=0, in_specs=None, out_specs=None, scratch=()):
    return pl.pallas_call(
        body,
        out_shape=out_shape,
        in_specs=in_specs or [VMEM] * len(args),
        out_specs=out_specs or [VMEM] * len(out_shape),
        scratch_shapes=list(scratch),
        cost_estimate=pl.CostEstimate(
            flops=flops, bytes_accessed=size_of(args) + size_of(out_shape), transcendentals=0
        ),
        compiler_params=pltpu.CompilerParams(vmem_limit_bytes=20 * 2**20),
    )(*args)


def signal(token):
    token[...] = jnp.zeros(token.shape, token.dtype)


def split_index(index, rows, group_rows):
    if group_rows & (group_rows - 1) or rows & (rows - 1):
        return index // group_rows, index % rows
    return index >> (group_rows.bit_length() - 1), index & (rows - 1)


def load_body(groups, group_rows, q_hbm, p_hbm, index_ref, q_ref, p_ref, *refs):
    pieces, token, sems = refs[:groups], refs[groups], refs[groups + 1]
    rows = q_ref.shape[0]
    cols = pieces[0].shape[1]
    g = lax.axis_index("grp")
    copies = []
    for r in range(groups):
        at = pl.ds(pl.multiple_of((g ^ r) * cols, 128), cols)
        pair = [
            pltpu.make_async_copy(source.at[:, at], target.at[:, at], sems.at[2 * r + n])
            for n, (source, target) in enumerate(((q_hbm, q_ref), (p_hbm, p_ref)))
        ]
        for copy in pair:
            copy.start()
        copies.append((at, pair))
    signal(token)
    index = jnp.concatenate([index_ref[...], jnp.zeros((TAIL - 3, rows), jnp.int32)], axis=0)
    named_group, named_row = split_index(index, rows, group_rows)
    named_group = named_group.astype(F32).astype(BF16)
    named_row = named_row.astype(F32).astype(BF16)
    for r in reversed(range(groups)):
        at, pair = copies[r]
        for copy in pair:
            copy.wait()
        pieces[r][:rows] = q_ref[:, at]
        pieces[r][rows : 2 * rows] = p_ref[:, at]
        pieces[r][2 * rows :, :rows] = named_group
        pieces[r][2 * rows :, rows : 2 * rows] = named_row


def places_of(piece_ref, rows):
    tail = piece_ref[2 * rows :, : 2 * rows].astype(F32).astype(jnp.int32)
    g = lax.axis_index("grp")
    return [(tail[k : k + 1, :rows] ^ g) * rows + tail[k : k + 1, rows:] for k in range(3)]


def hard_scores_body(groups, *refs):
    pieces, outs = refs[:groups], refs[groups + 1 :]
    rows = outs[0].shape[1]
    ids = lax.broadcasted_iota(jnp.int32, (groups * rows, rows), 0)
    p_all = jnp.concatenate([piece[rows : 2 * rows] for piece in pieces], axis=0)
    for r in range(groups):
        places = places_of(pieces[r], rows)
        dots = dot(p_all, pieces[r][:rows], ((1,), (1,)))
        for k in range(3):
            hit = jnp.where(ids == places[k], dots, 0.0)
            outs[r][k : k + 1] = jnp.sum(hit, axis=0, keepdims=True)


def hard_grads_body(groups, *refs):
    pieces, coefs, outs = refs[:groups], refs[groups : 2 * groups], refs[2 * groups + 1 : 3 * groups + 1]
    token, matrix, matrix_t = refs[3 * groups + 1 :]
    rows = coefs[0].shape[1]
    cols = outs[0].shape[1]
    signal(token)
    ids = lax.broadcasted_iota(jnp.int32, (groups * rows, rows), 0)
    for r in range(groups):
        places = places_of(pieces[r], rows)
        total = jnp.zeros(ids.shape, F32)
        for k in range(3):
            total += jnp.where(ids == places[k], coefs[r][k : k + 1], 0.0)
        mine = slice(r * rows, (r + 1) * rows)
        matrix[:, mine] = total.astype(BF16)
        matrix_t[mine] = total.T.astype(BF16)
    step = min(cols, 256)
    for c in range(0, cols, step):
        at = slice(c, c + step)
        q_all = jnp.concatenate([piece[:rows, at] for piece in pieces], axis=0)
        p_all = jnp.concatenate([piece[rows : 2 * rows, at] for piece in pieces], axis=0)
        grad_q = dot(matrix_t[...], p_all, ((1,), (0,))).astype(BF16)
        grad_p = dot(matrix[...], q_all, ((1,), (0,))).astype(BF16)
        for r in range(groups):
            mine = slice(r * rows, (r + 1) * rows)
            outs[r][:rows, at] = grad_q[mine]
            outs[r][rows:, at] = grad_p[mine]


def pass_body(source, token, out):
    out[...] = source[...]


def choose_body(n1_ref, e3_ref, q_ref, out):
    width = q_ref.shape[1]
    odd = lax.axis_index("blk") % 2 == 1
    out[:, width:] = q_ref[...]

    @pl.when(odd)
    def _():
        out[:, :width] = n1_ref[...]

    @pl.when(jnp.logical_not(odd))
    def _():
        out[:, :width] = e3_ref[...]


def scores_body(q_ref, *refs):
    half = len(refs) // 2
    for block, out in zip(refs[:half], refs[half:]):
        out[...] = dot(block[...], q_ref[...], ((1,), (1,)))


def last_score_body(q_ref, pair_ref, out):
    out[...] = dot(pair_ref[:, : q_ref.shape[1]], q_ref[...], ((1,), (1,)))


def weigh_body(
    groups, q_ref, s0_ref, s1_ref, s2_ref, s3_ref, last_ref, w_ref, *refs
):
    parts, (loss_ref, coef_ref, hard_out, swap_ref, term3_ref) = refs[:groups], refs[groups:]
    rows, width = q_ref.shape
    w = w_ref[...]
    s3 = INV_TEMP * (s3_ref[...] + dot(last_ref[...], q_ref[...], ((1,), (1,))))
    scores = [INV_TEMP * s0_ref[...], INV_TEMP * s1_ref[...], INV_TEMP * s2_ref[...], s3]
    hard = parts[0][...]
    for other in parts[1:]:
        hard = hard + other[...]
    hard = INV_TEMP * hard
    largest = jnp.max(hard, axis=0, keepdims=True)
    for block in scores:
        largest = jnp.maximum(largest, jnp.max(block, axis=0, keepdims=True))
    summed = jnp.sum(jnp.exp(hard - largest), axis=0, keepdims=True)
    for block in scores:
        summed = summed + jnp.sum(jnp.exp(block - largest), axis=0, keepdims=True)
    log_total = largest + jnp.log(summed)
    for s, block in enumerate(scores):
        coef = (w * jnp.exp(block - log_total)).astype(BF16)
        coef_ref[:, s * rows : (s + 1) * rows] = coef
        if s in (1, 2):
            swap_ref[:, (s - 1) * rows : s * rows] = coef
    coef3 = coef_ref[:, 3 * rows :]
    for c in range(0, width, CHUNK):
        at = slice(c, c + CHUNK)
        term3_ref[:, at] = dot(coef3, q_ref[:, at], ((1,), (0,))).astype(BF16)
    hard_out[...] = (w * jnp.exp(hard - log_total)).astype(BF16).astype(F32)
    eye = lax.broadcasted_iota(jnp.int32, (rows, rows), 0) == lax.broadcasted_iota(
        jnp.int32, (rows, rows), 1
    )
    loss_ref[...] = log_total - jnp.sum(jnp.where(eye, scores[0], 0.0), axis=0, keepdims=True)


def sums_body(q_ref, pair_ref, coef_ref, swap_ref, term3_ref, sent3, partial1, token):
    signal(token)
    rows, width = q_ref.shape
    odd = lax.axis_index("blk") % 2 == 1
    mine = jnp.where(odd, coef_ref[:, rows : 2 * rows], coef_ref[:, 3 * rows :])
    coef = jnp.concatenate([mine, swap_ref[:, rows:]], axis=1)
    for c in range(0, width, CHUNK):
        at = slice(c, c + CHUNK)
        held = jnp.concatenate([q_ref[:, at], pair_ref[:, width + c : width + c + CHUNK]], axis=0)
        total = dot(coef, held, ((1,), (0,)))
        sent3[:, at] = jnp.where(odd, term3_ref[:, at], total.astype(BF16))
        partial1[:, at] = total


def relay_body(partial1, got3_ref, out, done):
    signal(done)
    out[...] = (partial1[...] + got3_ref[...].astype(F32)).astype(BF16)


def base_body(
    q_ref, pair_ref, p_ref, n1_ref, e3_ref, o3_ref, coef_ref, swap_ref, w_ref, own3_ref,
    token, pulled, base, coef_t,
):
    rows, width = q_ref.shape
    w = jnp.broadcast_to(w_ref[...], (rows, rows)).T[:, :1]
    odd = lax.axis_index("blk") % 2 == 1
    blocks = (p_ref, n1_ref, pair_ref, e3_ref, o3_ref)
    for s in range(5):
        k = min(s, 3) * rows
        coef_t[:, s * rows : (s + 1) * rows] = coef_ref[:, k : k + rows].astype(F32).T.astype(BF16)
    coef = [coef_ref[:, :rows], jnp.where(odd, swap_ref[:, :rows], jnp.zeros((rows, rows), BF16))]
    coef = jnp.concatenate(coef, axis=1)
    for c in range(0, width, CHUNK):
        at = slice(c, c + CHUNK)
        held = jnp.concatenate([block[:, at] for block in blocks], axis=0)
        pulled[:, at] = dot(coef_t[...], held, ((1,), (0,))) - w * p_ref[:, at].astype(F32)
        held = jnp.concatenate([q_ref[:, at], pair_ref[:, width + c : width + c + CHUNK]], axis=0)
        own = dot(coef, held, ((1,), (0,))) + own3_ref[:, at].astype(F32)
        base[:, at] = own - w * q_ref[:, at].astype(F32)


def finish_body(groups, pulled, base, own1, *refs):
    backs = refs[:groups]
    q_out, p_out, q_held, p_held, sems = refs[groups:]
    rows, cols = pulled.shape[0], backs[0].shape[1]
    g = lax.axis_index("grp")
    copies = []
    for r, back in enumerate(backs):
        at = pl.ds(pl.multiple_of((g ^ r) * cols, 128), cols)
        q_held[:, at] = (INV_TEMP * (pulled[:, at] + back[:rows].astype(F32))).astype(BF16)
        copies.append(pltpu.make_async_copy(q_held.at[:, at], q_out.at[:, at], sems.at[2 * r]))
        copies[-1].start()
        total = base[:, at] + back[rows:].astype(F32) + own1[:, at].astype(F32)
        p_held[:, at] = (INV_TEMP * total).astype(BF16)
        copies.append(pltpu.make_async_copy(p_held.at[:, at], p_out.at[:, at], sems.at[2 * r + 1]))
        copies[-1].start()
    for copy in copies:
        copy.wait()


def per_device(queries, passages, hard_index, weights):
    rows, width = queries.shape
    groups = lax.axis_size("grp")
    loop = lax.axis_size("blk")
    cols = width // groups

    def shift(array, by, sources=range(loop)):
        return lax.ppermute(array, "blk", [(i, (i + by) % loop) for i in sources])

    evens, odds = range(0, loop, 2), range(1, loop, 2)

    def swap(array):
        return lax.ppermute(array, "blk", [(i, i ^ 1) for i in range(loop)])

    def over_groups(array, r):
        return lax.ppermute(array, "grp", [(i, i ^ r) for i in range(groups)])

    def exchange(arrays):
        out = list(arrays)
        for r in reversed(range(1, groups)):
            out[r] = over_groups(arrays[r], r)
        return out

    def like(*shape, dtype=BF16):
        return jax.ShapeDtypeStruct(shape, dtype)

    block, block32 = like(rows, width), like(rows, width, dtype=F32)
    square, triple = like(rows, rows, dtype=F32), like(3, rows, dtype=F32)
    piece, back = like(2 * rows + TAIL, cols), like(2 * rows, cols)

    next1 = shift(passages, -1)

    held_q, held_p, *pieces, token = local_call(
        functools.partial(load_body, groups, loop * rows),
        [block, block] + [piece] * groups + [TOKEN],
        queries, passages, hard_index.T,
        in_specs=[HBM, HBM, VMEM],
        scratch=[pltpu.SemaphoreType.DMA((2 * groups,))],
    )
    pieces = exchange(pieces)

    next3_even = shift(held_p, -3, [2, *odds])
    (next1,) = local_call(pass_body, [block], next1, token, flops=LONG)
    next3_odd = shift(next1, -2, odds[1:])
    pair = swap(
        local_call(choose_body, [like(rows, 2 * width)], next1, next3_even, held_q, flops=LONG)[0]
    )

    s0, s1, s3 = local_call(scores_body, [square] * 3, held_q, held_p, next1, next3_even)
    parts = local_call(
        functools.partial(hard_scores_body, groups), [triple] * groups, *pieces, s0, flops=LONG
    )
    (s2,) = local_call(last_score_body, [square], held_q, pair)
    parts = exchange(parts)
    loss_rows, coef, hard_coef, to_core, term3 = local_call(
        functools.partial(weigh_body, groups),
        [like(1, rows, dtype=F32), like(rows, 4 * rows), triple, like(rows, 2 * rows), block],
        held_q, s0, s1, s2, s3, next3_odd, weights[None, :], *parts,
    )

    got3 = shift(term3, 2, odds[:-1])
    from_core = swap(to_core)
    sent3, partial1, token = local_call(
        sums_body, [block, block32, TOKEN], held_q, pair, coef, from_core, term3
    )
    own3 = shift(sent3, 3, [*evens, loop - 1])

    hard_coefs = exchange([hard_coef] * groups)
    square_all = pltpu.VMEM((groups * rows, groups * rows), BF16)
    *backs, token = local_call(
        functools.partial(hard_grads_body, groups), [back] * groups + [TOKEN],
        *pieces, *hard_coefs, token, scratch=[square_all, square_all],
    )
    backs = exchange(backs)

    sent1, token = local_call(relay_body, [block, TOKEN], partial1, got3, flops=SOME)
    own1 = shift(sent1, 1, odds)

    pulled, base = local_call(
        base_body, [block32, block32],
        held_q, pair, held_p, next1, next3_even, next3_odd, coef, from_core,
        weights[None, :], own3, token, flops=LONG, scratch=[pltpu.VMEM((rows, 5 * rows), BF16)],
    )
    grad_queries, grad_passages = local_call(
        functools.partial(finish_body, groups), [block, block], pulled, base, own1, *backs,
        out_specs=[HBM, HBM],
        scratch=[
            pltpu.VMEM((rows, width), BF16),
            pltpu.VMEM((rows, width), BF16),
            pltpu.SemaphoreType.DMA((2 * groups,)),
        ],
    )
    return loss_rows.reshape(rows), grad_queries, grad_passages


def solution(mesh):
    rows = P(("grp", "blk"))
    matrix = P(("grp", "blk"), None)
    return jax.shard_map(
        per_device,
        mesh=mesh,
        in_specs=(matrix, matrix, matrix, rows),
        out_specs=(rows, matrix, matrix),
        check_vma=False,
    )
```

```python
import functools
import math

import jax
import jax.numpy as jnp
from jax import lax
from jax.experimental import pallas as pl
from jax.experimental.pallas import tpu as pltpu
from jax.sharding import PartitionSpec as P

INV_TEMP = 50.0
BF16 = jnp.bfloat16
F32 = jnp.float32
CHUNK = 512
TAIL = 16
LONG, SOME = 5 * 10**10, 16 * 10**9
VMEM = pl.BlockSpec(memory_space=pltpu.VMEM)
HBM = pl.BlockSpec(memory_space=pltpu.HBM)
TOKEN = jax.ShapeDtypeStruct((8, 128), F32)


def dot(left, right, dims):
    return lax.dot_general(left, right, (dims, ((), ())), preferred_element_type=F32)


def size_of(arrays):
    return sum(math.prod(a.shape) * jnp.dtype(a.dtype).itemsize for a in arrays)


def local_call(body, out_shape, *args, flops=0, in_specs=None, out_specs=None, scratch=(), limit=20):
    return pl.pallas_call(
        body,
        out_shape=out_shape,
        in_specs=in_specs or [VMEM] * len(args),
        out_specs=out_specs or [VMEM] * len(out_shape),
        scratch_shapes=list(scratch),
        cost_estimate=pl.CostEstimate(
            flops=flops, bytes_accessed=size_of(args) + size_of(out_shape), transcendentals=0
        ),
        compiler_params=pltpu.CompilerParams(vmem_limit_bytes=limit * 2**20),
    )(*args)


def signal(token):
    token[...] = jnp.zeros(token.shape, token.dtype)


def split_index(index, rows, group_rows):
    if group_rows & (group_rows - 1) or rows & (rows - 1):
        return index // group_rows, index % rows
    return index >> (group_rows.bit_length() - 1), index & (rows - 1)


def load_body(groups, group_rows, q_hbm, p_hbm, index_hbm, *refs):
    pieces, (token, index_ref, sems) = refs[:groups], refs[groups:]
    rows = q_hbm.shape[0]
    cols = pieces[0].shape[1]
    g = lax.axis_index("grp")
    index_copy = pltpu.make_async_copy(index_hbm, index_ref, sems.at[2 * groups])
    index_copy.start()
    copies = []
    for r, piece in enumerate(pieces):
        at = pl.ds(pl.multiple_of((g ^ r) * cols, 128), cols)
        for n, source in enumerate((q_hbm, p_hbm)):
            target = piece.at[pl.ds(n * rows, rows)]
            copies.append(pltpu.make_async_copy(source.at[:, at], target, sems.at[2 * r + n]))
            copies[-1].start()
    signal(token)
    index_copy.wait()
    index = jnp.concatenate([index_ref[...], jnp.zeros((TAIL - 3, rows), jnp.int32)], axis=0)
    named_group, named_row = split_index(index, rows, group_rows)
    named_group = named_group.astype(F32).astype(BF16)
    named_row = named_row.astype(F32).astype(BF16)
    for piece in pieces:
        piece[2 * rows :, :rows] = named_group
        piece[2 * rows :, rows : 2 * rows] = named_row
        if cols > 2 * rows:
            piece[2 * rows :, 2 * rows :] = jnp.zeros((TAIL, cols - 2 * rows), BF16)
    for copy in copies:
        copy.wait()


def places_of(piece_ref, rows):
    tail = piece_ref[2 * rows :, : 2 * rows].astype(F32).astype(jnp.int32)
    g = lax.axis_index("grp")
    return [(tail[k : k + 1, :rows] ^ g) * rows + tail[k : k + 1, rows:] for k in range(3)]


def hard_scores_body(groups, *refs):
    pieces, outs = refs[:groups], refs[groups + 1 :]
    rows = outs[0].shape[1]
    ids = lax.broadcasted_iota(jnp.int32, (groups * rows, rows), 0)
    p_all = jnp.concatenate([piece[rows : 2 * rows] for piece in pieces], axis=0)
    for r in range(groups):
        places = places_of(pieces[r], rows)
        dots = dot(p_all, pieces[r][:rows], ((1,), (1,)))
        for k in range(3):
            hit = jnp.where(ids == places[k], dots, 0.0)
            outs[r][k : k + 1] = jnp.sum(hit, axis=0, keepdims=True)


def hard_grads_body(groups, *refs):
    pieces, coefs, outs = refs[:groups], refs[groups : 2 * groups], refs[2 * groups + 1 : 3 * groups + 1]
    token, matrix, matrix_t = refs[3 * groups + 1 :]
    rows = coefs[0].shape[1]
    cols = outs[0].shape[1]
    signal(token)
    ids = lax.broadcasted_iota(jnp.int32, (groups * rows, rows), 0)
    for r in range(groups):
        places = places_of(pieces[r], rows)
        total = jnp.zeros(ids.shape, F32)
        for k in range(3):
            total += jnp.where(ids == places[k], coefs[r][k : k + 1], 0.0)
        mine = slice(r * rows, (r + 1) * rows)
        matrix[:, mine] = total.astype(BF16)
        matrix_t[mine] = total.T.astype(BF16)
    step = min(cols, 256)
    for c in range(0, cols, step):
        at = slice(c, c + step)
        q_all = jnp.concatenate([piece[:rows, at] for piece in pieces], axis=0)
        p_all = jnp.concatenate([piece[rows : 2 * rows, at] for piece in pieces], axis=0)
        grad_q = dot(matrix_t[...], p_all, ((1,), (0,))).astype(BF16)
        grad_p = dot(matrix[...], q_all, ((1,), (0,))).astype(BF16)
        for r in range(groups):
            mine = slice(r * rows, (r + 1) * rows)
            outs[r][:rows, at] = grad_q[mine]
            outs[r][rows:, at] = grad_p[mine]


def pass_body(source, token, out):
    out[...] = source[...]


def choose_body(n1_ref, e3_ref, q_ref, out):
    width = q_ref.shape[1]
    odd = lax.axis_index("blk") % 2 == 1
    out[:, width:] = q_ref[...]

    @pl.when(odd)
    def _():
        out[:, :width] = n1_ref[...]

    @pl.when(jnp.logical_not(odd))
    def _():
        out[:, :width] = e3_ref[...]


def scores_body(q_ref, *refs):
    half = len(refs) // 2
    for block, out in zip(refs[:half], refs[half:]):
        out[...] = dot(block[...], q_ref[...], ((1,), (1,)))


def last_score_body(q_ref, pair_ref, out):
    out[...] = dot(pair_ref[:, : q_ref.shape[1]], q_ref[...], ((1,), (1,)))


def weigh_body(
    groups, *refs
):
    parts, refs = refs[:groups], refs[groups:]
    q_ref, s0_ref, s1_ref, s2_ref, s3_ref, last_ref, w_ref, *refs = refs
    loss_ref, coef_ref, hard_out, swap_ref, term3_ref = refs
    rows, width = q_ref.shape
    w = w_ref[...]
    s3 = INV_TEMP * (s3_ref[...] + dot(last_ref[...], q_ref[...], ((1,), (1,))))
    scores = [INV_TEMP * s0_ref[...], INV_TEMP * s1_ref[...], INV_TEMP * s2_ref[...], s3]
    hard = parts[0][...]
    for other in parts[1:]:
        hard = hard + other[...]
    hard = INV_TEMP * hard
    largest = jnp.max(hard, axis=0, keepdims=True)
    for block in scores:
        largest = jnp.maximum(largest, jnp.max(block, axis=0, keepdims=True))
    summed = jnp.sum(jnp.exp(hard - largest), axis=0, keepdims=True)
    for block in scores:
        summed = summed + jnp.sum(jnp.exp(block - largest), axis=0, keepdims=True)
    log_total = largest + jnp.log(summed)
    for s, block in enumerate(scores):
        coef = (w * jnp.exp(block - log_total)).astype(BF16)
        coef_ref[:, s * rows : (s + 1) * rows] = coef
        if s in (1, 2):
            swap_ref[:, (s - 1) * rows : s * rows] = coef
    coef3 = coef_ref[:, 3 * rows :]
    for c in range(0, width, CHUNK):
        at = slice(c, c + CHUNK)
        term3_ref[:, at] = dot(coef3, q_ref[:, at], ((1,), (0,))).astype(BF16)
    hard_out[...] = (w * jnp.exp(hard - log_total)).astype(BF16).astype(F32)
    eye = lax.broadcasted_iota(jnp.int32, (rows, rows), 0) == lax.broadcasted_iota(
        jnp.int32, (rows, rows), 1
    )
    loss_ref[...] = log_total - jnp.sum(jnp.where(eye, scores[0], 0.0), axis=0, keepdims=True)


def sums_body(q_ref, pair_ref, coef_ref, swap_ref, sent3, partial1, token):
    signal(token)
    rows, width = q_ref.shape
    odd = lax.axis_index("blk") % 2 == 1
    mine = jnp.where(odd, coef_ref[:, rows : 2 * rows], coef_ref[:, 3 * rows :])
    coef = jnp.concatenate([mine, swap_ref[:, rows:]], axis=1)
    for c in range(0, width, CHUNK):
        at = slice(c, c + CHUNK)
        held = jnp.concatenate([q_ref[:, at], pair_ref[:, width + c : width + c + CHUNK]], axis=0)
        total = dot(coef, held, ((1,), (0,)))
        sent3[:, at] = total.astype(BF16)
        partial1[:, at] = total


def relay_body(partial1, got3_ref, out, done):
    signal(done)
    out[...] = (partial1[...] + got3_ref[...].astype(F32)).astype(BF16)


def base_body(
    q_ref, pair_ref, p_ref, n1_ref, e3_ref, o3_ref, coef_ref, swap_ref, w_ref, own3_ref,
    token, pulled, base, coef_t,
):
    rows, width = q_ref.shape
    w = jnp.broadcast_to(w_ref[...], (rows, rows)).T[:, :1]
    odd = lax.axis_index("blk") % 2 == 1
    blocks = (p_ref, n1_ref, pair_ref, e3_ref, o3_ref)
    for s in range(5):
        k = min(s, 3) * rows
        coef_t[:, s * rows : (s + 1) * rows] = coef_ref[:, k : k + rows].astype(F32).T.astype(BF16)
    coef = [coef_ref[:, :rows], jnp.where(odd, swap_ref[:, :rows], jnp.zeros((rows, rows), BF16))]
    coef = jnp.concatenate(coef, axis=1)
    for c in range(0, width, CHUNK):
        at = slice(c, c + CHUNK)
        held = jnp.concatenate([block[:, at] for block in blocks], axis=0)
        pulled[:, at] = dot(coef_t[...], held, ((1,), (0,))) - w * p_ref[:, at].astype(F32)
        held = jnp.concatenate([q_ref[:, at], pair_ref[:, width + c : width + c + CHUNK]], axis=0)
        own = dot(coef, held, ((1,), (0,))) + own3_ref[:, at].astype(F32)
        base[:, at] = own - w * q_ref[:, at].astype(F32)


def finish_body(groups, pulled, base, own1, *refs):
    backs = refs[:groups]
    q_out, p_out, q_held, p_held, sems = refs[groups:]
    rows, cols = pulled.shape[0], backs[0].shape[1]
    g = lax.axis_index("grp")
    copies = []
    for r, back in enumerate(backs):
        at = pl.ds(pl.multiple_of((g ^ r) * cols, 128), cols)
        q_held[:, at] = (INV_TEMP * (pulled[:, at] + back[:rows].astype(F32))).astype(BF16)
        copies.append(pltpu.make_async_copy(q_held.at[:, at], q_out.at[:, at], sems.at[2 * r]))
        copies[-1].start()
        total = base[:, at] + back[rows:].astype(F32) + own1[:, at].astype(F32)
        p_held[:, at] = (INV_TEMP * total).astype(BF16)
        copies.append(pltpu.make_async_copy(p_held.at[:, at], p_out.at[:, at], sems.at[2 * r + 1]))
        copies[-1].start()
    for copy in copies:
        copy.wait()


def per_device(queries, passages, hard_index, weights):
    rows, width = queries.shape
    groups = lax.axis_size("grp")
    loop = lax.axis_size("blk")
    cols = width // groups

    def shift(array, by, which=(0, 1)):
        pairs = [(i, (i + by) % loop) for i in range(loop) if i % 2 in which]
        return lax.ppermute(array, "blk", pairs)

    def swap(array):
        return lax.ppermute(array, "blk", [(i, i ^ 1) for i in range(loop)])

    def over_groups(array, r):
        return lax.ppermute(array, "grp", [(i, i ^ r) for i in range(groups)])

    def exchange(arrays):
        out = list(arrays)
        for r in reversed(range(1, groups)):
            out[r] = over_groups(arrays[r], r)
        return out

    def like(*shape, dtype=BF16):
        return jax.ShapeDtypeStruct(shape, dtype)

    block, block32 = like(rows, width), like(rows, width, dtype=F32)
    square, triple = like(rows, rows, dtype=F32), like(3, rows, dtype=F32)
    piece, back = like(2 * rows + TAIL, cols), like(2 * rows, cols)

    next1 = shift(passages, -1)

    *pieces, token = local_call(
        functools.partial(load_body, groups, loop * rows), [piece] * groups + [TOKEN],
        queries, passages, hard_index.T, in_specs=[HBM, HBM, HBM],
        scratch=[pltpu.VMEM((3, rows), jnp.int32), pltpu.SemaphoreType.DMA((2 * groups + 1,))],
        limit=51,
    )
    pieces = exchange(pieces)

    (later_p,) = local_call(pass_body, [block], passages, token)
    next3_even = shift(later_p, -3, (1,))
    (next1,) = local_call(pass_body, [block], next1, token, flops=LONG)
    next3_odd = shift(next1, -2, (1,))
    pair = swap(
        local_call(choose_body, [like(rows, 2 * width)], next1, next3_even, queries, flops=LONG)[0]
    )

    s0, s1, s3 = local_call(scores_body, [square] * 3, queries, passages, next1, next3_even)
    parts = local_call(
        functools.partial(hard_scores_body, groups), [triple] * groups, *pieces, s0, flops=LONG
    )
    (s2,) = local_call(last_score_body, [square], queries, pair)
    parts = exchange(parts)
    loss_rows, coef, hard_coef, to_core, term3 = local_call(
        functools.partial(weigh_body, groups),
        [like(1, rows, dtype=F32), like(rows, 4 * rows), triple, like(rows, 2 * rows), block],
        *parts, queries, s0, s1, s2, s3, next3_odd, weights[None, :],
    )

    got3 = shift(term3, 2, (1,))
    from_core = swap(to_core)
    sent3, partial1, token = local_call(
        sums_body, [block, block32, TOKEN], queries, pair, coef, from_core
    )
    own3 = shift(sent3, 3, (0,))

    hard_coefs = exchange([hard_coef] * groups)
    square_all = pltpu.VMEM((groups * rows, groups * rows), BF16)
    *backs, token = local_call(
        functools.partial(hard_grads_body, groups), [back] * groups + [TOKEN],
        *pieces, *hard_coefs, token, scratch=[square_all, square_all],
    )
    backs = exchange(backs)

    sent1, token = local_call(relay_body, [block, TOKEN], partial1, got3, flops=SOME)
    own1 = shift(sent1, 1, (1,))

    pulled, base = local_call(
        base_body, [block32, block32],
        queries, pair, passages, next1, next3_even, next3_odd, coef, from_core,
        weights[None, :], own3, token, flops=LONG, scratch=[pltpu.VMEM((rows, 5 * rows), BF16)],
    )
    grad_queries, grad_passages = local_call(
        functools.partial(finish_body, groups), [block, block], pulled, base, own1, *backs,
        out_specs=[HBM, HBM],
        scratch=[
            pltpu.VMEM((rows, width), BF16),
            pltpu.VMEM((rows, width), BF16),
            pltpu.SemaphoreType.DMA((2 * groups,)),
        ],
    )
    return loss_rows.reshape(rows), grad_queries, grad_passages


def solution(mesh):
    rows = P(("grp", "blk"))
    matrix = P(("grp", "blk"), None)
    return jax.shard_map(
        per_device,
        mesh=mesh,
        in_specs=(matrix, matrix, matrix, rows),
        out_specs=(rows, matrix, matrix),
        check_vma=False,
    )
```

```python
import functools
import math

import jax
import jax.numpy as jnp
from jax import lax
from jax.experimental import pallas as pl
from jax.experimental.pallas import tpu as pltpu
from jax.sharding import PartitionSpec as P

INV_TEMP = 50.0
BF16 = jnp.bfloat16
F32 = jnp.float32
CHUNK = 512
TAIL = 16
LONG, SOME = 5 * 10**10, 10 * 10**9
VMEM = pl.BlockSpec(memory_space=pltpu.VMEM)
HBM = pl.BlockSpec(memory_space=pltpu.HBM)
TOKEN = jax.ShapeDtypeStruct((8, 128), F32)


def dot(left, right, dims):
    return lax.dot_general(left, right, (dims, ((), ())), preferred_element_type=F32)


def size_of(arrays):
    return sum(math.prod(a.shape) * jnp.dtype(a.dtype).itemsize for a in arrays)


def local_call(body, out_shape, *args, flops=0, in_specs=None, out_specs=None, scratch=(), limit=20):
    return pl.pallas_call(
        body,
        out_shape=out_shape,
        in_specs=in_specs or [VMEM] * len(args),
        out_specs=out_specs or [VMEM] * len(out_shape),
        scratch_shapes=list(scratch),
        cost_estimate=pl.CostEstimate(
            flops=flops, bytes_accessed=size_of(args) + size_of(out_shape), transcendentals=0
        ),
        compiler_params=pltpu.CompilerParams(vmem_limit_bytes=limit * 2**20),
    )(*args)


def signal(token):
    token[...] = jnp.zeros(token.shape, token.dtype)


def split_index(index, rows, group_rows):
    if group_rows & (group_rows - 1) or rows & (rows - 1):
        return index // group_rows, index % rows
    return index >> (group_rows.bit_length() - 1), index & (rows - 1)


def load_body(groups, group_rows, q_hbm, p_hbm, index_hbm, *refs):
    pieces, (token, index_ref, sems) = refs[:groups], refs[groups:]
    rows = q_hbm.shape[0]
    cols = pieces[0].shape[1]
    g = lax.axis_index("grp")
    index_copy = pltpu.make_async_copy(index_hbm, index_ref, sems.at[2 * groups])
    index_copy.start()
    copies = []
    for r, piece in enumerate(pieces):
        at = pl.ds(pl.multiple_of((g ^ r) * cols, 128), cols)
        for n, source in enumerate((q_hbm, p_hbm)):
            target = piece.at[pl.ds(n * rows, rows)]
            copies.append(pltpu.make_async_copy(source.at[:, at], target, sems.at[2 * r + n]))
            copies[-1].start()
    signal(token)
    index_copy.wait()
    index = jnp.concatenate([index_ref[...], jnp.zeros((TAIL - 3, rows), jnp.int32)], axis=0)
    named_group, named_row = split_index(index, rows, group_rows)
    named_group = named_group.astype(F32).astype(BF16)
    named_row = named_row.astype(F32).astype(BF16)
    for piece in pieces:
        piece[2 * rows :, :rows] = named_group
        piece[2 * rows :, rows : 2 * rows] = named_row
        if cols > 2 * rows:
            piece[2 * rows :, 2 * rows :] = jnp.zeros((TAIL, cols - 2 * rows), BF16)
    for copy in copies:
        copy.wait()


def places_of(piece_ref, rows):
    tail = piece_ref[2 * rows :, : 2 * rows].astype(F32).astype(jnp.int32)
    g = lax.axis_index("grp")
    return [(tail[k : k + 1, :rows] ^ g) * rows + tail[k : k + 1, rows:] for k in range(3)]


def hard_scores_body(groups, *refs):
    pieces, outs = refs[:groups][::-1], refs[groups + 1 :]
    rows = outs[0].shape[1]
    ids = lax.broadcasted_iota(jnp.int32, (groups * rows, rows), 0)
    p_all = jnp.concatenate([piece[rows : 2 * rows] for piece in pieces], axis=0)
    for r in range(groups):
        places = places_of(pieces[r], rows)
        dots = dot(p_all, pieces[r][:rows], ((1,), (1,)))
        for k in range(3):
            hit = jnp.where(ids == places[k], dots, 0.0)
            outs[r][k : k + 1] = jnp.sum(hit, axis=0, keepdims=True)


def hard_grads_body(groups, *refs):
    coefs, pieces, outs = refs[:groups][::-1], refs[groups : 2 * groups][::-1], refs[2 * groups + 1 : 3 * groups + 1]
    token, matrix, matrix_t = refs[3 * groups + 1 :]
    rows = coefs[0].shape[1]
    cols = outs[0].shape[1]
    signal(token)
    ids = lax.broadcasted_iota(jnp.int32, (groups * rows, rows), 0)
    for r in range(groups):
        places = places_of(pieces[r], rows)
        total = jnp.zeros(ids.shape, F32)
        for k in range(3):
            total += jnp.where(ids == places[k], coefs[r][k : k + 1], 0.0)
        mine = slice(r * rows, (r + 1) * rows)
        matrix[:, mine] = total.astype(BF16)
        matrix_t[mine] = total.T.astype(BF16)
    step = min(cols, 256)
    for c in range(0, cols, step):
        at = slice(c, c + step)
        q_all = jnp.concatenate([piece[:rows, at] for piece in pieces], axis=0)
        p_all = jnp.concatenate([piece[rows : 2 * rows, at] for piece in pieces], axis=0)
        grad_q = dot(matrix_t[...], p_all, ((1,), (0,))).astype(BF16)
        grad_p = dot(matrix[...], q_all, ((1,), (0,))).astype(BF16)
        for r in range(groups):
            mine = slice(r * rows, (r + 1) * rows)
            outs[r][:rows, at] = grad_q[mine]
            outs[r][rows:, at] = grad_p[mine]


def pass_body(source, token, out):
    out[...] = source[...]


def choose_body(n1_ref, e3_ref, q_ref, out):
    width = q_ref.shape[1]
    odd = lax.axis_index("blk") % 2 == 1
    out[:, width:] = q_ref[...]

    @pl.when(odd)
    def _():
        out[:, :width] = n1_ref[...]

    @pl.when(jnp.logical_not(odd))
    def _():
        out[:, :width] = e3_ref[...]


def scores_body(q_ref, *refs):
    half = len(refs) // 2
    for block, out in zip(refs[:half], refs[half:]):
        out[...] = dot(block[...], q_ref[...], ((1,), (1,)))


def last_score_body(q_ref, pair_ref, out):
    out[...] = dot(pair_ref[:, : q_ref.shape[1]], q_ref[...], ((1,), (1,)))


def weigh_body(
    groups, *refs
):
    parts, refs = refs[:groups], refs[groups:]
    q_ref, s0_ref, s1_ref, s2_ref, s3_ref, last_ref, w_ref, *refs = refs
    loss_ref, coef_ref, hard_out, swap_ref, term3_ref = refs
    rows, width = q_ref.shape
    w = w_ref[...]
    s3 = INV_TEMP * (s3_ref[...] + dot(last_ref[...], q_ref[...], ((1,), (1,))))
    scores = [INV_TEMP * s0_ref[...], INV_TEMP * s1_ref[...], INV_TEMP * s2_ref[...], s3]
    hard = parts[-1][...]
    for other in parts[-2::-1]:
        hard = hard + other[...]
    hard = INV_TEMP * hard
    largest = jnp.max(hard, axis=0, keepdims=True)
    for block in scores:
        largest = jnp.maximum(largest, jnp.max(block, axis=0, keepdims=True))
    summed = jnp.sum(jnp.exp(hard - largest), axis=0, keepdims=True)
    for block in scores:
        summed = summed + jnp.sum(jnp.exp(block - largest), axis=0, keepdims=True)
    log_total = largest + jnp.log(summed)
    for s, block in enumerate(scores):
        coef = (w * jnp.exp(block - log_total)).astype(BF16)
        coef_ref[:, s * rows : (s + 1) * rows] = coef
        if s in (1, 2):
            swap_ref[:, (s - 1) * rows : s * rows] = coef
    coef3 = coef_ref[:, 3 * rows :]
    for c in range(0, width, CHUNK):
        at = slice(c, c + CHUNK)
        term3_ref[:, at] = dot(coef3, q_ref[:, at], ((1,), (0,))).astype(BF16)
    hard_out[...] = (w * jnp.exp(hard - log_total)).astype(BF16).astype(F32)
    eye = lax.broadcasted_iota(jnp.int32, (rows, rows), 0) == lax.broadcasted_iota(
        jnp.int32, (rows, rows), 1
    )
    loss_ref[...] = log_total - jnp.sum(jnp.where(eye, scores[0], 0.0), axis=0, keepdims=True)


def sums_body(q_ref, pair_ref, coef_ref, swap_ref, sent3, partial1, token):
    signal(token)
    rows, width = q_ref.shape
    odd = lax.axis_index("blk") % 2 == 1
    mine = jnp.where(odd, coef_ref[:, rows : 2 * rows], coef_ref[:, 3 * rows :])
    coef = jnp.concatenate([mine, swap_ref[:, rows:]], axis=1)
    for c in range(0, width, CHUNK):
        at = slice(c, c + CHUNK)
        held = jnp.concatenate([q_ref[:, at], pair_ref[:, width + c : width + c + CHUNK]], axis=0)
        total = dot(coef, held, ((1,), (0,)))
        sent3[:, at] = total.astype(BF16)
        partial1[:, at] = total


def relay_body(partial1, got3_ref, out, done):
    signal(done)
    out[...] = (partial1[...] + got3_ref[...].astype(F32)).astype(BF16)


def base_body(
    q_ref, pair_ref, p_ref, n1_ref, e3_ref, o3_ref, coef_ref, swap_ref, w_ref, own3_ref,
    token, pulled, base, coef_t,
):
    rows, width = q_ref.shape
    w = jnp.broadcast_to(w_ref[...], (rows, rows)).T[:, :1]
    odd = lax.axis_index("blk") % 2 == 1
    blocks = (p_ref, n1_ref, pair_ref, e3_ref, o3_ref)
    for s in range(5):
        k = min(s, 3) * rows
        coef_t[:, s * rows : (s + 1) * rows] = coef_ref[:, k : k + rows].astype(F32).T.astype(BF16)
    coef = [coef_ref[:, :rows], jnp.where(odd, swap_ref[:, :rows], jnp.zeros((rows, rows), BF16))]
    coef = jnp.concatenate(coef, axis=1)
    for c in range(0, width, CHUNK):
        at = slice(c, c + CHUNK)
        held = jnp.concatenate([block[:, at] for block in blocks], axis=0)
        pulled[:, at] = dot(coef_t[...], held, ((1,), (0,))) - w * p_ref[:, at].astype(F32)
        held = jnp.concatenate([q_ref[:, at], pair_ref[:, width + c : width + c + CHUNK]], axis=0)
        own = dot(coef, held, ((1,), (0,))) + own3_ref[:, at].astype(F32)
        base[:, at] = own - w * q_ref[:, at].astype(F32)


def finish_body(groups, pulled, base, own1, *refs):
    backs = refs[:groups][::-1]
    q_out, p_out, q_held, p_held, sems = refs[groups:]
    rows, cols = pulled.shape[0], backs[0].shape[1]
    g = lax.axis_index("grp")
    copies = []
    for r, back in enumerate(backs):
        at = pl.ds(pl.multiple_of((g ^ r) * cols, 128), cols)
        q_held[:, at] = (INV_TEMP * (pulled[:, at] + back[:rows].astype(F32))).astype(BF16)
        copies.append(pltpu.make_async_copy(q_held.at[:, at], q_out.at[:, at], sems.at[2 * r]))
        copies[-1].start()
        total = base[:, at] + back[rows:].astype(F32) + own1[:, at].astype(F32)
        p_held[:, at] = (INV_TEMP * total).astype(BF16)
        copies.append(pltpu.make_async_copy(p_held.at[:, at], p_out.at[:, at], sems.at[2 * r + 1]))
        copies[-1].start()
    for copy in copies:
        copy.wait()


def per_device(queries, passages, hard_index, weights):
    rows, width = queries.shape
    groups = lax.axis_size("grp")
    loop = lax.axis_size("blk")
    cols = width // groups

    def shift(array, by, which=(0, 1)):
        pairs = [(i, (i + by) % loop) for i in range(loop) if i % 2 in which]
        return lax.ppermute(array, "blk", pairs)

    def swap(array):
        return lax.ppermute(array, "blk", [(i, i ^ 1) for i in range(loop)])

    def over_groups(array, r):
        return lax.ppermute(array, "grp", [(i, i ^ r) for i in range(groups)])

    def exchange(arrays):
        out = list(arrays)
        for r in reversed(range(1, groups)):
            out[r] = over_groups(arrays[r], r)
        return out

    def like(*shape, dtype=BF16):
        return jax.ShapeDtypeStruct(shape, dtype)

    block, block32 = like(rows, width), like(rows, width, dtype=F32)
    square, triple = like(rows, rows, dtype=F32), like(3, rows, dtype=F32)
    piece, back = like(2 * rows + TAIL, cols), like(2 * rows, cols)

    next1 = shift(passages, -1)

    *pieces, token = local_call(
        functools.partial(load_body, groups, loop * rows), [piece] * groups + [TOKEN],
        queries, passages, hard_index.T, in_specs=[HBM, HBM, HBM],
        scratch=[pltpu.VMEM((3, rows), jnp.int32), pltpu.SemaphoreType.DMA((2 * groups + 1,))],
        limit=51,
    )
    pieces = exchange(pieces)

    (later_p,) = local_call(pass_body, [block], passages, token)
    next3_even = shift(later_p, -3, (1,))
    (next1,) = local_call(pass_body, [block], next1, token, flops=LONG)
    next3_odd = shift(next1, -2, (1,))
    pair = swap(
        local_call(choose_body, [like(rows, 2 * width)], next1, next3_even, queries, flops=LONG)[0]
    )

    s0, s1, s3 = local_call(scores_body, [square] * 3, queries, passages, next1, next3_even)
    parts = local_call(
        functools.partial(hard_scores_body, groups), [triple] * groups, *pieces[::-1], s0, flops=LONG
    )
    (s2,) = local_call(last_score_body, [square], queries, pair)
    parts = exchange(parts)
    loss_rows, coef, hard_coef, to_core, term3 = local_call(
        functools.partial(weigh_body, groups),
        [like(1, rows, dtype=F32), like(rows, 4 * rows), triple, like(rows, 2 * rows), block],
        *parts[::-1], queries, s0, s1, s2, s3, next3_odd, weights[None, :],
    )

    got3 = shift(term3, 2, (1,))
    from_core = swap(to_core)
    sent3, partial1, token = local_call(
        sums_body, [block, block32, TOKEN], queries, pair, coef, from_core
    )
    own3 = shift(sent3, 3, (0,))

    hard_coefs = exchange([hard_coef] * groups)
    square_all = pltpu.VMEM((groups * rows, groups * rows), BF16)
    *backs, token = local_call(
        functools.partial(hard_grads_body, groups), [back] * groups + [TOKEN],
        *hard_coefs[::-1], *pieces[::-1], token, scratch=[square_all, square_all],
    )
    backs = exchange(backs)

    sent1, token = local_call(relay_body, [block, TOKEN], partial1, got3, flops=SOME)
    own1 = shift(sent1, 1, (1,))

    pulled, base = local_call(
        base_body, [block32, block32],
        queries, pair, passages, next1, next3_even, next3_odd, coef, from_core,
        weights[None, :], own3, token, flops=LONG, scratch=[pltpu.VMEM((rows, 5 * rows), BF16)],
    )
    grad_queries, grad_passages = local_call(
        functools.partial(finish_body, groups), [block, block], pulled, base, own1, *backs[::-1],
        out_specs=[HBM, HBM],
        scratch=[
            pltpu.VMEM((rows, width), BF16),
            pltpu.VMEM((rows, width), BF16),
            pltpu.SemaphoreType.DMA((2 * groups,)),
        ],
    )
    return loss_rows.reshape(rows), grad_queries, grad_passages


def solution(mesh):
    rows = P(("grp", "blk"))
    matrix = P(("grp", "blk"), None)
    return jax.shard_map(
        per_device,
        mesh=mesh,
        in_specs=(matrix, matrix, matrix, rows),
        out_specs=(rows, matrix, matrix),
        check_vma=False,
    )
```

```python
import functools
import math

import jax
import jax.numpy as jnp
from jax import lax
from jax.experimental import pallas as pl
from jax.experimental.pallas import tpu as pltpu
from jax.sharding import PartitionSpec as P

INV_TEMP = 50.0
BF16 = jnp.bfloat16
F32 = jnp.float32
CHUNK = 512
TAIL = 16
LONG, SOME = 5 * 10**10, 16 * 10**9
VMEM = pl.BlockSpec(memory_space=pltpu.VMEM)
HBM = pl.BlockSpec(memory_space=pltpu.HBM)
TOKEN = jax.ShapeDtypeStruct((8, 128), F32)


def dot(left, right, dims):
    return lax.dot_general(left, right, (dims, ((), ())), preferred_element_type=F32)


def size_of(arrays):
    return sum(math.prod(a.shape) * jnp.dtype(a.dtype).itemsize for a in arrays)


def local_call(body, out_shape, *args, flops=0, in_specs=None, out_specs=None, scratch=(), limit=20):
    return pl.pallas_call(
        body,
        out_shape=out_shape,
        in_specs=in_specs or [VMEM] * len(args),
        out_specs=out_specs or [VMEM] * len(out_shape),
        scratch_shapes=list(scratch),
        cost_estimate=pl.CostEstimate(
            flops=flops, bytes_accessed=size_of(args) + size_of(out_shape), transcendentals=0
        ),
        compiler_params=pltpu.CompilerParams(vmem_limit_bytes=limit * 2**20),
    )(*args)


def signal(token):
    token[...] = jnp.zeros(token.shape, token.dtype)


def split_index(index, rows, group_rows):
    if group_rows & (group_rows - 1) or rows & (rows - 1):
        return index // group_rows, index % rows
    return index >> (group_rows.bit_length() - 1), index & (rows - 1)


def load_body(groups, group_rows, q_hbm, p_hbm, index_hbm, *refs):
    pieces, (token, index_ref, sems) = refs[:groups], refs[groups:]
    rows = q_hbm.shape[0]
    cols = pieces[0].shape[1]
    g = lax.axis_index("grp")
    index_copy = pltpu.make_async_copy(index_hbm, index_ref, sems.at[2 * groups])
    index_copy.start()
    copies = []
    for r, piece in enumerate(pieces):
        at = pl.ds(pl.multiple_of((g ^ r) * cols, 128), cols)
        for n, source in enumerate((q_hbm, p_hbm)):
            target = piece.at[pl.ds(n * rows, rows)]
            copies.append(pltpu.make_async_copy(source.at[:, at], target, sems.at[2 * r + n]))
            copies[-1].start()
    signal(token)
    index_copy.wait()
    index = jnp.concatenate([index_ref[...], jnp.zeros((TAIL - 3, rows), jnp.int32)], axis=0)
    named_group, named_row = split_index(index, rows, group_rows)
    named_group = named_group.astype(F32).astype(BF16)
    named_row = named_row.astype(F32).astype(BF16)
    for piece in pieces:
        piece[2 * rows :, :rows] = named_group
        piece[2 * rows :, rows : 2 * rows] = named_row
        if cols > 2 * rows:
            piece[2 * rows :, 2 * rows :] = jnp.zeros((TAIL, cols - 2 * rows), BF16)
    for copy in copies:
        copy.wait()


def places_of(piece_ref, rows):
    tail = piece_ref[2 * rows :, : 2 * rows].astype(F32).astype(jnp.int32)
    g = lax.axis_index("grp")
    return [(tail[k : k + 1, :rows] ^ g) * rows + tail[k : k + 1, rows:] for k in range(3)]


def hard_scores_body(groups, *refs):
    pieces, outs = refs[:groups][::-1], refs[groups + 1 :]
    rows = outs[0].shape[1]
    ids = lax.broadcasted_iota(jnp.int32, (groups * rows, rows), 0)
    p_all = jnp.concatenate([piece[rows : 2 * rows] for piece in pieces], axis=0)
    for r in range(groups):
        places = places_of(pieces[r], rows)
        dots = dot(p_all, pieces[r][:rows], ((1,), (1,)))
        for k in range(3):
            hit = jnp.where(ids == places[k], dots, 0.0)
            outs[r][k : k + 1] = jnp.sum(hit, axis=0, keepdims=True)


def hard_grads_body(groups, *refs):
    coefs, pieces, outs = refs[:groups][::-1], refs[groups : 2 * groups][::-1], refs[2 * groups + 1 : 3 * groups + 1]
    token, matrix, matrix_t = refs[3 * groups + 1 :]
    rows = coefs[0].shape[1]
    cols = outs[0].shape[1]
    signal(token)
    ids = lax.broadcasted_iota(jnp.int32, (groups * rows, rows), 0)
    for r in range(groups):
        places = places_of(pieces[r], rows)
        total = jnp.zeros(ids.shape, F32)
        for k in range(3):
            total += jnp.where(ids == places[k], coefs[r][k : k + 1], 0.0)
        mine = slice(r * rows, (r + 1) * rows)
        matrix[:, mine] = total.astype(BF16)
        matrix_t[mine] = total.T.astype(BF16)
    step = min(cols, 256)
    for c in range(0, cols, step):
        at = slice(c, c + step)
        q_all = jnp.concatenate([piece[:rows, at] for piece in pieces], axis=0)
        p_all = jnp.concatenate([piece[rows : 2 * rows, at] for piece in pieces], axis=0)
        grad_q = dot(matrix_t[...], p_all, ((1,), (0,))).astype(BF16)
        grad_p = dot(matrix[...], q_all, ((1,), (0,))).astype(BF16)
        for r in range(groups):
            mine = slice(r * rows, (r + 1) * rows)
            outs[r][:rows, at] = grad_q[mine]
            outs[r][rows:, at] = grad_p[mine]


def pass_body(source, token, out):
    out[...] = source[...]


def choose_body(n1_ref, e3_ref, q_ref, out):
    width = q_ref.shape[1]
    odd = lax.axis_index("blk") % 2 == 1
    out[:, width:] = q_ref[...]

    @pl.when(odd)
    def _():
        out[:, :width] = n1_ref[...]

    @pl.when(jnp.logical_not(odd))
    def _():
        out[:, :width] = e3_ref[...]


def scores_body(q_ref, *refs):
    half = len(refs) // 2
    for block, out in zip(refs[:half], refs[half:]):
        out[...] = dot(block[...], q_ref[...], ((1,), (1,)))


def last_score_body(q_ref, pair_ref, out):
    out[...] = dot(pair_ref[:, : q_ref.shape[1]], q_ref[...], ((1,), (1,)))


def weigh_body(
    groups, *refs
):
    parts, refs = refs[:groups], refs[groups:]
    q_ref, s0_ref, s1_ref, s2_ref, s3_ref, last_ref, w_ref, *refs = refs
    loss_ref, coef_ref, hard_out, swap_ref, term3_ref = refs
    rows, width = q_ref.shape
    w = w_ref[...]
    s3 = INV_TEMP * (s3_ref[...] + dot(last_ref[...], q_ref[...], ((1,), (1,))))
    scores = [INV_TEMP * s0_ref[...], INV_TEMP * s1_ref[...], INV_TEMP * s2_ref[...], s3]
    hard = parts[-1][...]
    for other in parts[-2::-1]:
        hard = hard + other[...]
    hard = INV_TEMP * hard
    largest = jnp.max(hard, axis=0, keepdims=True)
    for block in scores:
        largest = jnp.maximum(largest, jnp.max(block, axis=0, keepdims=True))
    summed = jnp.sum(jnp.exp(hard - largest), axis=0, keepdims=True)
    for block in scores:
        summed = summed + jnp.sum(jnp.exp(block - largest), axis=0, keepdims=True)
    log_total = largest + jnp.log(summed)
    for s, block in enumerate(scores):
        coef = (w * jnp.exp(block - log_total)).astype(BF16)
        coef_ref[:, s * rows : (s + 1) * rows] = coef
        if s in (1, 2):
            swap_ref[:, (s - 1) * rows : s * rows] = coef
    coef3 = coef_ref[:, 3 * rows :]
    for c in range(0, width, CHUNK):
        at = slice(c, c + CHUNK)
        term3_ref[:, at] = dot(coef3, q_ref[:, at], ((1,), (0,))).astype(BF16)
    hard_out[...] = (w * jnp.exp(hard - log_total)).astype(BF16).astype(F32)
    eye = lax.broadcasted_iota(jnp.int32, (rows, rows), 0) == lax.broadcasted_iota(
        jnp.int32, (rows, rows), 1
    )
    loss_ref[...] = log_total - jnp.sum(jnp.where(eye, scores[0], 0.0), axis=0, keepdims=True)


def sums_body(q_ref, pair_ref, coef_ref, swap_ref, sent3, partial1, token):
    signal(token)
    rows, width = q_ref.shape
    odd = lax.axis_index("blk") % 2 == 1
    mine = jnp.where(odd, coef_ref[:, rows : 2 * rows], coef_ref[:, 3 * rows :])
    coef = jnp.concatenate([mine, swap_ref[:, rows:]], axis=1)
    for c in range(0, width, CHUNK):
        at = slice(c, c + CHUNK)
        held = jnp.concatenate([q_ref[:, at], pair_ref[:, width + c : width + c + CHUNK]], axis=0)
        total = dot(coef, held, ((1,), (0,)))
        sent3[:, at] = total.astype(BF16)
        partial1[:, at] = total


def relay_body(partial1, got3_ref, out, done):
    signal(done)
    out[...] = (partial1[...] + got3_ref[...].astype(F32)).astype(BF16)


def base_body(
    q_ref, pair_ref, p_ref, n1_ref, e3_ref, o3_ref, coef_ref, swap_ref, w_ref, own3_ref,
    token, pulled, base, coef_t,
):
    rows, width = q_ref.shape
    w = jnp.broadcast_to(w_ref[...], (rows, rows)).T[:, :1]
    odd = lax.axis_index("blk") % 2 == 1
    blocks = (p_ref, n1_ref, pair_ref, e3_ref, o3_ref)
    for s in range(5):
        k = min(s, 3) * rows
        coef_t[:, s * rows : (s + 1) * rows] = coef_ref[:, k : k + rows].astype(F32).T.astype(BF16)
    coef = [coef_ref[:, :rows], jnp.where(odd, swap_ref[:, :rows], jnp.zeros((rows, rows), BF16))]
    coef = jnp.concatenate(coef, axis=1)
    for c in range(0, width, CHUNK):
        at = slice(c, c + CHUNK)
        held = jnp.concatenate([block[:, at] for block in blocks], axis=0)
        pulled[:, at] = dot(coef_t[...], held, ((1,), (0,))) - w * p_ref[:, at].astype(F32)
        held = jnp.concatenate([q_ref[:, at], pair_ref[:, width + c : width + c + CHUNK]], axis=0)
        own = dot(coef, held, ((1,), (0,))) + own3_ref[:, at].astype(F32)
        base[:, at] = own - w * q_ref[:, at].astype(F32)


def finish_body(groups, pulled, base, own1, *refs):
    backs = refs[:groups][::-1]
    q_out, p_out, q_held, p_held, sems = refs[groups:]
    rows, cols = pulled.shape[0], backs[0].shape[1]
    g = lax.axis_index("grp")
    copies = []
    for r, back in enumerate(backs):
        at = pl.ds(pl.multiple_of((g ^ r) * cols, 128), cols)
        q_held[:, at] = (INV_TEMP * (pulled[:, at] + back[:rows].astype(F32))).astype(BF16)
        copies.append(pltpu.make_async_copy(q_held.at[:, at], q_out.at[:, at], sems.at[2 * r]))
        copies[-1].start()
        total = base[:, at] + back[rows:].astype(F32) + own1[:, at].astype(F32)
        p_held[:, at] = (INV_TEMP * total).astype(BF16)
        copies.append(pltpu.make_async_copy(p_held.at[:, at], p_out.at[:, at], sems.at[2 * r + 1]))
        copies[-1].start()
    for copy in copies:
        copy.wait()


def per_device(queries, passages, hard_index, weights):
    rows, width = queries.shape
    groups = lax.axis_size("grp")
    loop = lax.axis_size("blk")
    cols = width // groups

    def shift(array, by, which=(0, 1)):
        pairs = [(i, (i + by) % loop) for i in range(loop) if i % 2 in which]
        return lax.ppermute(array, "blk", pairs)

    def swap(array):
        return lax.ppermute(array, "blk", [(i, i ^ 1) for i in range(loop)])

    def over_groups(array, r):
        return lax.ppermute(array, "grp", [(i, i ^ r) for i in range(groups)])

    def exchange(arrays):
        out = list(arrays)
        for r in reversed(range(1, groups)):
            out[r] = over_groups(arrays[r], r)
        return out

    def like(*shape, dtype=BF16):
        return jax.ShapeDtypeStruct(shape, dtype)

    block, block32 = like(rows, width), like(rows, width, dtype=F32)
    square, triple = like(rows, rows, dtype=F32), like(3, rows, dtype=F32)
    piece, back = like(2 * rows + TAIL, cols), like(2 * rows, cols)

    next1 = shift(passages, -1)

    *pieces, token = local_call(
        functools.partial(load_body, groups, loop * rows), [piece] * groups + [TOKEN],
        queries, passages, hard_index.T, in_specs=[HBM, HBM, HBM],
        scratch=[pltpu.VMEM((3, rows), jnp.int32), pltpu.SemaphoreType.DMA((2 * groups + 1,))],
        limit=51,
    )
    pieces = exchange(pieces)

    (later_p,) = local_call(pass_body, [block], passages, token)
    next3_even = shift(later_p, -3, (1,))
    (next1,) = local_call(pass_body, [block], next1, token, flops=LONG)
    next3_odd = shift(next1, -2, (1,))
    pair = swap(
        local_call(choose_body, [like(rows, 2 * width)], next1, next3_even, queries, flops=LONG)[0]
    )

    s0, s1, s3 = local_call(scores_body, [square] * 3, queries, passages, next1, next3_even)
    parts = local_call(
        functools.partial(hard_scores_body, groups), [triple] * groups, *pieces[::-1], s0, flops=LONG
    )
    (s2,) = local_call(last_score_body, [square], queries, pair)
    parts = exchange(parts)
    loss_rows, coef, hard_coef, to_core, term3 = local_call(
        functools.partial(weigh_body, groups),
        [like(1, rows, dtype=F32), like(rows, 4 * rows), triple, like(rows, 2 * rows), block],
        *parts[::-1], queries, s0, s1, s2, s3, next3_odd, weights[None, :],
    )

    got3 = shift(term3, 2, (1,))
    from_core = swap(to_core)
    sent3, partial1, token = local_call(
        sums_body, [block, block32, TOKEN], queries, pair, coef, from_core
    )
    own3 = shift(sent3, 3, (0,))

    hard_coefs = exchange([hard_coef] * groups)
    square_all = pltpu.VMEM((groups * rows, groups * rows), BF16)
    *backs, token = local_call(
        functools.partial(hard_grads_body, groups), [back] * groups + [TOKEN],
        *hard_coefs[::-1], *pieces[::-1], token, scratch=[square_all, square_all],
    )
    backs = exchange(backs)

    sent1, token = local_call(relay_body, [block, TOKEN], partial1, got3, flops=SOME)
    own1 = shift(sent1, 1, (1,))

    pulled, base = local_call(
        base_body, [block32, block32],
        queries, pair, passages, next1, next3_even, next3_odd, coef, from_core,
        weights[None, :], own3, token, flops=LONG, scratch=[pltpu.VMEM((rows, 5 * rows), BF16)],
    )
    grad_queries, grad_passages = local_call(
        functools.partial(finish_body, groups), [block, block], pulled, base, own1, *backs[::-1],
        out_specs=[HBM, HBM],
        scratch=[
            pltpu.VMEM((rows, width), BF16),
            pltpu.VMEM((rows, width), BF16),
            pltpu.SemaphoreType.DMA((2 * groups,)),
        ],
    )
    return loss_rows.reshape(rows), grad_queries, grad_passages


def solution(mesh):
    rows = P(("grp", "blk"))
    matrix = P(("grp", "blk"), None)
    return jax.shard_map(
        per_device,
        mesh=mesh,
        in_specs=(matrix, matrix, matrix, rows),
        out_specs=(rows, matrix, matrix),
        check_vma=False,
    )
```

```python
import functools
import math

import jax
import jax.numpy as jnp
from jax import lax
from jax.experimental import pallas as pl
from jax.experimental.pallas import tpu as pltpu
from jax.sharding import PartitionSpec as P

INV_TEMP = 50.0
BF16 = jnp.bfloat16
F32 = jnp.float32
CHUNK = 512
TAIL = 16
LONG, SOME = 5 * 10**10, 16 * 10**9
VMEM = pl.BlockSpec(memory_space=pltpu.VMEM)
HBM = pl.BlockSpec(memory_space=pltpu.HBM)
TOKEN = jax.ShapeDtypeStruct((8, 128), F32)


def dot(left, right, dims):
    return lax.dot_general(left, right, (dims, ((), ())), preferred_element_type=F32)


def size_of(arrays):
    return sum(math.prod(a.shape) * jnp.dtype(a.dtype).itemsize for a in arrays)


def local_call(body, out_shape, *args, flops=0, in_specs=None, out_specs=None, scratch=(), limit=20):
    return pl.pallas_call(
        body,
        out_shape=out_shape,
        in_specs=in_specs or [VMEM] * len(args),
        out_specs=out_specs or [VMEM] * len(out_shape),
        scratch_shapes=list(scratch),
        cost_estimate=pl.CostEstimate(
            flops=flops, bytes_accessed=size_of(args) + size_of(out_shape), transcendentals=0
        ),
        compiler_params=pltpu.CompilerParams(vmem_limit_bytes=limit * 2**20),
    )(*args)


def signal(token):
    token[...] = jnp.zeros(token.shape, token.dtype)


def split_index(index, rows, group_rows):
    if group_rows & (group_rows - 1) or rows & (rows - 1):
        return index // group_rows, index % rows
    return index >> (group_rows.bit_length() - 1), index & (rows - 1)


def load_body(groups, group_rows, q_hbm, p_hbm, index_hbm, *refs):
    pieces, (token, index_ref, sems) = refs[:groups], refs[groups:]
    rows = q_hbm.shape[0]
    cols = pieces[0].shape[1]
    g = lax.axis_index("grp")
    index_copy = pltpu.make_async_copy(index_hbm, index_ref, sems.at[2 * groups])
    index_copy.start()
    copies = []
    for r, piece in enumerate(pieces):
        at = pl.ds(pl.multiple_of((g ^ r) * cols, 128), cols)
        for n, source in enumerate((q_hbm, p_hbm)):
            target = piece.at[pl.ds(n * rows, rows)]
            copies.append(pltpu.make_async_copy(source.at[:, at], target, sems.at[2 * r + n]))
            copies[-1].start()
    signal(token)
    index_copy.wait()
    index = jnp.concatenate([index_ref[...], jnp.zeros((TAIL - 3, rows), jnp.int32)], axis=0)
    named_group, named_row = split_index(index, rows, group_rows)
    named_group = named_group.astype(F32).astype(BF16)
    named_row = named_row.astype(F32).astype(BF16)
    for piece in pieces:
        piece[2 * rows :, :rows] = named_group
        piece[2 * rows :, rows : 2 * rows] = named_row
        if cols > 2 * rows:
            piece[2 * rows :, 2 * rows :] = jnp.zeros((TAIL, cols - 2 * rows), BF16)
    for copy in copies:
        copy.wait()


def places_of(piece_ref, rows):
    tail = piece_ref[2 * rows :, : 2 * rows].astype(F32).astype(jnp.int32)
    g = lax.axis_index("grp")
    return [(tail[k : k + 1, :rows] ^ g) * rows + tail[k : k + 1, rows:] for k in range(3)]


def hard_scores_body(groups, *refs):
    pieces, outs = refs[:groups][::-1], refs[groups + 1 :]
    rows = outs[0].shape[1]
    ids = lax.broadcasted_iota(jnp.int32, (groups * rows, rows), 0)
    p_all = jnp.concatenate([piece[rows : 2 * rows] for piece in pieces], axis=0)
    for r in range(groups):
        places = places_of(pieces[r], rows)
        dots = dot(p_all, pieces[r][:rows], ((1,), (1,)))
        for k in range(3):
            hit = jnp.where(ids == places[k], dots, 0.0)
            outs[r][k : k + 1] = jnp.sum(hit, axis=0, keepdims=True)


def hard_grads_body(groups, *refs):
    coefs, pieces, outs = refs[:groups][::-1], refs[groups : 2 * groups][::-1], refs[2 * groups + 1 : 3 * groups + 1]
    token, matrix, matrix_t = refs[3 * groups + 1 :]
    rows = coefs[0].shape[1]
    cols = outs[0].shape[1]
    signal(token)
    ids = lax.broadcasted_iota(jnp.int32, (groups * rows, rows), 0)
    for r in range(groups):
        places = places_of(pieces[r], rows)
        total = jnp.zeros(ids.shape, F32)
        for k in range(3):
            total += jnp.where(ids == places[k], coefs[r][k : k + 1], 0.0)
        mine = slice(r * rows, (r + 1) * rows)
        matrix[:, mine] = total.astype(BF16)
        matrix_t[mine] = total.T.astype(BF16)
    step = min(cols, 256)
    for c in range(0, cols, step):
        at = slice(c, c + step)
        q_all = jnp.concatenate([piece[:rows, at] for piece in pieces], axis=0)
        p_all = jnp.concatenate([piece[rows : 2 * rows, at] for piece in pieces], axis=0)
        grad_q = dot(matrix_t[...], p_all, ((1,), (0,))).astype(BF16)
        grad_p = dot(matrix[...], q_all, ((1,), (0,))).astype(BF16)
        for r in range(groups):
            mine = slice(r * rows, (r + 1) * rows)
            outs[r][:rows, at] = grad_q[mine]
            outs[r][rows:, at] = grad_p[mine]


def pass_body(source, token, *outs):
    width = outs[0].shape[1]
    for n, out in enumerate(outs):
        out[...] = source[:, n * width : (n + 1) * width]


def choose_body(n1_a, n1_b, e3_ref, q_ref, out):
    width = q_ref.shape[1]
    odd = lax.axis_index("blk") % 2 == 1
    out[:, width:] = q_ref[...]

    @pl.when(odd)
    def _():
        out[:, : width // 2] = n1_a[...]
        out[:, width // 2 : width] = n1_b[...]

    @pl.when(jnp.logical_not(odd))
    def _():
        out[:, :width] = e3_ref[...]


def scores_body(q_ref, *refs):
    half = len(refs) // 2
    for block, out in zip(refs[:half], refs[half:]):
        out[...] = dot(block[...], q_ref[...], ((1,), (1,)))


def last_score_body(q_ref, pair_ref, out):
    out[...] = dot(pair_ref[:, : q_ref.shape[1]], q_ref[...], ((1,), (1,)))


def weigh_body(
    groups, *refs
):
    parts, refs = refs[:groups], refs[groups:]
    q_ref, s0_ref, s1_ref, s2_ref, s3_ref, last_a, last_b, w_ref, *refs = refs
    loss_ref, coef_ref, hard_out, swap_ref, term3_ref = refs
    rows, width = q_ref.shape
    w = w_ref[...]
    half = width // 2
    last = dot(last_a[...], q_ref[:, :half], ((1,), (1,)))
    s3 = INV_TEMP * (s3_ref[...] + last + dot(last_b[...], q_ref[:, half:], ((1,), (1,))))
    scores = [INV_TEMP * s0_ref[...], INV_TEMP * s1_ref[...], INV_TEMP * s2_ref[...], s3]
    hard = parts[-1][...]
    for other in parts[-2::-1]:
        hard = hard + other[...]
    hard = INV_TEMP * hard
    largest = jnp.max(hard, axis=0, keepdims=True)
    for block in scores:
        largest = jnp.maximum(largest, jnp.max(block, axis=0, keepdims=True))
    summed = jnp.sum(jnp.exp(hard - largest), axis=0, keepdims=True)
    for block in scores:
        summed = summed + jnp.sum(jnp.exp(block - largest), axis=0, keepdims=True)
    log_total = largest + jnp.log(summed)
    for s, block in enumerate(scores):
        coef = (w * jnp.exp(block - log_total)).astype(BF16)
        coef_ref[:, s * rows : (s + 1) * rows] = coef
        if s in (1, 2):
            swap_ref[:, (s - 1) * rows : s * rows] = coef
    coef3 = coef_ref[:, 3 * rows :]
    for c in range(0, width, CHUNK):
        at = slice(c, c + CHUNK)
        term3_ref[:, at] = dot(coef3, q_ref[:, at], ((1,), (0,))).astype(BF16)
    hard_out[...] = (w * jnp.exp(hard - log_total)).astype(BF16).astype(F32)
    eye = lax.broadcasted_iota(jnp.int32, (rows, rows), 0) == lax.broadcasted_iota(
        jnp.int32, (rows, rows), 1
    )
    loss_ref[...] = log_total - jnp.sum(jnp.where(eye, scores[0], 0.0), axis=0, keepdims=True)


def sums_body(q_ref, pair_ref, coef_ref, swap_ref, sent3, partial1, token):
    signal(token)
    rows, width = q_ref.shape
    odd = lax.axis_index("blk") % 2 == 1
    mine = jnp.where(odd, coef_ref[:, rows : 2 * rows], coef_ref[:, 3 * rows :])
    coef = jnp.concatenate([mine, swap_ref[:, rows:]], axis=1)
    for c in range(0, width, CHUNK):
        at = slice(c, c + CHUNK)
        held = jnp.concatenate([q_ref[:, at], pair_ref[:, width + c : width + c + CHUNK]], axis=0)
        total = dot(coef, held, ((1,), (0,)))
        sent3[:, at] = total.astype(BF16)
        partial1[:, at] = total


def relay_body(partial1, got3_ref, out, done):
    signal(done)
    out[...] = (partial1[...] + got3_ref[...].astype(F32)).astype(BF16)


def base_body(
    q_ref, pair_ref, p_ref, n1_ref, e3_ref, o3_a, o3_b, coef_ref, swap_ref, w_ref, own3_ref,
    token, pulled, base, coef_t,
):
    rows, width = q_ref.shape
    w = jnp.broadcast_to(w_ref[...], (rows, rows)).T[:, :1]
    odd = lax.axis_index("blk") % 2 == 1
    blocks = (p_ref, n1_ref, pair_ref, e3_ref)
    for s in range(5):
        k = min(s, 3) * rows
        coef_t[:, s * rows : (s + 1) * rows] = coef_ref[:, k : k + rows].astype(F32).T.astype(BF16)
    coef = [coef_ref[:, :rows], jnp.where(odd, swap_ref[:, :rows], jnp.zeros((rows, rows), BF16))]
    coef = jnp.concatenate(coef, axis=1)
    for c in range(0, width, CHUNK):
        at = slice(c, c + CHUNK)
        late = o3_a[:, at] if c < width // 2 else o3_b[:, c - width // 2 : c - width // 2 + CHUNK]
        held = jnp.concatenate([block[:, at] for block in blocks] + [late], axis=0)
        pulled[:, at] = dot(coef_t[...], held, ((1,), (0,))) - w * p_ref[:, at].astype(F32)
        held = jnp.concatenate([q_ref[:, at], pair_ref[:, width + c : width + c + CHUNK]], axis=0)
        own = dot(coef, held, ((1,), (0,))) + own3_ref[:, at].astype(F32)
        base[:, at] = own - w * q_ref[:, at].astype(F32)


def finish_body(groups, pulled, base, own1, *refs):
    backs = refs[:groups][::-1]
    q_out, p_out, q_held, p_held, sems = refs[groups:]
    rows, cols = pulled.shape[0], backs[0].shape[1]
    g = lax.axis_index("grp")
    copies = []
    for r, back in enumerate(backs):
        at = pl.ds(pl.multiple_of((g ^ r) * cols, 128), cols)
        q_held[:, at] = (INV_TEMP * (pulled[:, at] + back[:rows].astype(F32))).astype(BF16)
        copies.append(pltpu.make_async_copy(q_held.at[:, at], q_out.at[:, at], sems.at[2 * r]))
        copies[-1].start()
        total = base[:, at] + back[rows:].astype(F32) + own1[:, at].astype(F32)
        p_held[:, at] = (INV_TEMP * total).astype(BF16)
        copies.append(pltpu.make_async_copy(p_held.at[:, at], p_out.at[:, at], sems.at[2 * r + 1]))
        copies[-1].start()
    for copy in copies:
        copy.wait()


def per_device(queries, passages, hard_index, weights):
    rows, width = queries.shape
    groups = lax.axis_size("grp")
    loop = lax.axis_size("blk")
    cols = width // groups

    def shift(array, by, which=(0, 1)):
        pairs = [(i, (i + by) % loop) for i in range(loop) if i % 2 in which]
        return lax.ppermute(array, "blk", pairs)

    def swap(array):
        return lax.ppermute(array, "blk", [(i, i ^ 1) for i in range(loop)])

    def over_groups(array, r):
        return lax.ppermute(array, "grp", [(i, i ^ r) for i in range(groups)])

    def exchange(arrays):
        out = list(arrays)
        for r in reversed(range(1, groups)):
            out[r] = over_groups(arrays[r], r)
        return out

    def like(*shape, dtype=BF16):
        return jax.ShapeDtypeStruct(shape, dtype)

    half = like(rows, width // 2)
    block, block32 = like(rows, width), like(rows, width, dtype=F32)
    square, triple = like(rows, rows, dtype=F32), like(3, rows, dtype=F32)
    piece, back = like(2 * rows + TAIL, cols), like(2 * rows, cols)

    next1 = shift(passages, -1)

    *pieces, token = local_call(
        functools.partial(load_body, groups, loop * rows), [piece] * groups + [TOKEN],
        queries, passages, hard_index.T, in_specs=[HBM, HBM, HBM],
        scratch=[pltpu.VMEM((3, rows), jnp.int32), pltpu.SemaphoreType.DMA((2 * groups + 1,))],
        limit=51,
    )
    pieces = exchange(pieces)

    (later_p,) = local_call(pass_body, [block], passages, token)
    next3_even = shift(later_p, -3, (1,))
    halves = local_call(pass_body, [half] * 2, next1, token, flops=LONG)
    next3_odd = [shift(part, -2, (1,)) for part in halves]
    pair = swap(
        local_call(choose_body, [like(rows, 2 * width)], *halves, next3_even, queries, flops=LONG)[0]
    )

    s0, s1, s3 = local_call(scores_body, [square] * 3, queries, passages, next1, next3_even)
    parts = local_call(
        functools.partial(hard_scores_body, groups), [triple] * groups, *pieces[::-1], s0, flops=LONG
    )
    (s2,) = local_call(last_score_body, [square], queries, pair)
    parts = exchange(parts)
    loss_rows, coef, hard_coef, to_core, term3 = local_call(
        functools.partial(weigh_body, groups),
        [like(1, rows, dtype=F32), like(rows, 4 * rows), triple, like(rows, 2 * rows), block],
        *parts[::-1], queries, s0, s1, s2, s3, *next3_odd, weights[None, :],
    )

    got3 = shift(term3, 2, (1,))
    from_core = swap(to_core)
    sent3, partial1, token = local_call(
        sums_body, [block, block32, TOKEN], queries, pair, coef, from_core
    )
    own3 = shift(sent3, 3, (0,))

    hard_coefs = exchange([hard_coef] * groups)
    square_all = pltpu.VMEM((groups * rows, groups * rows), BF16)
    *backs, token = local_call(
        functools.partial(hard_grads_body, groups), [back] * groups + [TOKEN],
        *hard_coefs[::-1], *pieces[::-1], token, scratch=[square_all, square_all],
    )
    backs = exchange(backs)

    sent1, token = local_call(relay_body, [block, TOKEN], partial1, got3, flops=SOME)
    own1 = shift(sent1, 1, (1,))

    pulled, base = local_call(
        base_body, [block32, block32],
        queries, pair, passages, next1, next3_even, *next3_odd, coef, from_core,
        weights[None, :], own3, token, flops=LONG, scratch=[pltpu.VMEM((rows, 5 * rows), BF16)],
    )
    grad_queries, grad_passages = local_call(
        functools.partial(finish_body, groups), [block, block], pulled, base, own1, *backs[::-1],
        out_specs=[HBM, HBM],
        scratch=[
            pltpu.VMEM((rows, width), BF16),
            pltpu.VMEM((rows, width), BF16),
            pltpu.SemaphoreType.DMA((2 * groups,)),
        ],
    )
    return loss_rows.reshape(rows), grad_queries, grad_passages


def solution(mesh):
    rows = P(("grp", "blk"))
    matrix = P(("grp", "blk"), None)
    return jax.shard_map(
        per_device,
        mesh=mesh,
        in_specs=(matrix, matrix, matrix, rows),
        out_specs=(rows, matrix, matrix),
        check_vma=False,
    )
```

```python
import functools
import math

import jax
import jax.numpy as jnp
from jax import lax
from jax.experimental import pallas as pl
from jax.experimental.pallas import tpu as pltpu
from jax.sharding import PartitionSpec as P

INV_TEMP = 50.0
BF16 = jnp.bfloat16
F32 = jnp.float32
CHUNK = 512
TAIL = 16
LONG, SOME = 5 * 10**10, 16 * 10**9
VMEM = pl.BlockSpec(memory_space=pltpu.VMEM)
HBM = pl.BlockSpec(memory_space=pltpu.HBM)
TOKEN = jax.ShapeDtypeStruct((8, 128), F32)


def dot(left, right, dims):
    return lax.dot_general(left, right, (dims, ((), ())), preferred_element_type=F32)


def size_of(arrays):
    return sum(math.prod(a.shape) * jnp.dtype(a.dtype).itemsize for a in arrays)


def local_call(body, out_shape, *args, flops=0, in_specs=None, out_specs=None, scratch=(), limit=20):
    return pl.pallas_call(
        body,
        out_shape=out_shape,
        in_specs=in_specs or [VMEM] * len(args),
        out_specs=out_specs or [VMEM] * len(out_shape),
        scratch_shapes=list(scratch),
        cost_estimate=pl.CostEstimate(
            flops=flops, bytes_accessed=size_of(args) + size_of(out_shape), transcendentals=0
        ),
        compiler_params=pltpu.CompilerParams(vmem_limit_bytes=limit * 2**20),
    )(*args)


def signal(token):
    token[...] = jnp.zeros(token.shape, token.dtype)


def split_index(index, rows, group_rows):
    if group_rows & (group_rows - 1) or rows & (rows - 1):
        return index // group_rows, index % rows
    return index >> (group_rows.bit_length() - 1), index & (rows - 1)


def load_body(groups, group_rows, q_hbm, p_hbm, index_hbm, *refs):
    pieces, (token, index_ref, sems) = refs[:groups], refs[groups:]
    rows = q_hbm.shape[0]
    cols = pieces[0].shape[1]
    g = lax.axis_index("grp")
    index_copy = pltpu.make_async_copy(index_hbm, index_ref, sems.at[2 * groups])
    index_copy.start()
    copies = []
    for r, piece in enumerate(pieces):
        at = pl.ds(pl.multiple_of((g ^ r) * cols, 128), cols)
        for n, source in enumerate((q_hbm, p_hbm)):
            target = piece.at[pl.ds(n * rows, rows)]
            copies.append(pltpu.make_async_copy(source.at[:, at], target, sems.at[2 * r + n]))
            copies[-1].start()
    signal(token)
    index_copy.wait()
    index = jnp.concatenate([index_ref[...], jnp.zeros((TAIL - 3, rows), jnp.int32)], axis=0)
    named_group, named_row = split_index(index, rows, group_rows)
    named_group = named_group.astype(F32).astype(BF16)
    named_row = named_row.astype(F32).astype(BF16)
    for piece in pieces:
        piece[2 * rows :, :rows] = named_group
        piece[2 * rows :, rows : 2 * rows] = named_row
        if cols > 2 * rows:
            piece[2 * rows :, 2 * rows :] = jnp.zeros((TAIL, cols - 2 * rows), BF16)
    for copy in copies:
        copy.wait()


def places_of(piece_ref, rows):
    tail = piece_ref[2 * rows :, : 2 * rows].astype(F32).astype(jnp.int32)
    g = lax.axis_index("grp")
    return [(tail[k : k + 1, :rows] ^ g) * rows + tail[k : k + 1, rows:] for k in range(3)]


def hard_scores_body(groups, *refs):
    pieces, outs = refs[:groups][::-1], refs[groups + 1 :]
    rows = outs[0].shape[1]
    ids = lax.broadcasted_iota(jnp.int32, (rows, rows), 0)
    for r in range(groups):
        others = [other for other in range(groups) if other != r]
        places = places_of(pieces[r], rows)
        held = jnp.concatenate([pieces[other][rows : 2 * rows] for other in others], axis=0)
        dots = dot(held, pieces[r][:rows], ((1,), (1,)))
        sums = [jnp.zeros((1, rows), F32) for _ in places]
        for n, other in enumerate(others):
            block = dots[n * rows : (n + 1) * rows]
            for k, place in enumerate(places):
                hit = jnp.where(ids == place - other * rows, block, 0.0)
                sums[k] += jnp.sum(hit, axis=0, keepdims=True)
        outs[r][...] = jnp.concatenate(sums, axis=0)


def hard_grads_body(groups, *refs):
    coefs, pieces, outs = refs[:groups][::-1], refs[groups : 2 * groups][::-1], refs[2 * groups + 1 : 3 * groups + 1]
    token, matrix, matrix_t = refs[3 * groups + 1 :]
    rows = coefs[0].shape[1]
    cols = outs[0].shape[1]
    signal(token)
    ids = lax.broadcasted_iota(jnp.int32, (groups * rows, rows), 0)
    for r in range(groups):
        places = places_of(pieces[r], rows)
        total = jnp.zeros(ids.shape, F32)
        for k in range(3):
            total += jnp.where(ids == places[k], coefs[r][k : k + 1], 0.0)
        mine = slice(r * rows, (r + 1) * rows)
        matrix[:, mine] = total.astype(BF16)
        matrix_t[mine] = total.T.astype(BF16)
    step = min(cols, 256)
    for c in range(0, cols, step):
        at = slice(c, c + step)
        q_all = jnp.concatenate([piece[:rows, at] for piece in pieces], axis=0)
        p_all = jnp.concatenate([piece[rows : 2 * rows, at] for piece in pieces], axis=0)
        grad_q = dot(matrix_t[...], p_all, ((1,), (0,))).astype(BF16)
        grad_p = dot(matrix[...], q_all, ((1,), (0,))).astype(BF16)
        for r in range(groups):
            mine = slice(r * rows, (r + 1) * rows)
            outs[r][:rows, at] = grad_q[mine]
            outs[r][rows:, at] = grad_p[mine]


def pass_body(source, token, out):
    out[...] = source[...]


def choose_body(n1_ref, e3_ref, q_ref, out):
    width = q_ref.shape[1]
    odd = lax.axis_index("blk") % 2 == 1
    out[:, width:] = q_ref[...]

    @pl.when(odd)
    def _():
        out[:, :width] = n1_ref[...]

    @pl.when(jnp.logical_not(odd))
    def _():
        out[:, :width] = e3_ref[...]


def scores_body(q_ref, *refs):
    half = len(refs) // 2
    for block, out in zip(refs[:half], refs[half:]):
        out[...] = dot(block[...], q_ref[...], ((1,), (1,)))


def last_score_body(q_ref, pair_ref, out):
    out[...] = dot(pair_ref[:, : q_ref.shape[1]], q_ref[...], ((1,), (1,)))


def weigh_body(
    groups, *refs
):
    parts, refs = refs[:groups], refs[groups:]
    q_ref, s0_ref, s1_ref, s2_ref, s3_ref, last_ref, w_ref, *refs = refs
    loss_ref, coef_ref, hard_out, swap_ref, term3_ref = refs
    rows, width = q_ref.shape
    w = w_ref[...]
    s3 = INV_TEMP * (s3_ref[...] + dot(last_ref[...], q_ref[...], ((1,), (1,))))
    scores = [INV_TEMP * s0_ref[...], INV_TEMP * s1_ref[...], INV_TEMP * s2_ref[...], s3]
    hard = parts[-1][...]
    for other in parts[-2::-1]:
        hard = hard + other[...]
    hard = INV_TEMP * hard
    largest = jnp.max(hard, axis=0, keepdims=True)
    for block in scores:
        largest = jnp.maximum(largest, jnp.max(block, axis=0, keepdims=True))
    summed = jnp.sum(jnp.exp(hard - largest), axis=0, keepdims=True)
    for block in scores:
        summed = summed + jnp.sum(jnp.exp(block - largest), axis=0, keepdims=True)
    log_total = largest + jnp.log(summed)
    for s, block in enumerate(scores):
        coef = (w * jnp.exp(block - log_total)).astype(BF16)
        coef_ref[:, s * rows : (s + 1) * rows] = coef
        if s in (1, 2):
            swap_ref[:, (s - 1) * rows : s * rows] = coef
    coef3 = coef_ref[:, 3 * rows :]
    for c in range(0, width, CHUNK):
        at = slice(c, c + CHUNK)
        term3_ref[:, at] = dot(coef3, q_ref[:, at], ((1,), (0,))).astype(BF16)
    hard_out[...] = (w * jnp.exp(hard - log_total)).astype(BF16).astype(F32)
    eye = lax.broadcasted_iota(jnp.int32, (rows, rows), 0) == lax.broadcasted_iota(
        jnp.int32, (rows, rows), 1
    )
    loss_ref[...] = log_total - jnp.sum(jnp.where(eye, scores[0], 0.0), axis=0, keepdims=True)


def sums_body(q_ref, pair_ref, coef_ref, swap_ref, sent3, partial1, token):
    signal(token)
    rows, width = q_ref.shape
    odd = lax.axis_index("blk") % 2 == 1
    mine = jnp.where(odd, coef_ref[:, rows : 2 * rows], coef_ref[:, 3 * rows :])
    coef = jnp.concatenate([mine, swap_ref[:, rows:]], axis=1)
    for c in range(0, width, CHUNK):
        at = slice(c, c + CHUNK)
        held = jnp.concatenate([q_ref[:, at], pair_ref[:, width + c : width + c + CHUNK]], axis=0)
        total = dot(coef, held, ((1,), (0,)))
        sent3[:, at] = total.astype(BF16)
        partial1[:, at] = total


def relay_body(partial1, got3_ref, out, done):
    signal(done)
    out[...] = (partial1[...] + got3_ref[...].astype(F32)).astype(BF16)


def base_body(
    q_ref, pair_ref, p_ref, n1_ref, e3_ref, o3_ref, coef_ref, swap_ref, w_ref, own3_ref,
    token, pulled, base, coef_t,
):
    rows, width = q_ref.shape
    w = jnp.broadcast_to(w_ref[...], (rows, rows)).T[:, :1]
    odd = lax.axis_index("blk") % 2 == 1
    blocks = (p_ref, n1_ref, pair_ref, e3_ref, o3_ref)
    for s in range(5):
        k = min(s, 3) * rows
        coef_t[:, s * rows : (s + 1) * rows] = coef_ref[:, k : k + rows].astype(F32).T.astype(BF16)
    coef = [coef_ref[:, :rows], jnp.where(odd, swap_ref[:, :rows], jnp.zeros((rows, rows), BF16))]
    coef = jnp.concatenate(coef, axis=1)
    for c in range(0, width, CHUNK):
        at = slice(c, c + CHUNK)
        held = jnp.concatenate([block[:, at] for block in blocks], axis=0)
        pulled[:, at] = dot(coef_t[...], held, ((1,), (0,))) - w * p_ref[:, at].astype(F32)
        held = jnp.concatenate([q_ref[:, at], pair_ref[:, width + c : width + c + CHUNK]], axis=0)
        own = dot(coef, held, ((1,), (0,))) + own3_ref[:, at].astype(F32)
        base[:, at] = own - w * q_ref[:, at].astype(F32)


def gather_body(groups, pulled, base, *refs):
    backs, (out, almost, held, sems) = refs[:groups][::-1], refs[groups:]
    rows, cols = pulled.shape[0], backs[0].shape[1]
    g = lax.axis_index("grp")
    copies = []
    for r, back in enumerate(backs):
        at = pl.ds(pl.multiple_of((g ^ r) * cols, 128), cols)
        held[:, at] = (INV_TEMP * (pulled[:, at] + back[:rows].astype(F32))).astype(BF16)
        copies.append(pltpu.make_async_copy(held.at[:, at], out.at[:, at], sems.at[r]))
        copies[-1].start()
        almost[:, at] = base[:, at] + back[rows:].astype(F32)
    for copy in copies:
        copy.wait()


def finish_body(almost, own1, out, held, sems):
    width = almost.shape[1]
    copies = []
    for n, c in enumerate(range(0, width, CHUNK)):
        at = slice(c, c + CHUNK)
        held[:, at] = (INV_TEMP * (almost[:, at] + own1[:, at].astype(F32))).astype(BF16)
        copies.append(pltpu.make_async_copy(held.at[:, at], out.at[:, at], sems.at[n]))
        copies[-1].start()
    for copy in copies:
        copy.wait()


def per_device(queries, passages, hard_index, weights):
    rows, width = queries.shape
    groups = lax.axis_size("grp")
    loop = lax.axis_size("blk")
    cols = width // groups

    def shift(array, by, which=(0, 1)):
        pairs = [(i, (i + by) % loop) for i in range(loop) if i % 2 in which]
        return lax.ppermute(array, "blk", pairs)

    def swap(array):
        return lax.ppermute(array, "blk", [(i, i ^ 1) for i in range(loop)])

    def over_groups(array, r):
        return lax.ppermute(array, "grp", [(i, i ^ r) for i in range(groups)])

    def exchange(arrays):
        out = list(arrays)
        for r in reversed(range(1, groups)):
            out[r] = over_groups(arrays[r], r)
        return out

    def like(*shape, dtype=BF16):
        return jax.ShapeDtypeStruct(shape, dtype)

    block, block32 = like(rows, width), like(rows, width, dtype=F32)
    square, triple = like(rows, rows, dtype=F32), like(3, rows, dtype=F32)
    piece, back = like(2 * rows + TAIL, cols), like(2 * rows, cols)

    next1 = shift(passages, -1)

    *pieces, token = local_call(
        functools.partial(load_body, groups, loop * rows), [piece] * groups + [TOKEN],
        queries, passages, hard_index.T, in_specs=[HBM, HBM, HBM],
        scratch=[pltpu.VMEM((3, rows), jnp.int32), pltpu.SemaphoreType.DMA((2 * groups + 1,))],
        limit=51,
    )
    pieces = exchange(pieces)

    (later_p,) = local_call(pass_body, [block], passages, token)
    next3_even = shift(later_p, -3, (1,))
    (next1,) = local_call(pass_body, [block], next1, token, flops=LONG)
    next3_odd = shift(next1, -2, (1,))
    pair = swap(
        local_call(choose_body, [like(rows, 2 * width)], next1, next3_even, queries, flops=LONG)[0]
    )

    s0, s1, s3 = local_call(scores_body, [square] * 3, queries, passages, next1, next3_even)
    parts = local_call(
        functools.partial(hard_scores_body, groups), [triple] * groups, *pieces[::-1], s0, flops=LONG
    )
    (s2,) = local_call(last_score_body, [square], queries, pair)
    parts = exchange(parts)
    loss_rows, coef, hard_coef, to_core, term3 = local_call(
        functools.partial(weigh_body, groups),
        [like(1, rows, dtype=F32), like(rows, 4 * rows), triple, like(rows, 2 * rows), block],
        *parts[::-1], queries, s0, s1, s2, s3, next3_odd, weights[None, :],
    )

    got3 = shift(term3, 2, (1,))
    from_core = swap(to_core)
    sent3, partial1, token = local_call(
        sums_body, [block, block32, TOKEN], queries, pair, coef, from_core
    )
    own3 = shift(sent3, 3, (0,))

    hard_coefs = exchange([hard_coef] * groups)
    square_all = pltpu.VMEM((groups * rows, groups * rows), BF16)
    *backs, token = local_call(
        functools.partial(hard_grads_body, groups), [back] * groups + [TOKEN],
        *hard_coefs[::-1], *pieces[::-1], token, scratch=[square_all, square_all],
    )
    backs = exchange(backs)

    sent1, token = local_call(relay_body, [block, TOKEN], partial1, got3, flops=SOME)
    own1 = shift(sent1, 1, (1,))

    pulled, base = local_call(
        base_body, [block32, block32],
        queries, pair, passages, next1, next3_even, next3_odd, coef, from_core,
        weights[None, :], own3, token, flops=LONG, scratch=[pltpu.VMEM((rows, 5 * rows), BF16)],
    )
    held = pltpu.VMEM((rows, width), BF16)
    grad_queries, almost = local_call(
        functools.partial(gather_body, groups), [block, block32], pulled, base, *backs[::-1],
        out_specs=[HBM, VMEM], scratch=[held, pltpu.SemaphoreType.DMA((groups,))],
    )
    (grad_passages,) = local_call(
        finish_body, [block], almost, own1, out_specs=[HBM],
        scratch=[held, pltpu.SemaphoreType.DMA((width // CHUNK,))],
    )
    return loss_rows.reshape(rows), grad_queries, grad_passages


def solution(mesh):
    rows = P(("grp", "blk"))
    matrix = P(("grp", "blk"), None)
    return jax.shard_map(
        per_device,
        mesh=mesh,
        in_specs=(matrix, matrix, matrix, rows),
        out_specs=(rows, matrix, matrix),
        check_vma=False,
    )
```

```python
import functools
import math

import jax
import jax.numpy as jnp
from jax import lax
from jax.experimental import pallas as pl
from jax.experimental.pallas import tpu as pltpu
from jax.sharding import PartitionSpec as P

INV_TEMP = 50.0
BF16 = jnp.bfloat16
F32 = jnp.float32
CHUNK = 512
TAIL = 16
LONG, SOME = 5 * 10**10, 16 * 10**9
VMEM = pl.BlockSpec(memory_space=pltpu.VMEM)
HBM = pl.BlockSpec(memory_space=pltpu.HBM)
TOKEN = jax.ShapeDtypeStruct((8, 128), F32)


def dot(left, right, dims):
    return lax.dot_general(left, right, (dims, ((), ())), preferred_element_type=F32)


def size_of(arrays):
    return sum(math.prod(a.shape) * jnp.dtype(a.dtype).itemsize for a in arrays)


def local_call(body, out_shape, *args, flops=0, in_specs=None, out_specs=None, scratch=(), limit=20):
    return pl.pallas_call(
        body,
        out_shape=out_shape,
        in_specs=in_specs or [VMEM] * len(args),
        out_specs=out_specs or [VMEM] * len(out_shape),
        scratch_shapes=list(scratch),
        cost_estimate=pl.CostEstimate(
            flops=flops, bytes_accessed=size_of(args) + size_of(out_shape), transcendentals=0
        ),
        compiler_params=pltpu.CompilerParams(vmem_limit_bytes=limit * 2**20),
    )(*args)


def signal(token):
    token[...] = jnp.zeros(token.shape, token.dtype)


def split_index(index, rows, group_rows):
    if group_rows & (group_rows - 1) or rows & (rows - 1):
        return index // group_rows, index % rows
    return index >> (group_rows.bit_length() - 1), index & (rows - 1)


def load_body(groups, group_rows, q_hbm, p_hbm, index_hbm, *refs):
    pieces, (token, index_ref, sems) = refs[:groups], refs[groups:]
    rows = q_hbm.shape[0]
    cols = pieces[0].shape[1]
    g = lax.axis_index("grp")
    index_copy = pltpu.make_async_copy(index_hbm, index_ref, sems.at[2 * groups])
    index_copy.start()
    copies = []
    for r, piece in enumerate(pieces):
        at = pl.ds(pl.multiple_of((g ^ r) * cols, 128), cols)
        for n, source in enumerate((q_hbm, p_hbm)):
            target = piece.at[pl.ds(n * rows, rows)]
            copies.append(pltpu.make_async_copy(source.at[:, at], target, sems.at[2 * r + n]))
            copies[-1].start()
    signal(token)
    index_copy.wait()
    index = jnp.concatenate([index_ref[...], jnp.zeros((TAIL - 3, rows), jnp.int32)], axis=0)
    named_group, named_row = split_index(index, rows, group_rows)
    named_group = named_group.astype(F32).astype(BF16)
    named_row = named_row.astype(F32).astype(BF16)
    for piece in pieces:
        piece[2 * rows :, :rows] = named_group
        piece[2 * rows :, rows : 2 * rows] = named_row
        if cols > 2 * rows:
            piece[2 * rows :, 2 * rows :] = jnp.zeros((TAIL, cols - 2 * rows), BF16)
    for copy in copies:
        copy.wait()


def places_of(piece_ref, rows):
    tail = piece_ref[2 * rows :, : 2 * rows].astype(F32).astype(jnp.int32)
    g = lax.axis_index("grp")
    return [(tail[k : k + 1, :rows] ^ g) * rows + tail[k : k + 1, rows:] for k in range(3)]


def hard_scores_body(groups, *refs):
    pieces, outs = refs[:groups][::-1], refs[groups + 1 :]
    rows = outs[0].shape[1]
    ids = lax.broadcasted_iota(jnp.int32, (rows, rows), 0)
    for r in range(groups):
        others = [other for other in range(groups) if other != r]
        places = places_of(pieces[r], rows)
        held = jnp.concatenate([pieces[other][rows : 2 * rows] for other in others], axis=0)
        dots = dot(held, pieces[r][:rows], ((1,), (1,)))
        sums = [jnp.zeros((1, rows), F32) for _ in places]
        for n, other in enumerate(others):
            block = dots[n * rows : (n + 1) * rows]
            for k, place in enumerate(places):
                hit = jnp.where(ids == place - other * rows, block, 0.0)
                sums[k] += jnp.sum(hit, axis=0, keepdims=True)
        outs[r][...] = jnp.concatenate(sums, axis=0)


def hard_grads_body(groups, *refs):
    coefs, pieces, outs = refs[0], refs[1 : groups + 1], refs[groups + 2 : 2 * groups + 2]
    token, matrix, matrix_t = refs[2 * groups + 2 :]
    g = lax.axis_index("grp")
    rows = coefs.shape[2]
    cols = outs[0].shape[1]
    signal(token)
    ids = lax.broadcasted_iota(jnp.int32, (groups * rows, rows), 0)
    for r in range(groups):
        places = places_of(pieces[r], rows)
        coef = coefs[g ^ r]
        total = jnp.zeros(ids.shape, F32)
        for k in range(3):
            total += jnp.where(ids == places[k], coef[k : k + 1], 0.0)
        mine = slice(r * rows, (r + 1) * rows)
        matrix[:, mine] = total.astype(BF16)
        matrix_t[mine] = total.T.astype(BF16)
    step = min(cols, 256)
    for c in range(0, cols, step):
        at = slice(c, c + step)
        q_all = jnp.concatenate([piece[:rows, at] for piece in pieces], axis=0)
        p_all = jnp.concatenate([piece[rows : 2 * rows, at] for piece in pieces], axis=0)
        grad_q = dot(matrix_t[...], p_all, ((1,), (0,))).astype(BF16)
        grad_p = dot(matrix[...], q_all, ((1,), (0,))).astype(BF16)
        for r in range(groups):
            mine = slice(r * rows, (r + 1) * rows)
            outs[r][:rows, at] = grad_q[mine]
            outs[r][rows:, at] = grad_p[mine]


def pass_body(source, token, out):
    out[...] = source[...]


def choose_body(n1_ref, e3_ref, q_ref, out):
    width = q_ref.shape[1]
    odd = lax.axis_index("blk") % 2 == 1
    out[:, width:] = q_ref[...]

    @pl.when(odd)
    def _():
        out[:, :width] = n1_ref[...]

    @pl.when(jnp.logical_not(odd))
    def _():
        out[:, :width] = e3_ref[...]


def scores_body(q_ref, *refs):
    half = len(refs) // 2
    for block, out in zip(refs[:half], refs[half:]):
        out[...] = dot(block[...], q_ref[...], ((1,), (1,)))


def last_score_body(q_ref, pair_ref, out):
    out[...] = dot(pair_ref[:, : q_ref.shape[1]], q_ref[...], ((1,), (1,)))


def weigh_body(
    groups, *refs
):
    parts, refs = refs[:groups], refs[groups:]
    q_ref, s0_ref, s1_ref, s2_ref, s3_ref, last_ref, w_ref, *refs = refs
    loss_ref, coef_ref, hard_out, swap_ref, term3_ref = refs
    rows, width = q_ref.shape
    w = w_ref[...]
    s3 = INV_TEMP * (s3_ref[...] + dot(last_ref[...], q_ref[...], ((1,), (1,))))
    scores = [INV_TEMP * s0_ref[...], INV_TEMP * s1_ref[...], INV_TEMP * s2_ref[...], s3]
    hard = parts[-1][...]
    for other in parts[-2::-1]:
        hard = hard + other[...]
    hard = INV_TEMP * hard
    largest = jnp.max(hard, axis=0, keepdims=True)
    for block in scores:
        largest = jnp.maximum(largest, jnp.max(block, axis=0, keepdims=True))
    summed = jnp.sum(jnp.exp(hard - largest), axis=0, keepdims=True)
    for block in scores:
        summed = summed + jnp.sum(jnp.exp(block - largest), axis=0, keepdims=True)
    log_total = largest + jnp.log(summed)
    for s, block in enumerate(scores):
        coef = (w * jnp.exp(block - log_total)).astype(BF16)
        coef_ref[:, s * rows : (s + 1) * rows] = coef
        if s in (1, 2):
            swap_ref[:, (s - 1) * rows : s * rows] = coef
    coef3 = coef_ref[:, 3 * rows :]
    for c in range(0, width, CHUNK):
        at = slice(c, c + CHUNK)
        term3_ref[:, at] = dot(coef3, q_ref[:, at], ((1,), (0,))).astype(BF16)
    hard_out[...] = jnp.zeros(hard_out.shape, F32)
    hard_out[:3] = (w * jnp.exp(hard - log_total)).astype(BF16).astype(F32)
    eye = lax.broadcasted_iota(jnp.int32, (rows, rows), 0) == lax.broadcasted_iota(
        jnp.int32, (rows, rows), 1
    )
    loss_ref[...] = log_total - jnp.sum(jnp.where(eye, scores[0], 0.0), axis=0, keepdims=True)


def sums_body(q_ref, pair_ref, coef_ref, swap_ref, sent3, partial1, token):
    signal(token)
    rows, width = q_ref.shape
    odd = lax.axis_index("blk") % 2 == 1
    mine = jnp.where(odd, coef_ref[:, rows : 2 * rows], coef_ref[:, 3 * rows :])
    coef = jnp.concatenate([mine, swap_ref[:, rows:]], axis=1)
    for c in range(0, width, CHUNK):
        at = slice(c, c + CHUNK)
        held = jnp.concatenate([q_ref[:, at], pair_ref[:, width + c : width + c + CHUNK]], axis=0)
        total = dot(coef, held, ((1,), (0,)))
        sent3[:, at] = total.astype(BF16)
        partial1[:, at] = total


def relay_body(partial1, got3_ref, out, done):
    signal(done)
    out[...] = (partial1[...] + got3_ref[...].astype(F32)).astype(BF16)


def base_body(
    q_ref, pair_ref, p_ref, n1_ref, e3_ref, o3_ref, coef_ref, swap_ref, w_ref, own3_ref,
    token, pulled, base, coef_t,
):
    rows, width = q_ref.shape
    w = jnp.broadcast_to(w_ref[...], (rows, rows)).T[:, :1]
    odd = lax.axis_index("blk") % 2 == 1
    blocks = (p_ref, n1_ref, pair_ref, e3_ref, o3_ref)
    for s in range(5):
        k = min(s, 3) * rows
        coef_t[:, s * rows : (s + 1) * rows] = coef_ref[:, k : k + rows].astype(F32).T.astype(BF16)
    coef = [coef_ref[:, :rows], jnp.where(odd, swap_ref[:, :rows], jnp.zeros((rows, rows), BF16))]
    coef = jnp.concatenate(coef, axis=1)
    for c in range(0, width, CHUNK):
        at = slice(c, c + CHUNK)
        held = jnp.concatenate([block[:, at] for block in blocks], axis=0)
        pulled[:, at] = dot(coef_t[...], held, ((1,), (0,))) - w * p_ref[:, at].astype(F32)
        held = jnp.concatenate([q_ref[:, at], pair_ref[:, width + c : width + c + CHUNK]], axis=0)
        own = dot(coef, held, ((1,), (0,))) + own3_ref[:, at].astype(F32)
        base[:, at] = own - w * q_ref[:, at].astype(F32)


def gather_body(groups, pulled, base, *refs):
    backs, (out, almost, held, sems) = refs[:groups][::-1], refs[groups:]
    rows, cols = pulled.shape[0], backs[0].shape[1]
    g = lax.axis_index("grp")
    copies = []
    for r, back in enumerate(backs):
        at = pl.ds(pl.multiple_of((g ^ r) * cols, 128), cols)
        held[:, at] = (INV_TEMP * (pulled[:, at] + back[:rows].astype(F32))).astype(BF16)
        copies.append(pltpu.make_async_copy(held.at[:, at], out.at[:, at], sems.at[r]))
        copies[-1].start()
        almost[:, at] = base[:, at] + back[rows:].astype(F32)
    for copy in copies:
        copy.wait()


def finish_body(almost, own1, out, held, sems):
    width = almost.shape[1]
    copies = []
    for n, c in enumerate(range(0, width, CHUNK)):
        at = slice(c, c + CHUNK)
        held[:, at] = (INV_TEMP * (almost[:, at] + own1[:, at].astype(F32))).astype(BF16)
        copies.append(pltpu.make_async_copy(held.at[:, at], out.at[:, at], sems.at[n]))
        copies[-1].start()
    for copy in copies:
        copy.wait()


def per_device(queries, passages, hard_index, weights):
    rows, width = queries.shape
    groups = lax.axis_size("grp")
    loop = lax.axis_size("blk")
    cols = width // groups

    def shift(array, by, which=(0, 1)):
        pairs = [(i, (i + by) % loop) for i in range(loop) if i % 2 in which]
        return lax.ppermute(array, "blk", pairs)

    def swap(array):
        return lax.ppermute(array, "blk", [(i, i ^ 1) for i in range(loop)])

    def over_groups(array, r):
        return lax.ppermute(array, "grp", [(i, i ^ r) for i in range(groups)])

    def exchange(arrays):
        out = list(arrays)
        for r in reversed(range(1, groups)):
            out[r] = over_groups(arrays[r], r)
        return out

    def like(*shape, dtype=BF16):
        return jax.ShapeDtypeStruct(shape, dtype)

    block, block32 = like(rows, width), like(rows, width, dtype=F32)
    square, triple = like(rows, rows, dtype=F32), like(3, rows, dtype=F32)
    piece, back = like(2 * rows + TAIL, cols), like(2 * rows, cols)

    next1 = shift(passages, -1)

    *pieces, token = local_call(
        functools.partial(load_body, groups, loop * rows), [piece] * groups + [TOKEN],
        queries, passages, hard_index.T, in_specs=[HBM, HBM, HBM],
        scratch=[pltpu.VMEM((3, rows), jnp.int32), pltpu.SemaphoreType.DMA((2 * groups + 1,))],
        limit=51,
    )
    pieces = exchange(pieces)

    (later_p,) = local_call(pass_body, [block], passages, token)
    next3_even = shift(later_p, -3, (1,))
    (next1,) = local_call(pass_body, [block], next1, token, flops=LONG)
    next3_odd = shift(next1, -2, (1,))
    pair = swap(
        local_call(choose_body, [like(rows, 2 * width)], next1, next3_even, queries, flops=LONG)[0]
    )

    s0, s1, s3 = local_call(scores_body, [square] * 3, queries, passages, next1, next3_even)
    parts = local_call(
        functools.partial(hard_scores_body, groups), [triple] * groups, *pieces[::-1], s0, flops=LONG
    )
    (s2,) = local_call(last_score_body, [square], queries, pair)
    parts = exchange(parts)
    loss_rows, coef, hard_coef, to_core, term3 = local_call(
        functools.partial(weigh_body, groups),
        [like(1, rows, dtype=F32), like(rows, 4 * rows), like(8, rows, dtype=F32), like(rows, 2 * rows), block],
        *parts[::-1], queries, s0, s1, s2, s3, next3_odd, weights[None, :],
    )

    got3 = shift(term3, 2, (1,))
    from_core = swap(to_core)
    sent3, partial1, token = local_call(
        sums_body, [block, block32, TOKEN], queries, pair, coef, from_core
    )
    own3 = shift(sent3, 3, (0,))

    hard_coefs = lax.all_gather(hard_coef, "grp")
    square_all = pltpu.VMEM((groups * rows, groups * rows), BF16)
    *backs, token = local_call(
        functools.partial(hard_grads_body, groups), [back] * groups + [TOKEN],
        hard_coefs, *pieces, token, scratch=[square_all, square_all],
    )
    backs = exchange(backs)

    sent1, token = local_call(relay_body, [block, TOKEN], partial1, got3, flops=SOME)
    own1 = shift(sent1, 1, (1,))

    pulled, base = local_call(
        base_body, [block32, block32],
        queries, pair, passages, next1, next3_even, next3_odd, coef, from_core,
        weights[None, :], own3, token, flops=LONG, scratch=[pltpu.VMEM((rows, 5 * rows), BF16)],
    )
    held = pltpu.VMEM((rows, width), BF16)
    grad_queries, almost = local_call(
        functools.partial(gather_body, groups), [block, block32], pulled, base, *backs[::-1],
        out_specs=[HBM, VMEM], scratch=[held, pltpu.SemaphoreType.DMA((groups,))],
    )
    (grad_passages,) = local_call(
        finish_body, [block], almost, own1, out_specs=[HBM],
        scratch=[held, pltpu.SemaphoreType.DMA((width // CHUNK,))],
    )
    return loss_rows.reshape(rows), grad_queries, grad_passages


def solution(mesh):
    rows = P(("grp", "blk"))
    matrix = P(("grp", "blk"), None)
    return jax.shard_map(
        per_device,
        mesh=mesh,
        in_specs=(matrix, matrix, matrix, rows),
        out_specs=(rows, matrix, matrix),
        check_vma=False,
    )
```

```python
import functools
import math

import jax
import jax.numpy as jnp
from jax import lax
from jax.experimental import pallas as pl
from jax.experimental.pallas import tpu as pltpu
from jax.sharding import PartitionSpec as P

INV_TEMP = 50.0
BF16 = jnp.bfloat16
F32 = jnp.float32
CHUNK = 512
TAIL = 16
LONG, SOME = 5 * 10**10, 16 * 10**9
VMEM = pl.BlockSpec(memory_space=pltpu.VMEM)
HBM = pl.BlockSpec(memory_space=pltpu.HBM)
TOKEN = jax.ShapeDtypeStruct((8, 128), F32)


def dot(left, right, dims):
    return lax.dot_general(left, right, (dims, ((), ())), preferred_element_type=F32)


def size_of(arrays):
    return sum(math.prod(a.shape) * jnp.dtype(a.dtype).itemsize for a in arrays)


def local_call(body, out_shape, *args, flops=0, in_specs=None, out_specs=None, scratch=(), limit=20):
    return pl.pallas_call(
        body,
        out_shape=out_shape,
        in_specs=in_specs or [VMEM] * len(args),
        out_specs=out_specs or [VMEM] * len(out_shape),
        scratch_shapes=list(scratch),
        cost_estimate=pl.CostEstimate(
            flops=flops, bytes_accessed=size_of(args) + size_of(out_shape), transcendentals=0
        ),
        compiler_params=pltpu.CompilerParams(vmem_limit_bytes=limit * 2**20),
    )(*args)


def signal(token):
    token[...] = jnp.zeros(token.shape, token.dtype)


def split_index(index, rows, group_rows):
    if group_rows & (group_rows - 1) or rows & (rows - 1):
        return index // group_rows, index % rows
    return index >> (group_rows.bit_length() - 1), index & (rows - 1)


def load_body(groups, group_rows, q_hbm, p_hbm, index_hbm, *refs):
    pieces, (token, index_ref, sems) = refs[:groups], refs[groups:]
    rows = q_hbm.shape[0]
    cols = pieces[0].shape[1]
    g = lax.axis_index("grp")
    index_copy = pltpu.make_async_copy(index_hbm, index_ref, sems.at[2 * groups])
    index_copy.start()
    copies = []
    for r, piece in enumerate(pieces):
        at = pl.ds(pl.multiple_of((g ^ r) * cols, 128), cols)
        for n, source in enumerate((q_hbm, p_hbm)):
            target = piece.at[pl.ds(n * rows, rows)]
            copies.append(pltpu.make_async_copy(source.at[:, at], target, sems.at[2 * r + n]))
            copies[-1].start()
    signal(token)
    index_copy.wait()
    index = jnp.concatenate([index_ref[...], jnp.zeros((TAIL - 3, rows), jnp.int32)], axis=0)
    named_group, named_row = split_index(index, rows, group_rows)
    named_group = named_group.astype(F32).astype(BF16)
    named_row = named_row.astype(F32).astype(BF16)
    for piece in pieces:
        piece[2 * rows :, :rows] = named_group
        piece[2 * rows :, rows : 2 * rows] = named_row
        if cols > 2 * rows:
            piece[2 * rows :, 2 * rows :] = jnp.zeros((TAIL, cols - 2 * rows), BF16)
    for copy in copies:
        copy.wait()


def places_of(piece_ref, rows):
    tail = piece_ref[2 * rows :, : 2 * rows].astype(F32).astype(jnp.int32)
    g = lax.axis_index("grp")
    return [(tail[k : k + 1, :rows] ^ g) * rows + tail[k : k + 1, rows:] for k in range(3)]


def hard_scores_body(groups, *refs):
    pieces, outs = refs[:groups][::-1], refs[groups + 1 :]
    rows = outs[0].shape[1]
    ids = lax.broadcasted_iota(jnp.int32, (rows, rows), 0)
    for r in range(groups):
        others = [other for other in range(groups) if other != r]
        places = places_of(pieces[r], rows)
        held = jnp.concatenate([pieces[other][rows : 2 * rows] for other in others], axis=0)
        dots = dot(held, pieces[r][:rows], ((1,), (1,)))
        sums = [jnp.zeros((1, rows), F32) for _ in places]
        for n, other in enumerate(others):
            block = dots[n * rows : (n + 1) * rows]
            for k, place in enumerate(places):
                hit = jnp.where(ids == place - other * rows, block, 0.0)
                sums[k] += jnp.sum(hit, axis=0, keepdims=True)
        outs[r][...] = jnp.concatenate(sums, axis=0)


def hard_grads_body(groups, *refs):
    coefs, pieces, outs = refs[:groups][::-1], refs[groups : 2 * groups][::-1], refs[2 * groups + 1 : 3 * groups + 1]
    token, matrix, matrix_t = refs[3 * groups + 1 :]
    rows = coefs[0].shape[1]
    cols = outs[0].shape[1]
    signal(token)
    ids = lax.broadcasted_iota(jnp.int32, (groups * rows, rows), 0)
    for r in range(groups):
        places = places_of(pieces[r], rows)
        total = jnp.zeros(ids.shape, F32)
        for k in range(3):
            total += jnp.where(ids == places[k], coefs[r][k : k + 1], 0.0)
        mine = slice(r * rows, (r + 1) * rows)
        matrix[:, mine] = total.astype(BF16)
        matrix_t[mine] = total.T.astype(BF16)
    step = min(cols, 256)
    for c in range(0, cols, step):
        at = slice(c, c + step)
        q_all = jnp.concatenate([piece[:rows, at] for piece in pieces], axis=0)
        p_all = jnp.concatenate([piece[rows : 2 * rows, at] for piece in pieces], axis=0)
        grad_q = dot(matrix_t[...], p_all, ((1,), (0,))).astype(BF16)
        grad_p = dot(matrix[...], q_all, ((1,), (0,))).astype(BF16)
        for r in range(groups):
            mine = slice(r * rows, (r + 1) * rows)
            outs[r][:rows, at] = grad_q[mine]
            outs[r][rows:, at] = grad_p[mine]


def pass_body(source, token, out):
    out[...] = source[...]


def choose_body(n1_ref, e3_ref, q_ref, out):
    width = q_ref.shape[1]
    odd = lax.axis_index("blk") % 2 == 1
    out[:, width:] = q_ref[...]

    @pl.when(odd)
    def _():
        out[:, :width] = n1_ref[...]

    @pl.when(jnp.logical_not(odd))
    def _():
        out[:, :width] = e3_ref[...]


def scores_body(q_ref, *refs):
    half = len(refs) // 2
    for block, out in zip(refs[:half], refs[half:]):
        out[...] = dot(block[...], q_ref[...], ((1,), (1,)))


def last_score_body(q_ref, pair_ref, out):
    out[...] = dot(pair_ref[:, : q_ref.shape[1]], q_ref[...], ((1,), (1,)))


def weigh_body(
    groups, *refs
):
    parts, refs = refs[:groups], refs[groups:]
    q_ref, s0_ref, s1_ref, s2_ref, s3_ref, last_ref, w_ref, *refs = refs
    loss_ref, coef_ref, hard_out, swap_ref, term3_ref = refs
    rows, width = q_ref.shape
    w = w_ref[...]
    s3 = INV_TEMP * (s3_ref[...] + dot(last_ref[...], q_ref[...], ((1,), (1,))))
    scores = [INV_TEMP * s0_ref[...], INV_TEMP * s1_ref[...], INV_TEMP * s2_ref[...], s3]
    hard = parts[-1][...]
    for other in parts[-2::-1]:
        hard = hard + other[...]
    hard = INV_TEMP * hard
    largest = jnp.max(hard, axis=0, keepdims=True)
    for block in scores:
        largest = jnp.maximum(largest, jnp.max(block, axis=0, keepdims=True))
    summed = jnp.sum(jnp.exp(hard - largest), axis=0, keepdims=True)
    for block in scores:
        summed = summed + jnp.sum(jnp.exp(block - largest), axis=0, keepdims=True)
    log_total = largest + jnp.log(summed)
    for s, block in enumerate(scores):
        coef = (w * jnp.exp(block - log_total)).astype(BF16)
        coef_ref[:, s * rows : (s + 1) * rows] = coef
        if s in (1, 2):
            swap_ref[:, (s - 1) * rows : s * rows] = coef
    coef3 = coef_ref[:, 3 * rows :]
    for c in range(0, width, CHUNK):
        at = slice(c, c + CHUNK)
        term3_ref[:, at] = dot(coef3, q_ref[:, at], ((1,), (0,))).astype(BF16)
    hard_out[...] = (w * jnp.exp(hard - log_total)).astype(BF16).astype(F32)
    eye = lax.broadcasted_iota(jnp.int32, (rows, rows), 0) == lax.broadcasted_iota(
        jnp.int32, (rows, rows), 1
    )
    loss_ref[...] = log_total - jnp.sum(jnp.where(eye, scores[0], 0.0), axis=0, keepdims=True)


def sums_body(q_ref, pair_ref, coef_ref, swap_ref, sent3, partial1, token):
    signal(token)
    rows, width = q_ref.shape
    odd = lax.axis_index("blk") % 2 == 1
    mine = jnp.where(odd, coef_ref[:, rows : 2 * rows], coef_ref[:, 3 * rows :])
    coef = jnp.concatenate([mine, swap_ref[:, rows:]], axis=1)
    for c in range(0, width, CHUNK):
        at = slice(c, c + CHUNK)
        held = jnp.concatenate([q_ref[:, at], pair_ref[:, width + c : width + c + CHUNK]], axis=0)
        total = dot(coef, held, ((1,), (0,)))
        sent3[:, at] = total.astype(BF16)
        partial1[:, at] = total


def relay_body(partial1, got3_ref, out, done):
    signal(done)
    out[...] = (partial1[...] + got3_ref[...].astype(F32)).astype(BF16)


def base_body(
    q_ref, pair_ref, p_ref, n1_ref, e3_ref, o3_ref, coef_ref, swap_ref, w_ref, own3_ref,
    token, pulled, base, coef_t,
):
    rows, width = q_ref.shape
    w = jnp.broadcast_to(w_ref[...], (rows, rows)).T[:, :1]
    odd = lax.axis_index("blk") % 2 == 1
    blocks = (p_ref, n1_ref, pair_ref, e3_ref, o3_ref)
    for s in range(5):
        k = min(s, 3) * rows
        coef_t[:, s * rows : (s + 1) * rows] = coef_ref[:, k : k + rows].astype(F32).T.astype(BF16)
    coef = [coef_ref[:, :rows], jnp.where(odd, swap_ref[:, :rows], jnp.zeros((rows, rows), BF16))]
    coef = jnp.concatenate(coef, axis=1)
    for c in range(0, width, CHUNK):
        at = slice(c, c + CHUNK)
        held = jnp.concatenate([block[:, at] for block in blocks], axis=0)
        pulled[:, at] = dot(coef_t[...], held, ((1,), (0,))) - w * p_ref[:, at].astype(F32)
        held = jnp.concatenate([q_ref[:, at], pair_ref[:, width + c : width + c + CHUNK]], axis=0)
        own = dot(coef, held, ((1,), (0,))) + own3_ref[:, at].astype(F32)
        base[:, at] = own - w * q_ref[:, at].astype(F32)


def gather_body(groups, pulled, base, *refs):
    backs, (out, almost, held, sems) = refs[:groups][::-1], refs[groups:]
    rows, cols = pulled.shape[0], backs[0].shape[1]
    g = lax.axis_index("grp")
    copies = []
    for r, back in enumerate(backs):
        at = pl.ds(pl.multiple_of((g ^ r) * cols, 128), cols)
        held[:, at] = (INV_TEMP * (pulled[:, at] + back[:rows].astype(F32))).astype(BF16)
        copies.append(pltpu.make_async_copy(held.at[:, at], out.at[:, at], sems.at[r]))
        copies[-1].start()
        almost[:, at] = base[:, at] + back[rows:].astype(F32)
    for copy in copies:
        copy.wait()


def finish_body(almost, own1, out, held, sems):
    width = almost.shape[1]
    copies = []
    for n, c in enumerate(range(0, width, CHUNK)):
        at = slice(c, c + CHUNK)
        held[:, at] = (INV_TEMP * (almost[:, at] + own1[:, at].astype(F32))).astype(BF16)
        copies.append(pltpu.make_async_copy(held.at[:, at], out.at[:, at], sems.at[n]))
        copies[-1].start()
    for copy in copies:
        copy.wait()


def per_device(queries, passages, hard_index, weights):
    rows, width = queries.shape
    groups = lax.axis_size("grp")
    loop = lax.axis_size("blk")
    cols = width // groups

    def pairs_of(by, which=(0, 1)):
        return [(i, (i + by) % loop) for i in range(loop) if i % 2 in which]

    def shift(array, by, which=(0, 1)):
        return lax.ppermute(array, "blk", pairs_of(by, which))

    def swap(array):
        return lax.ppermute(array, "blk", [(i, i ^ 1) for i in range(loop)])

    def over_groups(array, r):
        return lax.ppermute(array, "grp", [(i, i ^ r) for i in range(groups)])

    def exchange(arrays):
        out = list(arrays)
        for r in reversed(range(1, groups)):
            out[r] = over_groups(arrays[r], r)
        return out

    def like(*shape, dtype=BF16):
        return jax.ShapeDtypeStruct(shape, dtype)

    block, block32 = like(rows, width), like(rows, width, dtype=F32)
    square, triple = like(rows, rows, dtype=F32), like(3, rows, dtype=F32)
    piece, back = like(2 * rows + TAIL, cols), like(2 * rows, cols)

    next1 = shift(passages, -1)

    *pieces, token = local_call(
        functools.partial(load_body, groups, loop * rows), [piece] * groups + [TOKEN],
        queries, passages, hard_index.T, in_specs=[HBM, HBM, HBM],
        scratch=[pltpu.VMEM((3, rows), jnp.int32), pltpu.SemaphoreType.DMA((2 * groups + 1,))],
        limit=51,
    )
    pieces = exchange(pieces)

    (later_p,) = local_call(pass_body, [block], passages, token)
    next3_even = shift(later_p, -3, (1,))
    (next1,) = local_call(pass_body, [block], next1, token, flops=LONG)
    next3_odd = shift(next1, -2, (1,))
    pair = swap(
        local_call(choose_body, [like(rows, 2 * width)], next1, next3_even, queries, flops=LONG)[0]
    )

    s0, s1, s3 = local_call(scores_body, [square] * 3, queries, passages, next1, next3_even)
    parts = local_call(
        functools.partial(hard_scores_body, groups), [triple] * groups, *pieces[::-1], s0, flops=LONG
    )
    (s2,) = local_call(last_score_body, [square], queries, pair)
    parts = exchange(parts)
    loss_rows, coef, hard_coef, to_core, term3 = local_call(
        functools.partial(weigh_body, groups),
        [like(1, rows, dtype=F32), like(rows, 4 * rows), triple, like(rows, 2 * rows), block],
        *parts[::-1], queries, s0, s1, s2, s3, next3_odd, weights[None, :],
    )

    got3 = shift(term3, 2, (1,))
    from_core = swap(to_core)
    sent3, partial1, token = local_call(
        sums_body, [block, block32, TOKEN], queries, pair, coef, from_core
    )
    late = (loop - 4, loop - 1)
    own3 = lax.ppermute(sent3, "blk", [pair for pair in pairs_of(3, (0,)) if pair != late])

    hard_coefs = exchange([hard_coef] * groups)
    square_all = pltpu.VMEM((groups * rows, groups * rows), BF16)
    *backs, token = local_call(
        functools.partial(hard_grads_body, groups), [back] * groups + [TOKEN],
        *hard_coefs[::-1], *pieces[::-1], token, scratch=[square_all, square_all],
    )
    backs = exchange(backs)

    sent1, token = local_call(relay_body, [block, TOKEN], partial1, got3, flops=SOME)
    own1 = lax.ppermute(sent1, "blk", pairs_of(1, (1,)) + [late])

    pulled, base = local_call(
        base_body, [block32, block32],
        queries, pair, passages, next1, next3_even, next3_odd, coef, from_core,
        weights[None, :], own3, token, flops=LONG, scratch=[pltpu.VMEM((rows, 5 * rows), BF16)],
    )
    held = pltpu.VMEM((rows, width), BF16)
    grad_queries, almost = local_call(
        functools.partial(gather_body, groups), [block, block32], pulled, base, *backs[::-1],
        out_specs=[HBM, VMEM], scratch=[held, pltpu.SemaphoreType.DMA((groups,))],
    )
    (grad_passages,) = local_call(
        finish_body, [block], almost, own1, out_specs=[HBM],
        scratch=[held, pltpu.SemaphoreType.DMA((width // CHUNK,))],
    )
    return loss_rows.reshape(rows), grad_queries, grad_passages


def solution(mesh):
    rows = P(("grp", "blk"))
    matrix = P(("grp", "blk"), None)
    return jax.shard_map(
        per_device,
        mesh=mesh,
        in_specs=(matrix, matrix, matrix, rows),
        out_specs=(rows, matrix, matrix),
        check_vma=False,
    )
```

```python
import functools
import math

import jax
import jax.numpy as jnp
from jax import lax
from jax.experimental import pallas as pl
from jax.experimental.pallas import tpu as pltpu
from jax.sharding import PartitionSpec as P

INV_TEMP = 50.0
BF16 = jnp.bfloat16
F32 = jnp.float32
CHUNK = 512
TAIL = 16
LONG, SOME = 5 * 10**10, 16 * 10**9
VMEM = pl.BlockSpec(memory_space=pltpu.VMEM)
HBM = pl.BlockSpec(memory_space=pltpu.HBM)
TOKEN = jax.ShapeDtypeStruct((8, 128), F32)


def dot(left, right, dims):
    return lax.dot_general(left, right, (dims, ((), ())), preferred_element_type=F32)


def size_of(arrays):
    return sum(math.prod(a.shape) * jnp.dtype(a.dtype).itemsize for a in arrays)


def local_call(body, out_shape, *args, flops=0, in_specs=None, out_specs=None, scratch=(), limit=20):
    return pl.pallas_call(
        body,
        out_shape=out_shape,
        in_specs=in_specs or [VMEM] * len(args),
        out_specs=out_specs or [VMEM] * len(out_shape),
        scratch_shapes=list(scratch),
        cost_estimate=pl.CostEstimate(
            flops=flops, bytes_accessed=size_of(args) + size_of(out_shape), transcendentals=0
        ),
        compiler_params=pltpu.CompilerParams(vmem_limit_bytes=limit * 2**20),
    )(*args)


def signal(token):
    token[...] = jnp.zeros(token.shape, token.dtype)


def split_index(index, rows, group_rows):
    if group_rows & (group_rows - 1) or rows & (rows - 1):
        return index // group_rows, index % rows
    return index >> (group_rows.bit_length() - 1), index & (rows - 1)


def load_body(groups, group_rows, q_hbm, p_hbm, index_hbm, *refs):
    pieces, (token, index_ref, sems) = refs[:groups], refs[groups:]
    rows = q_hbm.shape[0]
    cols = pieces[0].shape[1]
    g = lax.axis_index("grp")
    index_copy = pltpu.make_async_copy(index_hbm, index_ref, sems.at[2 * groups])
    index_copy.start()
    copies = []
    for r, piece in enumerate(pieces):
        at = pl.ds(pl.multiple_of((g ^ r) * cols, 128), cols)
        for n, source in enumerate((q_hbm, p_hbm)):
            target = piece.at[pl.ds(n * rows, rows)]
            copies.append(pltpu.make_async_copy(source.at[:, at], target, sems.at[2 * r + n]))
            copies[-1].start()
    signal(token)
    index_copy.wait()
    index = jnp.concatenate([index_ref[...], jnp.zeros((TAIL - 3, rows), jnp.int32)], axis=0)
    named_group, named_row = split_index(index, rows, group_rows)
    named_group = named_group.astype(F32).astype(BF16)
    named_row = named_row.astype(F32).astype(BF16)
    for piece in pieces:
        piece[2 * rows :, :rows] = named_group
        piece[2 * rows :, rows : 2 * rows] = named_row
        if cols > 2 * rows:
            piece[2 * rows :, 2 * rows :] = jnp.zeros((TAIL, cols - 2 * rows), BF16)
    for copy in copies:
        copy.wait()


def places_of(piece_ref, rows):
    tail = piece_ref[2 * rows :, : 2 * rows].astype(F32).astype(jnp.int32)
    g = lax.axis_index("grp")
    return [(tail[k : k + 1, :rows] ^ g) * rows + tail[k : k + 1, rows:] for k in range(3)]


def hard_scores_body(groups, *refs):
    pieces, outs = refs[:groups][::-1], refs[groups + 1 :]
    rows = outs[0].shape[1]
    ids = lax.broadcasted_iota(jnp.int32, (rows, rows), 0)
    for r in range(groups):
        others = [other for other in range(groups) if other != r]
        places = places_of(pieces[r], rows)
        held = jnp.concatenate([pieces[other][rows : 2 * rows] for other in others], axis=0)
        dots = dot(held, pieces[r][:rows], ((1,), (1,)))
        sums = [jnp.zeros((1, rows), F32) for _ in places]
        for n, other in enumerate(others):
            block = dots[n * rows : (n + 1) * rows]
            for k, place in enumerate(places):
                hit = jnp.where(ids == place - other * rows, block, 0.0)
                sums[k] += jnp.sum(hit, axis=0, keepdims=True)
        outs[r][...] = jnp.concatenate(sums, axis=0)


def hard_grads_body(groups, *refs):
    coefs, pieces, outs = refs[:groups][::-1], refs[groups : 2 * groups][::-1], refs[2 * groups + 1 : 3 * groups + 1]
    token, matrix, matrix_t = refs[3 * groups + 1 :]
    rows = coefs[0].shape[1]
    cols = outs[0].shape[1]
    signal(token)
    ids = lax.broadcasted_iota(jnp.int32, (groups * rows, rows), 0)
    for r in range(groups):
        places = places_of(pieces[r], rows)
        total = jnp.zeros(ids.shape, F32)
        for k in range(3):
            total += jnp.where(ids == places[k], coefs[r][k : k + 1], 0.0)
        mine = slice(r * rows, (r + 1) * rows)
        matrix[:, mine] = total.astype(BF16)
        matrix_t[mine] = total.T.astype(BF16)
    step = min(cols, 256)
    for c in range(0, cols, step):
        at = slice(c, c + step)
        q_all = jnp.concatenate([piece[:rows, at] for piece in pieces], axis=0)
        p_all = jnp.concatenate([piece[rows : 2 * rows, at] for piece in pieces], axis=0)
        grad_q = dot(matrix_t[...], p_all, ((1,), (0,))).astype(BF16)
        grad_p = dot(matrix[...], q_all, ((1,), (0,))).astype(BF16)
        for r in range(groups):
            mine = slice(r * rows, (r + 1) * rows)
            outs[r][:rows, at] = grad_q[mine]
            outs[r][rows:, at] = grad_p[mine]


def pass_body(source, token, out):
    out[...] = source[...]


def relay_passages_body(next_ref, p_ref, token, out, relay):
    out[...] = next_ref[...]
    own = lax.axis_index("blk") == 2

    @pl.when(own)
    def _():
        relay[...] = p_ref[...]

    @pl.when(jnp.logical_not(own))
    def _():
        relay[...] = next_ref[...]


def choose_body(n1_ref, e3_ref, q_ref, out):
    width = q_ref.shape[1]
    odd = lax.axis_index("blk") % 2 == 1
    out[:, width:] = q_ref[...]

    @pl.when(odd)
    def _():
        out[:, :width] = n1_ref[...]

    @pl.when(jnp.logical_not(odd))
    def _():
        out[:, :width] = e3_ref[...]


def scores_body(q_ref, *refs):
    half = len(refs) // 2
    for block, out in zip(refs[:half], refs[half:]):
        out[...] = dot(block[...], q_ref[...], ((1,), (1,)))


def last_score_body(q_ref, pair_ref, out):
    out[...] = dot(pair_ref[:, : q_ref.shape[1]], q_ref[...], ((1,), (1,)))


def weigh_body(
    groups, *refs
):
    parts, refs = refs[:groups], refs[groups:]
    last_ref, q_ref, s0_ref, s1_ref, s2_ref, s3_ref, w_ref, *refs = refs
    loss_ref, coef_ref, hard_out, swap_ref, term3_ref = refs
    rows, width = q_ref.shape
    w = w_ref[...]
    s3 = INV_TEMP * (s3_ref[...] + dot(last_ref[...], q_ref[...], ((1,), (1,))))
    scores = [INV_TEMP * s0_ref[...], INV_TEMP * s1_ref[...], INV_TEMP * s2_ref[...], s3]
    hard = parts[-1][...]
    for other in parts[-2::-1]:
        hard = hard + other[...]
    hard = INV_TEMP * hard
    largest = jnp.max(hard, axis=0, keepdims=True)
    for block in scores:
        largest = jnp.maximum(largest, jnp.max(block, axis=0, keepdims=True))
    summed = jnp.sum(jnp.exp(hard - largest), axis=0, keepdims=True)
    for block in scores:
        summed = summed + jnp.sum(jnp.exp(block - largest), axis=0, keepdims=True)
    log_total = largest + jnp.log(summed)
    for s, block in enumerate(scores):
        coef = (w * jnp.exp(block - log_total)).astype(BF16)
        coef_ref[:, s * rows : (s + 1) * rows] = coef
        if s in (1, 2):
            swap_ref[:, (s - 1) * rows : s * rows] = coef
    coef3 = coef_ref[:, 3 * rows :]
    for c in range(0, width, CHUNK):
        at = slice(c, c + CHUNK)
        term3_ref[:, at] = dot(coef3, q_ref[:, at], ((1,), (0,))).astype(BF16)
    hard_out[...] = (w * jnp.exp(hard - log_total)).astype(BF16).astype(F32)
    eye = lax.broadcasted_iota(jnp.int32, (rows, rows), 0) == lax.broadcasted_iota(
        jnp.int32, (rows, rows), 1
    )
    loss_ref[...] = log_total - jnp.sum(jnp.where(eye, scores[0], 0.0), axis=0, keepdims=True)


def sums_body(q_ref, pair_ref, coef_ref, swap_ref, sent3, partial1, token):
    signal(token)
    rows, width = q_ref.shape
    odd = lax.axis_index("blk") % 2 == 1
    mine = jnp.where(odd, coef_ref[:, rows : 2 * rows], coef_ref[:, 3 * rows :])
    coef = jnp.concatenate([mine, swap_ref[:, rows:]], axis=1)
    for c in range(0, width, CHUNK):
        at = slice(c, c + CHUNK)
        held = jnp.concatenate([q_ref[:, at], pair_ref[:, width + c : width + c + CHUNK]], axis=0)
        total = dot(coef, held, ((1,), (0,)))
        sent3[:, at] = total.astype(BF16)
        partial1[:, at] = total


def relay_body(partial1, got3_ref, out, done):
    signal(done)
    out[...] = (partial1[...] + got3_ref[...].astype(F32)).astype(BF16)


def base_body(
    q_ref, pair_ref, p_ref, n1_ref, e3_ref, o3_ref, coef_ref, swap_ref, w_ref, own3_ref,
    token, pulled, base, coef_t,
):
    rows, width = q_ref.shape
    w = jnp.broadcast_to(w_ref[...], (rows, rows)).T[:, :1]
    odd = lax.axis_index("blk") % 2 == 1
    blocks = (p_ref, n1_ref, pair_ref, e3_ref, o3_ref)
    for s in range(5):
        k = min(s, 3) * rows
        coef_t[:, s * rows : (s + 1) * rows] = coef_ref[:, k : k + rows].astype(F32).T.astype(BF16)
    coef = [coef_ref[:, :rows], jnp.where(odd, swap_ref[:, :rows], jnp.zeros((rows, rows), BF16))]
    coef = jnp.concatenate(coef, axis=1)
    for c in range(0, width, CHUNK):
        at = slice(c, c + CHUNK)
        held = jnp.concatenate([block[:, at] for block in blocks], axis=0)
        pulled[:, at] = dot(coef_t[...], held, ((1,), (0,))) - w * p_ref[:, at].astype(F32)
        held = jnp.concatenate([q_ref[:, at], pair_ref[:, width + c : width + c + CHUNK]], axis=0)
        own = dot(coef, held, ((1,), (0,))) + own3_ref[:, at].astype(F32)
        base[:, at] = own - w * q_ref[:, at].astype(F32)


def gather_body(groups, pulled, base, *refs):
    backs, (out, almost, held, sems) = refs[:groups][::-1], refs[groups:]
    rows, cols = pulled.shape[0], backs[0].shape[1]
    g = lax.axis_index("grp")
    copies = []
    for r, back in enumerate(backs):
        at = pl.ds(pl.multiple_of((g ^ r) * cols, 128), cols)
        held[:, at] = (INV_TEMP * (pulled[:, at] + back[:rows].astype(F32))).astype(BF16)
        copies.append(pltpu.make_async_copy(held.at[:, at], out.at[:, at], sems.at[r]))
        copies[-1].start()
        almost[:, at] = base[:, at] + back[rows:].astype(F32)
    for copy in copies:
        copy.wait()


def finish_body(almost, own1, out, held, sems):
    width = almost.shape[1]
    copies = []
    for n, c in enumerate(range(0, width, CHUNK)):
        at = slice(c, c + CHUNK)
        held[:, at] = (INV_TEMP * (almost[:, at] + own1[:, at].astype(F32))).astype(BF16)
        copies.append(pltpu.make_async_copy(held.at[:, at], out.at[:, at], sems.at[n]))
        copies[-1].start()
    for copy in copies:
        copy.wait()


def per_device(queries, passages, hard_index, weights):
    rows, width = queries.shape
    groups = lax.axis_size("grp")
    loop = lax.axis_size("blk")
    cols = width // groups

    def pairs_of(by, which=(0, 1)):
        return [(i, (i + by) % loop) for i in range(loop) if i % 2 in which]

    def shift(array, by, which=(0, 1)):
        return lax.ppermute(array, "blk", pairs_of(by, which))

    def swap(array):
        return lax.ppermute(array, "blk", [(i, i ^ 1) for i in range(loop)])

    def over_groups(array, r):
        return lax.ppermute(array, "grp", [(i, i ^ r) for i in range(groups)])

    def exchange(arrays):
        out = list(arrays)
        for r in reversed(range(1, groups)):
            out[r] = over_groups(arrays[r], r)
        return out

    def like(*shape, dtype=BF16):
        return jax.ShapeDtypeStruct(shape, dtype)

    block, block32 = like(rows, width), like(rows, width, dtype=F32)
    square, triple = like(rows, rows, dtype=F32), like(3, rows, dtype=F32)
    piece, back = like(2 * rows + TAIL, cols), like(2 * rows, cols)

    next1 = shift(passages, -1)

    *pieces, token = local_call(
        functools.partial(load_body, groups, loop * rows), [piece] * groups + [TOKEN],
        queries, passages, hard_index.T, in_specs=[HBM, HBM, HBM],
        scratch=[pltpu.VMEM((3, rows), jnp.int32), pltpu.SemaphoreType.DMA((2 * groups + 1,))],
        limit=51,
    )
    pieces = exchange(pieces)

    (later_p,) = local_call(pass_body, [block], passages, token)
    next3_even = shift(later_p, -3, (1,))
    next1, relay = local_call(
        relay_passages_body, [block] * 2, next1, passages, token, flops=LONG
    )
    round_pair = (1, loop - 1)
    pairs = [pair for pair in pairs_of(-2, (1,)) if pair != round_pair] + [(2, loop - 1)]
    next3_odd = lax.ppermute(relay, "blk", pairs)
    pair = swap(
        local_call(choose_body, [like(rows, 2 * width)], next1, next3_even, queries, flops=LONG)[0]
    )

    s0, s1, s3 = local_call(scores_body, [square] * 3, queries, passages, next1, next3_even)
    parts = local_call(
        functools.partial(hard_scores_body, groups), [triple] * groups, *pieces[::-1], s0, flops=LONG
    )
    (s2,) = local_call(last_score_body, [square], queries, pair)
    parts = exchange(parts)
    loss_rows, coef, hard_coef, to_core, term3 = local_call(
        functools.partial(weigh_body, groups),
        [like(1, rows, dtype=F32), like(rows, 4 * rows), triple, like(rows, 2 * rows), block],
        *parts[::-1], next3_odd, queries, s0, s1, s2, s3, weights[None, :],
    )

    got3 = shift(term3, 2, (1,))
    from_core = swap(to_core)
    sent3, partial1, token = local_call(
        sums_body, [block, block32, TOKEN], queries, pair, coef, from_core
    )
    own3 = shift(sent3, 3, (0,))

    hard_coefs = exchange([hard_coef] * groups)
    square_all = pltpu.VMEM((groups * rows, groups * rows), BF16)
    *backs, token = local_call(
        functools.partial(hard_grads_body, groups), [back] * groups + [TOKEN],
        *hard_coefs[::-1], *pieces[::-1], token, scratch=[square_all, square_all],
    )
    backs = exchange(backs)

    sent1, token = local_call(relay_body, [block, TOKEN], partial1, got3, flops=SOME)
    own1 = shift(sent1, 1, (1,))

    pulled, base = local_call(
        base_body, [block32, block32],
        queries, pair, passages, next1, next3_even, next3_odd, coef, from_core,
        weights[None, :], own3, token, flops=LONG, scratch=[pltpu.VMEM((rows, 5 * rows), BF16)],
    )
    held = pltpu.VMEM((rows, width), BF16)
    grad_queries, almost = local_call(
        functools.partial(gather_body, groups), [block, block32], pulled, base, *backs[::-1],
        out_specs=[HBM, VMEM], scratch=[held, pltpu.SemaphoreType.DMA((groups,))],
    )
    (grad_passages,) = local_call(
        finish_body, [block], almost, own1, out_specs=[HBM],
        scratch=[held, pltpu.SemaphoreType.DMA((width // CHUNK,))],
    )
    return loss_rows.reshape(rows), grad_queries, grad_passages


def solution(mesh):
    rows = P(("grp", "blk"))
    matrix = P(("grp", "blk"), None)
    return jax.shard_map(
        per_device,
        mesh=mesh,
        in_specs=(matrix, matrix, matrix, rows),
        out_specs=(rows, matrix, matrix),
        check_vma=False,
    )
```

```python
import functools
import math

import jax
import jax.numpy as jnp
from jax import lax
from jax.experimental import pallas as pl
from jax.experimental.pallas import tpu as pltpu
from jax.sharding import PartitionSpec as P

INV_TEMP = 50.0
BF16 = jnp.bfloat16
F32 = jnp.float32
CHUNK = 512
TAIL = 16
LONG, SOME = 5 * 10**10, 16 * 10**9
VMEM = pl.BlockSpec(memory_space=pltpu.VMEM)
HBM = pl.BlockSpec(memory_space=pltpu.HBM)
TOKEN = jax.ShapeDtypeStruct((8, 128), F32)


def dot(left, right, dims):
    return lax.dot_general(left, right, (dims, ((), ())), preferred_element_type=F32)


def size_of(arrays):
    return sum(math.prod(a.shape) * jnp.dtype(a.dtype).itemsize for a in arrays)


def local_call(body, out_shape, *args, flops=0, in_specs=None, out_specs=None, scratch=(), limit=20):
    return pl.pallas_call(
        body,
        out_shape=out_shape,
        in_specs=in_specs or [VMEM] * len(args),
        out_specs=out_specs or [VMEM] * len(out_shape),
        scratch_shapes=list(scratch),
        cost_estimate=pl.CostEstimate(
            flops=flops, bytes_accessed=size_of(args) + size_of(out_shape), transcendentals=0
        ),
        compiler_params=pltpu.CompilerParams(vmem_limit_bytes=limit * 2**20),
    )(*args)


def signal(token):
    token[...] = jnp.zeros(token.shape, token.dtype)


def split_index(index, rows, group_rows):
    if group_rows & (group_rows - 1) or rows & (rows - 1):
        return index // group_rows, index % rows
    return index >> (group_rows.bit_length() - 1), index & (rows - 1)


def load_body(groups, group_rows, q_hbm, p_hbm, index_hbm, *refs):
    pieces, (token, index_ref, sems) = refs[:groups], refs[groups:]
    rows = q_hbm.shape[0]
    cols = pieces[0].shape[1]
    g = lax.axis_index("grp")
    index_copy = pltpu.make_async_copy(index_hbm, index_ref, sems.at[2 * groups])
    index_copy.start()
    copies = []
    for r, piece in enumerate(pieces):
        at = pl.ds(pl.multiple_of((g ^ r) * cols, 128), cols)
        for n, source in enumerate((q_hbm, p_hbm)):
            target = piece.at[pl.ds(n * rows, rows)]
            copies.append(pltpu.make_async_copy(source.at[:, at], target, sems.at[2 * r + n]))
            copies[-1].start()
    signal(token)
    index_copy.wait()
    index = jnp.concatenate([index_ref[...], jnp.zeros((TAIL - 3, rows), jnp.int32)], axis=0)
    named_group, named_row = split_index(index, rows, group_rows)
    named_group = named_group.astype(F32).astype(BF16)
    named_row = named_row.astype(F32).astype(BF16)
    for piece in pieces:
        piece[2 * rows :, :rows] = named_group
        piece[2 * rows :, rows : 2 * rows] = named_row
        if cols > 2 * rows:
            piece[2 * rows :, 2 * rows :] = jnp.zeros((TAIL, cols - 2 * rows), BF16)
    for copy in copies:
        copy.wait()


def places_of(piece_ref, rows):
    tail = piece_ref[2 * rows :, : 2 * rows].astype(F32).astype(jnp.int32)
    g = lax.axis_index("grp")
    return [(tail[k : k + 1, :rows] ^ g) * rows + tail[k : k + 1, rows:] for k in range(3)]


def hard_scores_body(groups, *refs):
    pieces, outs = [*refs[2 : groups + 1][::-1], refs[0]], refs[groups + 1 :]
    rows = outs[0].shape[1]
    ids = lax.broadcasted_iota(jnp.int32, (rows, rows), 0)
    for r in range(groups):
        others = [other for other in range(groups) if other != r]
        places = places_of(pieces[r], rows)
        held = jnp.concatenate([pieces[other][rows : 2 * rows] for other in others], axis=0)
        dots = dot(held, pieces[r][:rows], ((1,), (1,)))
        sums = [jnp.zeros((1, rows), F32) for _ in places]
        for n, other in enumerate(others):
            block = dots[n * rows : (n + 1) * rows]
            for k, place in enumerate(places):
                hit = jnp.where(ids == place - other * rows, block, 0.0)
                sums[k] += jnp.sum(hit, axis=0, keepdims=True)
        outs[r][...] = jnp.concatenate(sums, axis=0)


def hard_grads_body(groups, *refs):
    coefs, pieces, outs = refs[:groups][::-1], refs[groups : 2 * groups][::-1], refs[2 * groups + 1 : 3 * groups + 1]
    token, matrix, matrix_t = refs[3 * groups + 1 :]
    rows = coefs[0].shape[1]
    cols = outs[0].shape[1]
    signal(token)
    ids = lax.broadcasted_iota(jnp.int32, (groups * rows, rows), 0)
    for r in range(groups):
        places = places_of(pieces[r], rows)
        total = jnp.zeros(ids.shape, F32)
        for k in range(3):
            total += jnp.where(ids == places[k], coefs[r][k : k + 1], 0.0)
        mine = slice(r * rows, (r + 1) * rows)
        matrix[:, mine] = total.astype(BF16)
        matrix_t[mine] = total.T.astype(BF16)
    step = min(cols, 256)
    for c in range(0, cols, step):
        at = slice(c, c + step)
        q_all = jnp.concatenate([piece[:rows, at] for piece in pieces], axis=0)
        p_all = jnp.concatenate([piece[rows : 2 * rows, at] for piece in pieces], axis=0)
        grad_q = dot(matrix_t[...], p_all, ((1,), (0,))).astype(BF16)
        grad_p = dot(matrix[...], q_all, ((1,), (0,))).astype(BF16)
        for r in range(groups):
            mine = slice(r * rows, (r + 1) * rows)
            outs[r][:rows, at] = grad_q[mine]
            outs[r][rows:, at] = grad_p[mine]


def pass_body(source, token, out):
    out[...] = source[...]


def choose_body(n1_ref, e3_ref, q_ref, out):
    width = q_ref.shape[1]
    odd = lax.axis_index("blk") % 2 == 1
    out[:, width:] = q_ref[...]

    @pl.when(odd)
    def _():
        out[:, :width] = n1_ref[...]

    @pl.when(jnp.logical_not(odd))
    def _():
        out[:, :width] = e3_ref[...]


def scores_body(q_ref, *refs):
    half = len(refs) // 2
    for block, out in zip(refs[:half], refs[half:]):
        out[...] = dot(block[...], q_ref[...], ((1,), (1,)))


def last_score_body(q_ref, pair_ref, out):
    out[...] = dot(pair_ref[:, : q_ref.shape[1]], q_ref[...], ((1,), (1,)))


def weigh_body(
    groups, *refs
):
    parts, refs = refs[:groups], refs[groups:]
    q_ref, s0_ref, s1_ref, s2_ref, s3_ref, last_ref, w_ref, *refs = refs
    loss_ref, coef_ref, hard_out, swap_ref, term3_ref = refs
    rows, width = q_ref.shape
    w = w_ref[...]
    s3 = INV_TEMP * (s3_ref[...] + dot(last_ref[...], q_ref[...], ((1,), (1,))))
    scores = [INV_TEMP * s0_ref[...], INV_TEMP * s1_ref[...], INV_TEMP * s2_ref[...], s3]
    hard = parts[-1][...]
    for other in parts[-2::-1]:
        hard = hard + other[...]
    hard = INV_TEMP * hard
    largest = jnp.max(hard, axis=0, keepdims=True)
    for block in scores:
        largest = jnp.maximum(largest, jnp.max(block, axis=0, keepdims=True))
    summed = jnp.sum(jnp.exp(hard - largest), axis=0, keepdims=True)
    for block in scores:
        summed = summed + jnp.sum(jnp.exp(block - largest), axis=0, keepdims=True)
    log_total = largest + jnp.log(summed)
    for s, block in enumerate(scores):
        coef = (w * jnp.exp(block - log_total)).astype(BF16)
        coef_ref[:, s * rows : (s + 1) * rows] = coef
        if s in (1, 2):
            swap_ref[:, (s - 1) * rows : s * rows] = coef
    coef3 = coef_ref[:, 3 * rows :]
    for c in range(0, width, CHUNK):
        at = slice(c, c + CHUNK)
        term3_ref[:, at] = dot(coef3, q_ref[:, at], ((1,), (0,))).astype(BF16)
    hard_out[...] = (w * jnp.exp(hard - log_total)).astype(BF16).astype(F32)
    eye = lax.broadcasted_iota(jnp.int32, (rows, rows), 0) == lax.broadcasted_iota(
        jnp.int32, (rows, rows), 1
    )
    loss_ref[...] = log_total - jnp.sum(jnp.where(eye, scores[0], 0.0), axis=0, keepdims=True)


def sums_body(q_ref, pair_ref, coef_ref, swap_ref, sent3, partial1, token):
    signal(token)
    rows, width = q_ref.shape
    odd = lax.axis_index("blk") % 2 == 1
    mine = jnp.where(odd, coef_ref[:, rows : 2 * rows], coef_ref[:, 3 * rows :])
    coef = jnp.concatenate([mine, swap_ref[:, rows:]], axis=1)
    for c in range(0, width, CHUNK):
        at = slice(c, c + CHUNK)
        held = jnp.concatenate([q_ref[:, at], pair_ref[:, width + c : width + c + CHUNK]], axis=0)
        total = dot(coef, held, ((1,), (0,)))
        sent3[:, at] = total.astype(BF16)
        partial1[:, at] = total


def relay_body(partial1, got3_ref, out, done):
    signal(done)
    out[...] = (partial1[...] + got3_ref[...].astype(F32)).astype(BF16)


def base_body(
    q_ref, pair_ref, p_ref, n1_ref, e3_ref, o3_ref, coef_ref, swap_ref, w_ref, own3_ref,
    token, pulled, base, coef_t,
):
    rows, width = q_ref.shape
    w = jnp.broadcast_to(w_ref[...], (rows, rows)).T[:, :1]
    odd = lax.axis_index("blk") % 2 == 1
    blocks = (p_ref, n1_ref, pair_ref, e3_ref, o3_ref)
    for s in range(5):
        k = min(s, 3) * rows
        coef_t[:, s * rows : (s + 1) * rows] = coef_ref[:, k : k + rows].astype(F32).T.astype(BF16)
    coef = [coef_ref[:, :rows], jnp.where(odd, swap_ref[:, :rows], jnp.zeros((rows, rows), BF16))]
    coef = jnp.concatenate(coef, axis=1)
    for c in range(0, width, CHUNK):
        at = slice(c, c + CHUNK)
        held = jnp.concatenate([block[:, at] for block in blocks], axis=0)
        pulled[:, at] = dot(coef_t[...], held, ((1,), (0,))) - w * p_ref[:, at].astype(F32)
        held = jnp.concatenate([q_ref[:, at], pair_ref[:, width + c : width + c + CHUNK]], axis=0)
        own = dot(coef, held, ((1,), (0,))) + own3_ref[:, at].astype(F32)
        base[:, at] = own - w * q_ref[:, at].astype(F32)


def gather_body(groups, pulled, base, *refs):
    backs, (out, almost, held, sems) = refs[:groups][::-1], refs[groups:]
    rows, cols = pulled.shape[0], backs[0].shape[1]
    g = lax.axis_index("grp")
    copies = []
    for r, back in enumerate(backs):
        at = pl.ds(pl.multiple_of((g ^ r) * cols, 128), cols)
        held[:, at] = (INV_TEMP * (pulled[:, at] + back[:rows].astype(F32))).astype(BF16)
        copies.append(pltpu.make_async_copy(held.at[:, at], out.at[:, at], sems.at[r]))
        copies[-1].start()
        almost[:, at] = base[:, at] + back[rows:].astype(F32)
    for copy in copies:
        copy.wait()


def finish_body(almost, own1, out, held, sems):
    width = almost.shape[1]
    copies = []
    for n, c in enumerate(range(0, width, CHUNK)):
        at = slice(c, c + CHUNK)
        held[:, at] = (INV_TEMP * (almost[:, at] + own1[:, at].astype(F32))).astype(BF16)
        copies.append(pltpu.make_async_copy(held.at[:, at], out.at[:, at], sems.at[n]))
        copies[-1].start()
    for copy in copies:
        copy.wait()


def per_device(queries, passages, hard_index, weights):
    rows, width = queries.shape
    groups = lax.axis_size("grp")
    loop = lax.axis_size("blk")
    cols = width // groups

    def shift(array, by, which=(0, 1)):
        pairs = [(i, (i + by) % loop) for i in range(loop) if i % 2 in which]
        return lax.ppermute(array, "blk", pairs)

    def swap(array):
        return lax.ppermute(array, "blk", [(i, i ^ 1) for i in range(loop)])

    def over_groups(array, r):
        return lax.ppermute(array, "grp", [(i, i ^ r) for i in range(groups)])

    def exchange(arrays):
        out = list(arrays)
        for r in reversed(range(1, groups)):
            out[r] = over_groups(arrays[r], r)
        return out

    def like(*shape, dtype=BF16):
        return jax.ShapeDtypeStruct(shape, dtype)

    block, block32 = like(rows, width), like(rows, width, dtype=F32)
    square, triple = like(rows, rows, dtype=F32), like(3, rows, dtype=F32)
    piece, back = like(2 * rows + TAIL, cols), like(2 * rows, cols)

    next1 = shift(passages, -1)

    *pieces, token = local_call(
        functools.partial(load_body, groups, loop * rows), [piece] * groups + [TOKEN],
        queries, passages, hard_index.T, in_specs=[HBM, HBM, HBM],
        scratch=[pltpu.VMEM((3, rows), jnp.int32), pltpu.SemaphoreType.DMA((2 * groups + 1,))],
        limit=51,
    )
    pieces = exchange(pieces)

    (later_p,) = local_call(pass_body, [block], passages, token)
    next3_even = shift(later_p, -3, (1,))
    (next1,) = local_call(pass_body, [block], next1, token, flops=LONG)
    next3_odd = shift(next1, -2, (1,))
    pair = swap(
        local_call(choose_body, [like(rows, 2 * width)], next1, next3_even, queries, flops=LONG)[0]
    )

    s0, s1, s3 = local_call(scores_body, [square] * 3, queries, passages, next1, next3_even)
    parts = local_call(
        functools.partial(hard_scores_body, groups), [triple] * groups, pieces[-1], s0, *pieces[-2::-1], flops=LONG
    )
    (s2,) = local_call(last_score_body, [square], queries, pair)
    parts = exchange(parts)
    loss_rows, coef, hard_coef, to_core, term3 = local_call(
        functools.partial(weigh_body, groups),
        [like(1, rows, dtype=F32), like(rows, 4 * rows), triple, like(rows, 2 * rows), block],
        *parts[::-1], queries, s0, s1, s2, s3, next3_odd, weights[None, :],
    )

    got3 = shift(term3, 2, (1,))
    from_core = swap(to_core)
    sent3, partial1, token = local_call(
        sums_body, [block, block32, TOKEN], queries, pair, coef, from_core
    )
    own3 = shift(sent3, 3, (0,))

    hard_coefs = exchange([hard_coef] * groups)
    square_all = pltpu.VMEM((groups * rows, groups * rows), BF16)
    *backs, token = local_call(
        functools.partial(hard_grads_body, groups), [back] * groups + [TOKEN],
        *hard_coefs[::-1], *pieces[::-1], token, scratch=[square_all, square_all],
    )
    backs = exchange(backs)

    sent1, token = local_call(relay_body, [block, TOKEN], partial1, got3, flops=SOME)
    own1 = shift(sent1, 1, (1,))

    pulled, base = local_call(
        base_body, [block32, block32],
        queries, pair, passages, next1, next3_even, next3_odd, coef, from_core,
        weights[None, :], own3, token, flops=LONG, scratch=[pltpu.VMEM((rows, 5 * rows), BF16)],
    )
    held = pltpu.VMEM((rows, width), BF16)
    grad_queries, almost = local_call(
        functools.partial(gather_body, groups), [block, block32], pulled, base, *backs[::-1],
        out_specs=[HBM, VMEM], scratch=[held, pltpu.SemaphoreType.DMA((groups,))],
    )
    (grad_passages,) = local_call(
        finish_body, [block], almost, own1, out_specs=[HBM],
        scratch=[held, pltpu.SemaphoreType.DMA((width // CHUNK,))],
    )
    return loss_rows.reshape(rows), grad_queries, grad_passages


def solution(mesh):
    rows = P(("grp", "blk"))
    matrix = P(("grp", "blk"), None)
    return jax.shard_map(
        per_device,
        mesh=mesh,
        in_specs=(matrix, matrix, matrix, rows),
        out_specs=(rows, matrix, matrix),
        check_vma=False,
    )
```

```python
import functools
import math

import jax
import jax.numpy as jnp
from jax import lax
from jax.experimental import pallas as pl
from jax.experimental.pallas import tpu as pltpu
from jax.sharding import PartitionSpec as P

INV_TEMP = 50.0
BF16 = jnp.bfloat16
F32 = jnp.float32
CHUNK = 512
TAIL = 16
LONG, SOME = 5 * 10**10, 16 * 10**9
VMEM = pl.BlockSpec(memory_space=pltpu.VMEM)
HBM = pl.BlockSpec(memory_space=pltpu.HBM)
TOKEN = jax.ShapeDtypeStruct((8, 128), F32)


def dot(left, right, dims):
    return lax.dot_general(left, right, (dims, ((), ())), preferred_element_type=F32)


def size_of(arrays):
    return sum(math.prod(a.shape) * jnp.dtype(a.dtype).itemsize for a in arrays)


def local_call(body, out_shape, *args, flops=0, in_specs=None, out_specs=None, scratch=(), limit=20):
    return pl.pallas_call(
        body,
        out_shape=out_shape,
        in_specs=in_specs or [VMEM] * len(args),
        out_specs=out_specs or [VMEM] * len(out_shape),
        scratch_shapes=list(scratch),
        cost_estimate=pl.CostEstimate(
            flops=flops, bytes_accessed=size_of(args) + size_of(out_shape), transcendentals=0
        ),
        compiler_params=pltpu.CompilerParams(vmem_limit_bytes=limit * 2**20),
    )(*args)


def signal(token):
    token[...] = jnp.zeros(token.shape, token.dtype)


def split_index(index, rows, group_rows):
    if group_rows & (group_rows - 1) or rows & (rows - 1):
        return index // group_rows, index % rows
    return index >> (group_rows.bit_length() - 1), index & (rows - 1)


def load_body(groups, group_rows, q_hbm, p_hbm, index_hbm, *refs):
    pieces, (token, index_ref, sems) = refs[:groups], refs[groups:]
    rows = q_hbm.shape[0]
    cols = pieces[0].shape[1]
    g = lax.axis_index("grp")
    index_copy = pltpu.make_async_copy(index_hbm, index_ref, sems.at[2 * groups])
    index_copy.start()
    copies = []
    for r, piece in enumerate(pieces):
        at = pl.ds(pl.multiple_of((g ^ r) * cols, 128), cols)
        for n, source in enumerate((q_hbm, p_hbm)):
            target = piece.at[pl.ds(n * rows, rows)]
            copies.append(pltpu.make_async_copy(source.at[:, at], target, sems.at[2 * r + n]))
            copies[-1].start()
    signal(token)
    index_copy.wait()
    index = jnp.concatenate([index_ref[...], jnp.zeros((TAIL - 3, rows), jnp.int32)], axis=0)
    named_group, named_row = split_index(index, rows, group_rows)
    named_group = named_group.astype(F32).astype(BF16)
    named_row = named_row.astype(F32).astype(BF16)
    for piece in pieces:
        piece[2 * rows :, :rows] = named_group
        piece[2 * rows :, rows : 2 * rows] = named_row
        if cols > 2 * rows:
            piece[2 * rows :, 2 * rows :] = jnp.zeros((TAIL, cols - 2 * rows), BF16)
    for copy in copies:
        copy.wait()


def places_of(piece_ref, rows):
    tail = piece_ref[2 * rows :, : 2 * rows].astype(F32).astype(jnp.int32)
    g = lax.axis_index("grp")
    return [(tail[k : k + 1, :rows] ^ g) * rows + tail[k : k + 1, rows:] for k in range(3)]


def hard_scores_body(groups, *refs):
    pieces, outs = refs[:groups][::-1], refs[groups + 1 :]
    rows = outs[0].shape[1]
    ids = lax.broadcasted_iota(jnp.int32, (rows, rows), 0)
    for r in range(groups):
        others = [other for other in range(groups) if other != r]
        places = places_of(pieces[r], rows)
        held = jnp.concatenate([pieces[other][rows : 2 * rows] for other in others], axis=0)
        dots = dot(held, pieces[r][:rows], ((1,), (1,)))
        sums = [jnp.zeros((1, rows), F32) for _ in places]
        for n, other in enumerate(others):
            block = dots[n * rows : (n + 1) * rows]
            for k, place in enumerate(places):
                hit = jnp.where(ids == place - other * rows, block, 0.0)
                sums[k] += jnp.sum(hit, axis=0, keepdims=True)
        outs[r][...] = jnp.concatenate(sums, axis=0)


def hard_grads_body(groups, *refs):
    coefs, pieces, outs = refs[:groups][::-1], refs[groups : 2 * groups][::-1], refs[2 * groups + 1 : 3 * groups + 1]
    token, matrix, matrix_t = refs[3 * groups + 1 :]
    rows = coefs[0].shape[1]
    cols = outs[0].shape[1]
    signal(token)
    ids = lax.broadcasted_iota(jnp.int32, (groups * rows, rows), 0)
    for r in range(groups):
        places = places_of(pieces[r], rows)
        total = jnp.zeros(ids.shape, F32)
        for k in range(3):
            total += jnp.where(ids == places[k], coefs[r][k : k + 1], 0.0)
        mine = slice(r * rows, (r + 1) * rows)
        matrix[:, mine] = total.astype(BF16)
        matrix_t[mine] = total.T.astype(BF16)
    step = min(cols, 256)
    for c in range(0, cols, step):
        at = slice(c, c + step)
        q_all = jnp.concatenate([piece[:rows, at] for piece in pieces], axis=0)
        p_all = jnp.concatenate([piece[rows : 2 * rows, at] for piece in pieces], axis=0)
        grad_q = dot(matrix_t[...], p_all, ((1,), (0,))).astype(BF16)
        grad_p = dot(matrix[...], q_all, ((1,), (0,))).astype(BF16)
        for r in range(groups):
            mine = slice(r * rows, (r + 1) * rows)
            outs[r][:rows, at] = grad_q[mine]
            outs[r][rows:, at] = grad_p[mine]


def pass_body(source, token, out):
    out[...] = source[...]


def choose_body(n1_ref, e3_ref, q_ref, out):
    width = q_ref.shape[1]
    odd = lax.axis_index("blk") % 2 == 1
    out[:, width:] = q_ref[...]

    @pl.when(odd)
    def _():
        out[:, :width] = n1_ref[...]

    @pl.when(jnp.logical_not(odd))
    def _():
        out[:, :width] = e3_ref[...]


def scores_body(q_ref, *refs):
    half = len(refs) // 2
    for block, out in zip(refs[:half], refs[half:]):
        out[...] = dot(block[...], q_ref[...], ((1,), (1,)))


def last_score_body(q_ref, pair_ref, out):
    out[...] = dot(pair_ref[:, : q_ref.shape[1]], q_ref[...], ((1,), (1,)))


def hard_total(parts):
    total = parts[-1][...]
    for other in parts[-2::-1]:
        total = total + other[...]
    return INV_TEMP * total


def first_sum_body(groups, *refs):
    parts, refs = refs[:groups], refs[groups:]
    q_ref, s0_ref, s1_ref, s2_ref, s3_ref, last_ref, w_ref, total_ref, whole3_ref, term3_ref = refs
    width = q_ref.shape[1]
    s3 = INV_TEMP * (s3_ref[...] + dot(last_ref[...], q_ref[...], ((1,), (1,))))
    scores = [INV_TEMP * s0_ref[...], INV_TEMP * s1_ref[...], INV_TEMP * s2_ref[...], s3]
    hard = hard_total(parts)
    largest = jnp.max(hard, axis=0, keepdims=True)
    for block in scores:
        largest = jnp.maximum(largest, jnp.max(block, axis=0, keepdims=True))
    summed = jnp.sum(jnp.exp(hard - largest), axis=0, keepdims=True)
    for block in scores:
        summed = summed + jnp.sum(jnp.exp(block - largest), axis=0, keepdims=True)
    log_total = largest + jnp.log(summed)
    total_ref[...] = log_total
    whole3_ref[...] = s3
    coef3 = (w_ref[...] * jnp.exp(s3 - log_total)).astype(BF16)
    for c in range(0, width, CHUNK):
        at = slice(c, c + CHUNK)
        term3_ref[:, at] = dot(coef3, q_ref[:, at], ((1,), (0,))).astype(BF16)


def weigh_body(groups, *refs):
    parts, refs = refs[:groups], refs[groups:]
    s0_ref, s1_ref, s2_ref, whole3_ref, total_ref, w_ref, *refs = refs
    loss_ref, coef_ref, hard_out, swap_ref = refs
    rows = s0_ref.shape[0]
    w, log_total = w_ref[...], total_ref[...]
    hard_out[...] = (w * jnp.exp(hard_total(parts) - log_total)).astype(BF16).astype(F32)
    scores = [INV_TEMP * s0_ref[...], INV_TEMP * s1_ref[...], INV_TEMP * s2_ref[...]]
    for s, block in enumerate(scores + [whole3_ref[...]]):
        coef = (w * jnp.exp(block - log_total)).astype(BF16)
        coef_ref[:, s * rows : (s + 1) * rows] = coef
        if s in (1, 2):
            swap_ref[:, (s - 1) * rows : s * rows] = coef
    eye = lax.broadcasted_iota(jnp.int32, (rows, rows), 0) == lax.broadcasted_iota(
        jnp.int32, (rows, rows), 1
    )
    loss_ref[...] = log_total - jnp.sum(jnp.where(eye, scores[0], 0.0), axis=0, keepdims=True)


def sums_body(q_ref, pair_ref, coef_ref, swap_ref, sent3, partial1, token):
    signal(token)
    rows, width = q_ref.shape
    odd = lax.axis_index("blk") % 2 == 1
    mine = jnp.where(odd, coef_ref[:, rows : 2 * rows], coef_ref[:, 3 * rows :])
    coef = jnp.concatenate([mine, swap_ref[:, rows:]], axis=1)
    for c in range(0, width, CHUNK):
        at = slice(c, c + CHUNK)
        held = jnp.concatenate([q_ref[:, at], pair_ref[:, width + c : width + c + CHUNK]], axis=0)
        total = dot(coef, held, ((1,), (0,)))
        sent3[:, at] = total.astype(BF16)
        partial1[:, at] = total


def relay_body(partial1, got3_ref, out, done):
    signal(done)
    out[...] = (partial1[...] + got3_ref[...].astype(F32)).astype(BF16)


def base_body(
    q_ref, pair_ref, p_ref, n1_ref, e3_ref, o3_ref, coef_ref, swap_ref, w_ref, own3_ref,
    token, pulled, base, coef_t,
):
    rows, width = q_ref.shape
    w = jnp.broadcast_to(w_ref[...], (rows, rows)).T[:, :1]
    odd = lax.axis_index("blk") % 2 == 1
    blocks = (p_ref, n1_ref, pair_ref, e3_ref, o3_ref)
    for s in range(5):
        k = min(s, 3) * rows
        coef_t[:, s * rows : (s + 1) * rows] = coef_ref[:, k : k + rows].astype(F32).T.astype(BF16)
    coef = [coef_ref[:, :rows], jnp.where(odd, swap_ref[:, :rows], jnp.zeros((rows, rows), BF16))]
    coef = jnp.concatenate(coef, axis=1)
    for c in range(0, width, CHUNK):
        at = slice(c, c + CHUNK)
        held = jnp.concatenate([block[:, at] for block in blocks], axis=0)
        pulled[:, at] = dot(coef_t[...], held, ((1,), (0,))) - w * p_ref[:, at].astype(F32)
        held = jnp.concatenate([q_ref[:, at], pair_ref[:, width + c : width + c + CHUNK]], axis=0)
        own = dot(coef, held, ((1,), (0,))) + own3_ref[:, at].astype(F32)
        base[:, at] = own - w * q_ref[:, at].astype(F32)


def gather_body(groups, pulled, base, *refs):
    backs, (out, almost, held, sems) = refs[:groups][::-1], refs[groups:]
    rows, cols = pulled.shape[0], backs[0].shape[1]
    g = lax.axis_index("grp")
    copies = []
    for r, back in enumerate(backs):
        at = pl.ds(pl.multiple_of((g ^ r) * cols, 128), cols)
        held[:, at] = (INV_TEMP * (pulled[:, at] + back[:rows].astype(F32))).astype(BF16)
        copies.append(pltpu.make_async_copy(held.at[:, at], out.at[:, at], sems.at[r]))
        copies[-1].start()
        almost[:, at] = base[:, at] + back[rows:].astype(F32)
    for copy in copies:
        copy.wait()


def finish_body(almost, own1, out, held, sems):
    width = almost.shape[1]
    copies = []
    for n, c in enumerate(range(0, width, CHUNK)):
        at = slice(c, c + CHUNK)
        held[:, at] = (INV_TEMP * (almost[:, at] + own1[:, at].astype(F32))).astype(BF16)
        copies.append(pltpu.make_async_copy(held.at[:, at], out.at[:, at], sems.at[n]))
        copies[-1].start()
    for copy in copies:
        copy.wait()


def per_device(queries, passages, hard_index, weights):
    rows, width = queries.shape
    groups = lax.axis_size("grp")
    loop = lax.axis_size("blk")
    cols = width // groups

    def shift(array, by, which=(0, 1)):
        pairs = [(i, (i + by) % loop) for i in range(loop) if i % 2 in which]
        return lax.ppermute(array, "blk", pairs)

    def swap(array):
        return lax.ppermute(array, "blk", [(i, i ^ 1) for i in range(loop)])

    def over_groups(array, r):
        return lax.ppermute(array, "grp", [(i, i ^ r) for i in range(groups)])

    def exchange(arrays):
        out = list(arrays)
        for r in reversed(range(1, groups)):
            out[r] = over_groups(arrays[r], r)
        return out

    def like(*shape, dtype=BF16):
        return jax.ShapeDtypeStruct(shape, dtype)

    block, block32 = like(rows, width), like(rows, width, dtype=F32)
    square, triple = like(rows, rows, dtype=F32), like(3, rows, dtype=F32)
    piece, back = like(2 * rows + TAIL, cols), like(2 * rows, cols)

    next1 = shift(passages, -1)

    *pieces, token = local_call(
        functools.partial(load_body, groups, loop * rows), [piece] * groups + [TOKEN],
        queries, passages, hard_index.T, in_specs=[HBM, HBM, HBM],
        scratch=[pltpu.VMEM((3, rows), jnp.int32), pltpu.SemaphoreType.DMA((2 * groups + 1,))],
        limit=51,
    )
    pieces = exchange(pieces)

    (later_p,) = local_call(pass_body, [block], passages, token)
    next3_even = shift(later_p, -3, (1,))
    (next1,) = local_call(pass_body, [block], next1, token, flops=LONG)
    next3_odd = shift(next1, -2, (1,))
    pair = swap(
        local_call(choose_body, [like(rows, 2 * width)], next1, next3_even, queries, flops=LONG)[0]
    )

    s0, s1, s3 = local_call(scores_body, [square] * 3, queries, passages, next1, next3_even)
    parts = local_call(
        functools.partial(hard_scores_body, groups), [triple] * groups, *pieces[::-1], s0, flops=LONG
    )
    (s2,) = local_call(last_score_body, [square], queries, pair)
    parts = exchange(parts)
    one_row = like(1, rows, dtype=F32)
    log_total, whole3, term3 = local_call(
        functools.partial(first_sum_body, groups), [one_row, square, block],
        *parts[::-1], queries, s0, s1, s2, s3, next3_odd, weights[None, :],
    )
    loss_rows, coef, hard_coef, to_core = local_call(
        functools.partial(weigh_body, groups),
        [one_row, like(rows, 4 * rows), triple, like(rows, 2 * rows)],
        *parts[::-1], s0, s1, s2, whole3, log_total, weights[None, :],
    )

    got3 = shift(term3, 2, (1,))
    from_core = swap(to_core)
    sent3, partial1, token = local_call(
        sums_body, [block, block32, TOKEN], queries, pair, coef, from_core
    )
    own3 = shift(sent3, 3, (0,))

    hard_coefs = exchange([hard_coef] * groups)
    square_all = pltpu.VMEM((groups * rows, groups * rows), BF16)
    *backs, token = local_call(
        functools.partial(hard_grads_body, groups), [back] * groups + [TOKEN],
        *hard_coefs[::-1], *pieces[::-1], token, scratch=[square_all, square_all],
    )
    backs = exchange(backs)

    sent1, token = local_call(relay_body, [block, TOKEN], partial1, got3, flops=SOME)
    own1 = shift(sent1, 1, (1,))

    pulled, base = local_call(
        base_body, [block32, block32],
        queries, pair, passages, next1, next3_even, next3_odd, coef, from_core,
        weights[None, :], own3, token, flops=LONG, scratch=[pltpu.VMEM((rows, 5 * rows), BF16)],
    )
    held = pltpu.VMEM((rows, width), BF16)
    grad_queries, almost = local_call(
        functools.partial(gather_body, groups), [block, block32], pulled, base, *backs[::-1],
        out_specs=[HBM, VMEM], scratch=[held, pltpu.SemaphoreType.DMA((groups,))],
    )
    (grad_passages,) = local_call(
        finish_body, [block], almost, own1, out_specs=[HBM],
        scratch=[held, pltpu.SemaphoreType.DMA((width // CHUNK,))],
    )
    return loss_rows.reshape(rows), grad_queries, grad_passages


def solution(mesh):
    rows = P(("grp", "blk"))
    matrix = P(("grp", "blk"), None)
    return jax.shard_map(
        per_device,
        mesh=mesh,
        in_specs=(matrix, matrix, matrix, rows),
        out_specs=(rows, matrix, matrix),
        check_vma=False,
    )
```

```python
import functools
import math

import jax
import jax.numpy as jnp
from jax import lax
from jax.experimental import pallas as pl
from jax.experimental.pallas import tpu as pltpu
from jax.sharding import PartitionSpec as P

INV_TEMP = 50.0
BF16 = jnp.bfloat16
F32 = jnp.float32
CHUNK = 512
TAIL = 16
LONG, SOME = 5 * 10**10, 10 * 10**9
VMEM = pl.BlockSpec(memory_space=pltpu.VMEM)
HBM = pl.BlockSpec(memory_space=pltpu.HBM)
TOKEN = jax.ShapeDtypeStruct((8, 128), F32)


def dot(left, right, dims):
    return lax.dot_general(left, right, (dims, ((), ())), preferred_element_type=F32)


def size_of(arrays):
    return sum(math.prod(a.shape) * jnp.dtype(a.dtype).itemsize for a in arrays)


def local_call(body, out_shape, *args, flops=0, in_specs=None, out_specs=None, scratch=(), limit=20):
    return pl.pallas_call(
        body,
        out_shape=out_shape,
        in_specs=in_specs or [VMEM] * len(args),
        out_specs=out_specs or [VMEM] * len(out_shape),
        scratch_shapes=list(scratch),
        cost_estimate=pl.CostEstimate(
            flops=flops, bytes_accessed=size_of(args) + size_of(out_shape), transcendentals=0
        ),
        compiler_params=pltpu.CompilerParams(vmem_limit_bytes=limit * 2**20),
    )(*args)


def signal(token):
    token[...] = jnp.zeros(token.shape, token.dtype)


def split_index(index, rows, group_rows):
    if group_rows & (group_rows - 1) or rows & (rows - 1):
        return index // group_rows, index % rows
    return index >> (group_rows.bit_length() - 1), index & (rows - 1)


def load_body(groups, group_rows, q_hbm, p_hbm, index_hbm, *refs):
    pieces, (token, index_ref, sems) = refs[:groups], refs[groups:]
    rows = q_hbm.shape[0]
    cols = pieces[0].shape[1]
    g = lax.axis_index("grp")
    index_copy = pltpu.make_async_copy(index_hbm, index_ref, sems.at[2 * groups])
    index_copy.start()
    copies = []
    for r, piece in enumerate(pieces):
        at = pl.ds(pl.multiple_of((g ^ r) * cols, 128), cols)
        for n, source in enumerate((q_hbm, p_hbm)):
            target = piece.at[pl.ds(n * rows, rows)]
            copies.append(pltpu.make_async_copy(source.at[:, at], target, sems.at[2 * r + n]))
            copies[-1].start()
    signal(token)
    index_copy.wait()
    index = jnp.concatenate([index_ref[...], jnp.zeros((TAIL - 3, rows), jnp.int32)], axis=0)
    named_group, named_row = split_index(index, rows, group_rows)
    named_group = named_group.astype(F32).astype(BF16)
    named_row = named_row.astype(F32).astype(BF16)
    for piece in pieces:
        piece[2 * rows :, :rows] = named_group
        piece[2 * rows :, rows : 2 * rows] = named_row
        if cols > 2 * rows:
            piece[2 * rows :, 2 * rows :] = jnp.zeros((TAIL, cols - 2 * rows), BF16)
    for copy in copies:
        copy.wait()


def places_of(piece_ref, rows):
    tail = piece_ref[2 * rows :, : 2 * rows].astype(F32).astype(jnp.int32)
    g = lax.axis_index("grp")
    return [(tail[k : k + 1, :rows] ^ g) * rows + tail[k : k + 1, rows:] for k in range(3)]


def hard_scores_body(groups, *refs):
    pieces, outs = refs[:groups][::-1], refs[groups + 1 :]
    rows = outs[0].shape[1]
    ids = lax.broadcasted_iota(jnp.int32, (rows, rows), 0)
    for r in range(groups):
        others = [other for other in range(groups) if other != r]
        places = places_of(pieces[r], rows)
        held = jnp.concatenate([pieces[other][rows : 2 * rows] for other in others], axis=0)
        dots = dot(held, pieces[r][:rows], ((1,), (1,)))
        sums = [jnp.zeros((1, rows), F32) for _ in places]
        for n, other in enumerate(others):
            block = dots[n * rows : (n + 1) * rows]
            for k, place in enumerate(places):
                hit = jnp.where(ids == place - other * rows, block, 0.0)
                sums[k] += jnp.sum(hit, axis=0, keepdims=True)
        outs[r][...] = jnp.concatenate(sums, axis=0)


def hard_grads_body(groups, *refs):
    coefs, pieces, outs = refs[:groups][::-1], refs[groups : 2 * groups][::-1], refs[2 * groups + 1 : 3 * groups + 1]
    token, matrix, matrix_t = refs[3 * groups + 1 :]
    rows = coefs[0].shape[1]
    cols = outs[0].shape[1]
    signal(token)
    ids = lax.broadcasted_iota(jnp.int32, (groups * rows, rows), 0)
    for r in range(groups):
        places = places_of(pieces[r], rows)
        total = jnp.zeros(ids.shape, F32)
        for k in range(3):
            total += jnp.where(ids == places[k], coefs[r][k : k + 1], 0.0)
        mine = slice(r * rows, (r + 1) * rows)
        matrix[:, mine] = total.astype(BF16)
        matrix_t[mine] = total.T.astype(BF16)
    step = min(cols, 256)
    for c in range(0, cols, step):
        at = slice(c, c + step)
        q_all = jnp.concatenate([piece[:rows, at] for piece in pieces], axis=0)
        p_all = jnp.concatenate([piece[rows : 2 * rows, at] for piece in pieces], axis=0)
        grad_q = dot(matrix_t[...], p_all, ((1,), (0,))).astype(BF16)
        grad_p = dot(matrix[...], q_all, ((1,), (0,))).astype(BF16)
        for r in range(groups):
            mine = slice(r * rows, (r + 1) * rows)
            outs[r][:rows, at] = grad_q[mine]
            outs[r][rows:, at] = grad_p[mine]


def pass_body(source, token, out):
    out[...] = source[...]


def choose_body(n1_ref, e3_ref, q_ref, out):
    width = q_ref.shape[1]
    odd = lax.axis_index("blk") % 2 == 1
    out[:, width:] = q_ref[...]

    @pl.when(odd)
    def _():
        out[:, :width] = n1_ref[...]

    @pl.when(jnp.logical_not(odd))
    def _():
        out[:, :width] = e3_ref[...]


def scores_body(q_ref, *refs):
    half = len(refs) // 2
    for block, out in zip(refs[:half], refs[half:]):
        out[...] = dot(block[...], q_ref[...], ((1,), (1,)))


def last_score_body(q_ref, pair_ref, out):
    out[...] = dot(pair_ref[:, : q_ref.shape[1]], q_ref[...], ((1,), (1,)))


def weigh_body(
    groups, *refs
):
    parts, refs = refs[:groups], refs[groups:]
    q_ref, s0_ref, s1_ref, s2_ref, s3_ref, last_ref, w_ref, *refs = refs
    loss_ref, coef_ref, hard_out, swap_ref, term3_ref = refs
    rows, width = q_ref.shape
    w = w_ref[...]
    s3 = INV_TEMP * (s3_ref[...] + dot(last_ref[...], q_ref[...], ((1,), (1,))))
    scores = [INV_TEMP * s0_ref[...], INV_TEMP * s1_ref[...], INV_TEMP * s2_ref[...], s3]
    hard = parts[-1][...]
    for other in parts[-2::-1]:
        hard = hard + other[...]
    hard = INV_TEMP * hard
    largest = jnp.max(hard, axis=0, keepdims=True)
    for block in scores:
        largest = jnp.maximum(largest, jnp.max(block, axis=0, keepdims=True))
    summed = jnp.sum(jnp.exp(hard - largest), axis=0, keepdims=True)
    for block in scores:
        summed = summed + jnp.sum(jnp.exp(block - largest), axis=0, keepdims=True)
    log_total = largest + jnp.log(summed)
    for s, block in enumerate(scores):
        coef = (w * jnp.exp(block - log_total)).astype(BF16)
        coef_ref[:, s * rows : (s + 1) * rows] = coef
        if s in (1, 2):
            swap_ref[:, (s - 1) * rows : s * rows] = coef
    coef3 = coef_ref[:, 3 * rows :]
    for c in range(0, width, CHUNK):
        at = slice(c, c + CHUNK)
        term3_ref[:, at] = dot(coef3, q_ref[:, at], ((1,), (0,))).astype(BF16)
    hard_out[...] = (w * jnp.exp(hard - log_total)).astype(BF16).astype(F32)
    eye = lax.broadcasted_iota(jnp.int32, (rows, rows), 0) == lax.broadcasted_iota(
        jnp.int32, (rows, rows), 1
    )
    loss_ref[...] = log_total - jnp.sum(jnp.where(eye, scores[0], 0.0), axis=0, keepdims=True)


def sums_body(q_ref, pair_ref, coef_ref, swap_ref, sent3, partial1, token):
    signal(token)
    rows, width = q_ref.shape
    odd = lax.axis_index("blk") % 2 == 1
    mine = jnp.where(odd, coef_ref[:, rows : 2 * rows], coef_ref[:, 3 * rows :])
    coef = jnp.concatenate([mine, swap_ref[:, rows:]], axis=1)
    for c in range(0, width, CHUNK):
        at = slice(c, c + CHUNK)
        held = jnp.concatenate([q_ref[:, at], pair_ref[:, width + c : width + c + CHUNK]], axis=0)
        total = dot(coef, held, ((1,), (0,)))
        sent3[:, at] = total.astype(BF16)
        partial1[:, at] = total


def relay_body(partial1, got3_ref, out, done):
    signal(done)
    out[...] = (partial1[...] + got3_ref[...].astype(F32)).astype(BF16)


def base_body(
    q_ref, pair_ref, p_ref, n1_ref, e3_ref, o3_ref, coef_ref, swap_ref, w_ref, own3_ref,
    token, got3_ref, pulled, base, coef_t,
):
    rows, width = q_ref.shape
    w = jnp.broadcast_to(w_ref[...], (rows, rows)).T[:, :1]
    odd = lax.axis_index("blk") % 2 == 1
    blocks = (p_ref, n1_ref, pair_ref, e3_ref, o3_ref)
    for s in range(5):
        k = min(s, 3) * rows
        coef_t[:, s * rows : (s + 1) * rows] = coef_ref[:, k : k + rows].astype(F32).T.astype(BF16)
    coef = [coef_ref[:, :rows], jnp.where(odd, swap_ref[:, :rows], jnp.zeros((rows, rows), BF16))]
    coef = jnp.concatenate(coef, axis=1)
    for c in range(0, width, CHUNK):
        at = slice(c, c + CHUNK)
        held = jnp.concatenate([block[:, at] for block in blocks], axis=0)
        pulled[:, at] = dot(coef_t[...], held, ((1,), (0,))) - w * p_ref[:, at].astype(F32)
        held = jnp.concatenate([q_ref[:, at], pair_ref[:, width + c : width + c + CHUNK]], axis=0)
        came = jnp.where(odd, 0.0, got3_ref[:, at].astype(F32)) + own3_ref[:, at].astype(F32)
        own = dot(coef, held, ((1,), (0,))) + came
        base[:, at] = own - w * q_ref[:, at].astype(F32)


def gather_body(groups, pulled, base, *refs):
    backs, (out, almost, held, sems) = refs[:groups][::-1], refs[groups:]
    rows, cols = pulled.shape[0], backs[0].shape[1]
    g = lax.axis_index("grp")
    copies = []
    for r, back in enumerate(backs):
        at = pl.ds(pl.multiple_of((g ^ r) * cols, 128), cols)
        held[:, at] = (INV_TEMP * (pulled[:, at] + back[:rows].astype(F32))).astype(BF16)
        copies.append(pltpu.make_async_copy(held.at[:, at], out.at[:, at], sems.at[r]))
        copies[-1].start()
        almost[:, at] = base[:, at] + back[rows:].astype(F32)
    for copy in copies:
        copy.wait()


def finish_body(almost, own1, out, held, sems):
    width = almost.shape[1]
    copies = []
    for n, c in enumerate(range(0, width, CHUNK)):
        at = slice(c, c + CHUNK)
        held[:, at] = (INV_TEMP * (almost[:, at] + own1[:, at].astype(F32))).astype(BF16)
        copies.append(pltpu.make_async_copy(held.at[:, at], out.at[:, at], sems.at[n]))
        copies[-1].start()
    for copy in copies:
        copy.wait()


def per_device(queries, passages, hard_index, weights):
    rows, width = queries.shape
    groups = lax.axis_size("grp")
    loop = lax.axis_size("blk")
    cols = width // groups

    def pairs_of(by, which=(0, 1)):
        return [(i, (i + by) % loop) for i in range(loop) if i % 2 in which]

    def shift(array, by, which=(0, 1)):
        return lax.ppermute(array, "blk", pairs_of(by, which))

    def swap(array):
        return lax.ppermute(array, "blk", [(i, i ^ 1) for i in range(loop)])

    def over_groups(array, r):
        return lax.ppermute(array, "grp", [(i, i ^ r) for i in range(groups)])

    def exchange(arrays):
        out = list(arrays)
        for r in reversed(range(1, groups)):
            out[r] = over_groups(arrays[r], r)
        return out

    def like(*shape, dtype=BF16):
        return jax.ShapeDtypeStruct(shape, dtype)

    block, block32 = like(rows, width), like(rows, width, dtype=F32)
    square, triple = like(rows, rows, dtype=F32), like(3, rows, dtype=F32)
    piece, back = like(2 * rows + TAIL, cols), like(2 * rows, cols)

    next1 = shift(passages, -1)

    *pieces, token = local_call(
        functools.partial(load_body, groups, loop * rows), [piece] * groups + [TOKEN],
        queries, passages, hard_index.T, in_specs=[HBM, HBM, HBM],
        scratch=[pltpu.VMEM((3, rows), jnp.int32), pltpu.SemaphoreType.DMA((2 * groups + 1,))],
        limit=51,
    )
    pieces = exchange(pieces)

    (later_p,) = local_call(pass_body, [block], passages, token)
    next3_even = shift(later_p, -3, (1,))
    (next1,) = local_call(pass_body, [block], next1, token, flops=LONG)
    next3_odd = shift(next1, -2, (1,))
    pair = swap(
        local_call(choose_body, [like(rows, 2 * width)], next1, next3_even, queries, flops=LONG)[0]
    )

    s0, s1, s3 = local_call(scores_body, [square] * 3, queries, passages, next1, next3_even)
    parts = local_call(
        functools.partial(hard_scores_body, groups), [triple] * groups, *pieces[::-1], s0, flops=LONG
    )
    (s2,) = local_call(last_score_body, [square], queries, pair)
    parts = exchange(parts)
    loss_rows, coef, hard_coef, to_core, term3 = local_call(
        functools.partial(weigh_body, groups),
        [like(1, rows, dtype=F32), like(rows, 4 * rows), triple, like(rows, 2 * rows), block],
        *parts[::-1], queries, s0, s1, s2, s3, next3_odd, weights[None, :],
    )

    got3 = lax.ppermute(term3, "blk", pairs_of(2, (1,))[:-1] + [(loop - 1, 2)])
    from_core = swap(to_core)
    sent3, partial1, token = local_call(
        sums_body, [block, block32, TOKEN], queries, pair, coef, from_core
    )
    own3 = shift(sent3, 3, (0,))

    hard_coefs = exchange([hard_coef] * groups)
    square_all = pltpu.VMEM((groups * rows, groups * rows), BF16)
    *backs, token = local_call(
        functools.partial(hard_grads_body, groups), [back] * groups + [TOKEN],
        *hard_coefs[::-1], *pieces[::-1], token, scratch=[square_all, square_all],
    )
    backs = exchange(backs)

    sent1, token = local_call(relay_body, [block, TOKEN], partial1, got3, flops=SOME)
    own1 = shift(sent1, 1, (1,))

    pulled, base = local_call(
        base_body, [block32, block32],
        queries, pair, passages, next1, next3_even, next3_odd, coef, from_core,
        weights[None, :], own3, token, got3, flops=LONG, scratch=[pltpu.VMEM((rows, 5 * rows), BF16)],
    )
    held = pltpu.VMEM((rows, width), BF16)
    grad_queries, almost = local_call(
        functools.partial(gather_body, groups), [block, block32], pulled, base, *backs[::-1],
        out_specs=[HBM, VMEM], scratch=[held, pltpu.SemaphoreType.DMA((groups,))],
    )
    (grad_passages,) = local_call(
        finish_body, [block], almost, own1, out_specs=[HBM],
        scratch=[held, pltpu.SemaphoreType.DMA((width // CHUNK,))],
    )
    return loss_rows.reshape(rows), grad_queries, grad_passages


def solution(mesh):
    rows = P(("grp", "blk"))
    matrix = P(("grp", "blk"), None)
    return jax.shard_map(
        per_device,
        mesh=mesh,
        in_specs=(matrix, matrix, matrix, rows),
        out_specs=(rows, matrix, matrix),
        check_vma=False,
    )
```

```python
import functools
import math

import jax
import jax.numpy as jnp
from jax import lax
from jax.experimental import pallas as pl
from jax.experimental.pallas import tpu as pltpu
from jax.sharding import PartitionSpec as P

INV_TEMP = 50.0
BF16 = jnp.bfloat16
F32 = jnp.float32
CHUNK = 512
TAIL = 16
LONG, SOME = 5 * 10**10, 10 * 10**9
VMEM = pl.BlockSpec(memory_space=pltpu.VMEM)
HBM = pl.BlockSpec(memory_space=pltpu.HBM)
TOKEN = jax.ShapeDtypeStruct((8, 128), F32)


def dot(left, right, dims):
    return lax.dot_general(left, right, (dims, ((), ())), preferred_element_type=F32)


def size_of(arrays):
    return sum(math.prod(a.shape) * jnp.dtype(a.dtype).itemsize for a in arrays)


def local_call(body, out_shape, *args, flops=0, in_specs=None, out_specs=None, scratch=(), limit=20):
    return pl.pallas_call(
        body,
        out_shape=out_shape,
        in_specs=in_specs or [VMEM] * len(args),
        out_specs=out_specs or [VMEM] * len(out_shape),
        scratch_shapes=list(scratch),
        cost_estimate=pl.CostEstimate(
            flops=flops, bytes_accessed=size_of(args) + size_of(out_shape), transcendentals=0
        ),
        compiler_params=pltpu.CompilerParams(vmem_limit_bytes=limit * 2**20),
    )(*args)


def signal(token):
    token[...] = jnp.zeros(token.shape, token.dtype)


def split_index(index, rows, group_rows):
    if group_rows & (group_rows - 1) or rows & (rows - 1):
        return index // group_rows, index % rows
    return index >> (group_rows.bit_length() - 1), index & (rows - 1)


def load_body(groups, group_rows, q_hbm, p_hbm, index_hbm, *refs):
    pieces, (token, index_ref, sems) = refs[:groups], refs[groups:]
    rows = q_hbm.shape[0]
    cols = pieces[0].shape[1]
    g = lax.axis_index("grp")
    index_copy = pltpu.make_async_copy(index_hbm, index_ref, sems.at[2 * groups])
    index_copy.start()
    copies = []
    for r, piece in enumerate(pieces):
        at = pl.ds(pl.multiple_of((g ^ r) * cols, 128), cols)
        for n, source in enumerate((q_hbm, p_hbm)):
            target = piece.at[pl.ds(n * rows, rows)]
            copies.append(pltpu.make_async_copy(source.at[:, at], target, sems.at[2 * r + n]))
            copies[-1].start()
    signal(token)
    index_copy.wait()
    index = jnp.concatenate([index_ref[...], jnp.zeros((TAIL - 3, rows), jnp.int32)], axis=0)
    named_group, named_row = split_index(index, rows, group_rows)
    named_group = named_group.astype(F32).astype(BF16)
    named_row = named_row.astype(F32).astype(BF16)
    for piece in pieces:
        piece[2 * rows :, :rows] = named_group
        piece[2 * rows :, rows : 2 * rows] = named_row
        if cols > 2 * rows:
            piece[2 * rows :, 2 * rows :] = jnp.zeros((TAIL, cols - 2 * rows), BF16)
    for copy in copies:
        copy.wait()


def places_of(piece_ref, rows):
    tail = piece_ref[2 * rows :, : 2 * rows].astype(F32).astype(jnp.int32)
    g = lax.axis_index("grp")
    return [(tail[k : k + 1, :rows] ^ g) * rows + tail[k : k + 1, rows:] for k in range(3)]


def hard_scores_body(groups, *refs):
    pieces, outs = refs[:groups][::-1], refs[groups + 1 :]
    rows = outs[0].shape[1]
    ids = lax.broadcasted_iota(jnp.int32, (rows, rows), 0)
    for r in range(groups):
        others = [other for other in range(groups) if other != r]
        places = places_of(pieces[r], rows)
        held = jnp.concatenate([pieces[other][rows : 2 * rows] for other in others], axis=0)
        dots = dot(held, pieces[r][:rows], ((1,), (1,)))
        sums = [jnp.zeros((1, rows), F32) for _ in places]
        for n, other in enumerate(others):
            block = dots[n * rows : (n + 1) * rows]
            for k, place in enumerate(places):
                hit = jnp.where(ids == place - other * rows, block, 0.0)
                sums[k] += jnp.sum(hit, axis=0, keepdims=True)
        outs[r][...] = jnp.concatenate(sums, axis=0)


def hard_grads_body(groups, *refs):
    coefs, pieces, outs = refs[:groups], refs[groups : 2 * groups][::-1], refs[2 * groups + 1 : 3 * groups + 1]
    token, matrix, matrix_t = refs[3 * groups + 1 :]
    rows = coefs[0].shape[1]
    cols = outs[0].shape[1]
    signal(token)
    ids = lax.broadcasted_iota(jnp.int32, (groups * rows, rows), 0)
    for r in range(groups):
        places = places_of(pieces[r], rows)
        total = jnp.zeros(ids.shape, F32)
        for k in range(3):
            total += jnp.where(ids == places[k], coefs[r][k : k + 1], 0.0)
        mine = slice(r * rows, (r + 1) * rows)
        matrix[:, mine] = total.astype(BF16)
        matrix_t[mine] = total.T.astype(BF16)
    step = min(cols, 256)
    for c in range(0, cols, step):
        at = slice(c, c + step)
        q_all = jnp.concatenate([piece[:rows, at] for piece in pieces], axis=0)
        p_all = jnp.concatenate([piece[rows : 2 * rows, at] for piece in pieces], axis=0)
        grad_q = dot(matrix_t[...], p_all, ((1,), (0,))).astype(BF16)
        grad_p = dot(matrix[...], q_all, ((1,), (0,))).astype(BF16)
        for r in range(groups):
            mine = slice(r * rows, (r + 1) * rows)
            outs[r][:rows, at] = grad_q[mine]
            outs[r][rows:, at] = grad_p[mine]


def pass_body(source, token, out):
    out[...] = source[...]


def choose_body(n1_ref, e3_ref, q_ref, out):
    width = q_ref.shape[1]
    odd = lax.axis_index("blk") % 2 == 1
    out[:, width:] = q_ref[...]

    @pl.when(odd)
    def _():
        out[:, :width] = n1_ref[...]

    @pl.when(jnp.logical_not(odd))
    def _():
        out[:, :width] = e3_ref[...]


def scores_body(q_ref, *refs):
    half = len(refs) // 2
    for block, out in zip(refs[:half], refs[half:]):
        out[...] = dot(block[...], q_ref[...], ((1,), (1,)))


def last_score_body(q_ref, pair_ref, out):
    out[...] = dot(pair_ref[:, : q_ref.shape[1]], q_ref[...], ((1,), (1,)))


def hard_total(parts):
    total = parts[-1][...]
    for other in parts[-2::-1]:
        total = total + other[...]
    return INV_TEMP * total


def first_sum_body(groups, *refs):
    parts, refs = refs[:groups], refs[groups:]
    q_ref, s0_ref, s1_ref, s2_ref, s3_ref, last_ref, w_ref, total_ref, whole3_ref, term3_ref = refs
    width = q_ref.shape[1]
    s3 = INV_TEMP * (s3_ref[...] + dot(last_ref[...], q_ref[...], ((1,), (1,))))
    scores = [INV_TEMP * s0_ref[...], INV_TEMP * s1_ref[...], INV_TEMP * s2_ref[...], s3]
    hard = hard_total(parts)
    largest = jnp.max(hard, axis=0, keepdims=True)
    for block in scores:
        largest = jnp.maximum(largest, jnp.max(block, axis=0, keepdims=True))
    summed = jnp.sum(jnp.exp(hard - largest), axis=0, keepdims=True)
    for block in scores:
        summed = summed + jnp.sum(jnp.exp(block - largest), axis=0, keepdims=True)
    log_total = largest + jnp.log(summed)
    total_ref[...] = log_total
    whole3_ref[...] = s3
    coef3 = (w_ref[...] * jnp.exp(s3 - log_total)).astype(BF16)
    for c in range(0, width, CHUNK):
        at = slice(c, c + CHUNK)
        term3_ref[:, at] = dot(coef3, q_ref[:, at], ((1,), (0,))).astype(BF16)


def weigh_body(groups, *refs):
    parts, refs = refs[:groups], refs[groups:]
    s0_ref, s1_ref, s2_ref, whole3_ref, total_ref, w_ref, *refs = refs
    loss_ref, coef_ref, hard_out, swap_ref = refs
    rows = s0_ref.shape[0]
    w, log_total = w_ref[...], total_ref[...]
    hard_out[...] = (w * jnp.exp(hard_total(parts) - log_total)).astype(BF16).astype(F32)
    scores = [INV_TEMP * s0_ref[...], INV_TEMP * s1_ref[...], INV_TEMP * s2_ref[...]]
    for s, block in enumerate(scores + [whole3_ref[...]]):
        coef = (w * jnp.exp(block - log_total)).astype(BF16)
        coef_ref[:, s * rows : (s + 1) * rows] = coef
        if s in (1, 2):
            swap_ref[:, (s - 1) * rows : s * rows] = coef
    eye = lax.broadcasted_iota(jnp.int32, (rows, rows), 0) == lax.broadcasted_iota(
        jnp.int32, (rows, rows), 1
    )
    loss_ref[...] = log_total - jnp.sum(jnp.where(eye, scores[0], 0.0), axis=0, keepdims=True)


def sums_body(q_ref, pair_ref, coef_ref, swap_ref, sent3, partial1, token):
    signal(token)
    rows, width = q_ref.shape
    odd = lax.axis_index("blk") % 2 == 1
    mine = jnp.where(odd, coef_ref[:, rows : 2 * rows], coef_ref[:, 3 * rows :])
    coef = jnp.concatenate([mine, swap_ref[:, rows:]], axis=1)
    for c in range(0, width, CHUNK):
        at = slice(c, c + CHUNK)
        held = jnp.concatenate([q_ref[:, at], pair_ref[:, width + c : width + c + CHUNK]], axis=0)
        total = dot(coef, held, ((1,), (0,)))
        sent3[:, at] = total.astype(BF16)
        partial1[:, at] = total


def relay_body(partial1, got3_ref, out, done):
    signal(done)
    out[...] = (partial1[...] + got3_ref[...].astype(F32)).astype(BF16)


def base_body(
    q_ref, pair_ref, p_ref, n1_ref, e3_ref, o3_ref, coef_ref, swap_ref, w_ref, own3_ref,
    token, got3_ref, pulled, base, coef_t,
):
    rows, width = q_ref.shape
    w = jnp.broadcast_to(w_ref[...], (rows, rows)).T[:, :1]
    odd = lax.axis_index("blk") % 2 == 1
    blocks = (p_ref, n1_ref, pair_ref, e3_ref, o3_ref)
    for s in range(5):
        k = min(s, 3) * rows
        coef_t[:, s * rows : (s + 1) * rows] = coef_ref[:, k : k + rows].astype(F32).T.astype(BF16)
    coef = [coef_ref[:, :rows], jnp.where(odd, swap_ref[:, :rows], jnp.zeros((rows, rows), BF16))]
    coef = jnp.concatenate(coef, axis=1)
    for c in range(0, width, CHUNK):
        at = slice(c, c + CHUNK)
        held = jnp.concatenate([block[:, at] for block in blocks], axis=0)
        pulled[:, at] = dot(coef_t[...], held, ((1,), (0,))) - w * p_ref[:, at].astype(F32)
        held = jnp.concatenate([q_ref[:, at], pair_ref[:, width + c : width + c + CHUNK]], axis=0)
        came = jnp.where(odd, 0.0, got3_ref[:, at].astype(F32)) + own3_ref[:, at].astype(F32)
        own = dot(coef, held, ((1,), (0,))) + came
        base[:, at] = own - w * q_ref[:, at].astype(F32)


def gather_body(groups, pulled, base, *refs):
    backs, (out, almost, held, sems) = refs[:groups][::-1], refs[groups:]
    rows, cols = pulled.shape[0], backs[0].shape[1]
    g = lax.axis_index("grp")
    copies = []
    for r, back in enumerate(backs):
        at = pl.ds(pl.multiple_of((g ^ r) * cols, 128), cols)
        held[:, at] = (INV_TEMP * (pulled[:, at] + back[:rows].astype(F32))).astype(BF16)
        copies.append(pltpu.make_async_copy(held.at[:, at], out.at[:, at], sems.at[r]))
        copies[-1].start()
        almost[:, at] = base[:, at] + back[rows:].astype(F32)
    for copy in copies:
        copy.wait()


def finish_body(almost, own1, out, held, sems):
    width = almost.shape[1]
    copies = []
    for n, c in enumerate(range(0, width, CHUNK)):
        at = slice(c, c + CHUNK)
        held[:, at] = (INV_TEMP * (almost[:, at] + own1[:, at].astype(F32))).astype(BF16)
        copies.append(pltpu.make_async_copy(held.at[:, at], out.at[:, at], sems.at[n]))
        copies[-1].start()
    for copy in copies:
        copy.wait()


def per_device(queries, passages, hard_index, weights):
    rows, width = queries.shape
    groups = lax.axis_size("grp")
    loop = lax.axis_size("blk")
    cols = width // groups

    def pairs_of(by, which=(0, 1)):
        return [(i, (i + by) % loop) for i in range(loop) if i % 2 in which]

    def shift(array, by, which=(0, 1)):
        return lax.ppermute(array, "blk", pairs_of(by, which))

    def swap(array):
        return lax.ppermute(array, "blk", [(i, i ^ 1) for i in range(loop)])

    def over_groups(array, r):
        return lax.ppermute(array, "grp", [(i, i ^ r) for i in range(groups)])

    def exchange(arrays):
        out = list(arrays)
        for r in reversed(range(1, groups)):
            out[r] = over_groups(arrays[r], r)
        return out

    def like(*shape, dtype=BF16):
        return jax.ShapeDtypeStruct(shape, dtype)

    block, block32 = like(rows, width), like(rows, width, dtype=F32)
    square, triple = like(rows, rows, dtype=F32), like(3, rows, dtype=F32)
    piece, back = like(2 * rows + TAIL, cols), like(2 * rows, cols)

    next1 = shift(passages, -1)

    *pieces, token = local_call(
        functools.partial(load_body, groups, loop * rows), [piece] * groups + [TOKEN],
        queries, passages, hard_index.T, in_specs=[HBM, HBM, HBM],
        scratch=[pltpu.VMEM((3, rows), jnp.int32), pltpu.SemaphoreType.DMA((2 * groups + 1,))],
        limit=51,
    )
    pieces = exchange(pieces)

    (later_p,) = local_call(pass_body, [block], passages, token)
    next3_even = shift(later_p, -3, (1,))
    (next1,) = local_call(pass_body, [block], next1, token, flops=LONG)
    next3_odd = shift(next1, -2, (1,))
    pair = swap(
        local_call(choose_body, [like(rows, 2 * width)], next1, next3_even, queries, flops=LONG)[0]
    )

    s0, s1, s3 = local_call(scores_body, [square] * 3, queries, passages, next1, next3_even)
    parts = local_call(
        functools.partial(hard_scores_body, groups), [triple] * groups, *pieces[::-1], s0, flops=LONG
    )
    (s2,) = local_call(last_score_body, [square], queries, pair)
    parts = exchange(parts)
    one_row = like(1, rows, dtype=F32)
    log_total, whole3, term3 = local_call(
        functools.partial(first_sum_body, groups), [one_row, square, block],
        *parts[::-1], queries, s0, s1, s2, s3, next3_odd, weights[None, :],
    )
    loss_rows, coef, hard_coef, to_core = local_call(
        functools.partial(weigh_body, groups),
        [one_row, like(rows, 4 * rows), triple, like(rows, 2 * rows)],
        *parts[::-1], s0, s1, s2, whole3, log_total, weights[None, :],
    )

    got3 = lax.ppermute(term3, "blk", pairs_of(2, (1,))[:-1] + [(loop - 1, 2)])
    from_core = swap(to_core)
    sent3, partial1, token = local_call(
        sums_body, [block, block32, TOKEN], queries, pair, coef, from_core
    )
    own3 = shift(sent3, 3, (0,))

    hard_coefs = exchange([hard_coef] * groups)
    square_all = pltpu.VMEM((groups * rows, groups * rows), BF16)
    *backs, token = local_call(
        functools.partial(hard_grads_body, groups), [back] * groups + [TOKEN],
        *hard_coefs, *pieces[::-1], token, scratch=[square_all, square_all],
    )
    backs = exchange(backs)

    sent1, token = local_call(relay_body, [block, TOKEN], partial1, got3, flops=SOME)
    own1 = shift(sent1, 1, (1,))

    pulled, base = local_call(
        base_body, [block32, block32],
        queries, pair, passages, next1, next3_even, next3_odd, coef, from_core,
        weights[None, :], own3, token, got3, flops=LONG, scratch=[pltpu.VMEM((rows, 5 * rows), BF16)],
    )
    held = pltpu.VMEM((rows, width), BF16)
    grad_queries, almost = local_call(
        functools.partial(gather_body, groups), [block, block32], pulled, base, *backs[::-1],
        out_specs=[HBM, VMEM], scratch=[held, pltpu.SemaphoreType.DMA((groups,))],
    )
    (grad_passages,) = local_call(
        finish_body, [block], almost, own1, out_specs=[HBM],
        scratch=[held, pltpu.SemaphoreType.DMA((width // CHUNK,))],
    )
    return loss_rows.reshape(rows), grad_queries, grad_passages


def solution(mesh):
    rows = P(("grp", "blk"))
    matrix = P(("grp", "blk"), None)
    return jax.shard_map(
        per_device,
        mesh=mesh,
        in_specs=(matrix, matrix, matrix, rows),
        out_specs=(rows, matrix, matrix),
        check_vma=False,
    )
```

```python
import functools
import math

import jax
import jax.numpy as jnp
from jax import lax
from jax.experimental import pallas as pl
from jax.experimental.pallas import tpu as pltpu
from jax.sharding import PartitionSpec as P

INV_TEMP = 50.0
BF16 = jnp.bfloat16
F32 = jnp.float32
CHUNK = 512
TAIL = 16
LONG, SOME = 5 * 10**10, 16 * 10**9
VMEM = pl.BlockSpec(memory_space=pltpu.VMEM)
HBM = pl.BlockSpec(memory_space=pltpu.HBM)
TOKEN = jax.ShapeDtypeStruct((8, 128), F32)


def dot(left, right, dims):
    return lax.dot_general(left, right, (dims, ((), ())), preferred_element_type=F32)


def size_of(arrays):
    return sum(math.prod(a.shape) * jnp.dtype(a.dtype).itemsize for a in arrays)


def local_call(body, out_shape, *args, flops=0, in_specs=None, out_specs=None, scratch=(), limit=20):
    return pl.pallas_call(
        body,
        out_shape=out_shape,
        in_specs=in_specs or [VMEM] * len(args),
        out_specs=out_specs or [VMEM] * len(out_shape),
        scratch_shapes=list(scratch),
        cost_estimate=pl.CostEstimate(
            flops=flops, bytes_accessed=size_of(args) + size_of(out_shape), transcendentals=0
        ),
        compiler_params=pltpu.CompilerParams(vmem_limit_bytes=limit * 2**20),
    )(*args)


def signal(token):
    token[...] = jnp.zeros(token.shape, token.dtype)


def split_index(index, rows, group_rows):
    if group_rows & (group_rows - 1) or rows & (rows - 1):
        return index // group_rows, index % rows
    return index >> (group_rows.bit_length() - 1), index & (rows - 1)


def load_body(groups, group_rows, q_hbm, p_hbm, index_hbm, *refs):
    pieces, (token, index_ref, sems) = refs[:groups], refs[groups:]
    rows = q_hbm.shape[0]
    cols = pieces[0].shape[1]
    g = lax.axis_index("grp")
    index_copy = pltpu.make_async_copy(index_hbm, index_ref, sems.at[2 * groups])
    index_copy.start()
    copies = []
    for r, piece in enumerate(pieces):
        at = pl.ds(pl.multiple_of((g ^ r) * cols, 128), cols)
        for n, source in enumerate((q_hbm, p_hbm)):
            target = piece.at[pl.ds(n * rows, rows)]
            copies.append(pltpu.make_async_copy(source.at[:, at], target, sems.at[2 * r + n]))
            copies[-1].start()
    signal(token)
    index_copy.wait()
    index = jnp.concatenate([index_ref[...], jnp.zeros((TAIL - 3, rows), jnp.int32)], axis=0)
    named_group, named_row = split_index(index, rows, group_rows)
    named_group = named_group.astype(F32).astype(BF16)
    named_row = named_row.astype(F32).astype(BF16)
    for piece in pieces:
        piece[2 * rows :, :rows] = named_group
        piece[2 * rows :, rows : 2 * rows] = named_row
        if cols > 2 * rows:
            piece[2 * rows :, 2 * rows :] = jnp.zeros((TAIL, cols - 2 * rows), BF16)
    for copy in copies:
        copy.wait()


def places_of(piece_ref, rows):
    tail = piece_ref[2 * rows :, : 2 * rows].astype(F32).astype(jnp.int32)
    g = lax.axis_index("grp")
    return [(tail[k : k + 1, :rows] ^ g) * rows + tail[k : k + 1, rows:] for k in range(3)]


def hard_scores_body(groups, *refs):
    pieces, outs = refs[:groups][::-1], refs[groups + 1 :]
    rows = outs[0].shape[1]
    ids = lax.broadcasted_iota(jnp.int32, (rows, rows), 0)
    for r in range(groups):
        others = [other for other in range(groups) if other != r]
        places = places_of(pieces[r], rows)
        held = jnp.concatenate([pieces[other][rows : 2 * rows] for other in others], axis=0)
        dots = dot(held, pieces[r][:rows], ((1,), (1,)))
        sums = [jnp.zeros((1, rows), F32) for _ in places]
        for n, other in enumerate(others):
            block = dots[n * rows : (n + 1) * rows]
            for k, place in enumerate(places):
                hit = jnp.where(ids == place - other * rows, block, 0.0)
                sums[k] += jnp.sum(hit, axis=0, keepdims=True)
        outs[r][...] = jnp.concatenate(sums, axis=0)


def hard_grads_body(groups, *refs):
    coefs, pieces, outs = refs[:groups], refs[groups : 2 * groups][::-1], refs[2 * groups + 1 : 3 * groups + 1]
    token, matrix, matrix_t = refs[3 * groups + 1 :]
    rows = coefs[0].shape[1]
    cols = outs[0].shape[1]
    signal(token)
    ids = lax.broadcasted_iota(jnp.int32, (groups * rows, rows), 0)
    for r in range(groups):
        places = places_of(pieces[r], rows)
        total = jnp.zeros(ids.shape, F32)
        for k in range(3):
            total += jnp.where(ids == places[k], coefs[r][k : k + 1], 0.0)
        mine = slice(r * rows, (r + 1) * rows)
        matrix[:, mine] = total.astype(BF16)
        matrix_t[mine] = total.T.astype(BF16)
    step = min(cols, 256)
    for c in range(0, cols, step):
        at = slice(c, c + step)
        q_all = jnp.concatenate([piece[:rows, at] for piece in pieces], axis=0)
        p_all = jnp.concatenate([piece[rows : 2 * rows, at] for piece in pieces], axis=0)
        grad_q = dot(matrix_t[...], p_all, ((1,), (0,))).astype(BF16)
        grad_p = dot(matrix[...], q_all, ((1,), (0,))).astype(BF16)
        for r in range(groups):
            mine = slice(r * rows, (r + 1) * rows)
            outs[r][:rows, at] = grad_q[mine]
            outs[r][rows:, at] = grad_p[mine]


def pass_body(source, token, out):
    out[...] = source[...]


def choose_body(n1_ref, e3_ref, q_ref, out):
    width = q_ref.shape[1]
    odd = lax.axis_index("blk") % 2 == 1
    out[:, width:] = q_ref[...]

    @pl.when(odd)
    def _():
        out[:, :width] = n1_ref[...]

    @pl.when(jnp.logical_not(odd))
    def _():
        out[:, :width] = e3_ref[...]


def scores_body(q_ref, *refs):
    half = len(refs) // 2
    for block, out in zip(refs[:half], refs[half:]):
        out[...] = dot(block[...], q_ref[...], ((1,), (1,)))


def last_score_body(q_ref, pair_ref, out):
    out[...] = dot(pair_ref[:, : q_ref.shape[1]], q_ref[...], ((1,), (1,)))


def hard_total(parts):
    total = parts[-1][...]
    for other in parts[-2::-1]:
        total = total + other[...]
    return INV_TEMP * total


def first_sum_body(groups, *refs):
    parts, refs = refs[:groups], refs[groups:]
    q_ref, s0_ref, s1_ref, s2_ref, s3_ref, last_ref, w_ref, total_ref, whole3_ref, term3_ref = refs
    width = q_ref.shape[1]
    s3 = INV_TEMP * (s3_ref[...] + dot(last_ref[...], q_ref[...], ((1,), (1,))))
    scores = [INV_TEMP * s0_ref[...], INV_TEMP * s1_ref[...], INV_TEMP * s2_ref[...], s3]
    hard = hard_total(parts)
    largest = jnp.max(hard, axis=0, keepdims=True)
    for block in scores:
        largest = jnp.maximum(largest, jnp.max(block, axis=0, keepdims=True))
    summed = jnp.sum(jnp.exp(hard - largest), axis=0, keepdims=True)
    for block in scores:
        summed = summed + jnp.sum(jnp.exp(block - largest), axis=0, keepdims=True)
    log_total = largest + jnp.log(summed)
    total_ref[...] = log_total
    whole3_ref[...] = s3
    coef3 = (w_ref[...] * jnp.exp(s3 - log_total)).astype(BF16)
    for c in range(0, width, CHUNK):
        at = slice(c, c + CHUNK)
        term3_ref[:, at] = dot(coef3, q_ref[:, at], ((1,), (0,))).astype(BF16)


def weigh_body(groups, *refs):
    parts, refs = refs[:groups], refs[groups:]
    s0_ref, s1_ref, s2_ref, whole3_ref, total_ref, w_ref, *refs = refs
    loss_ref, coef_ref, hard_out, swap_ref = refs
    rows = s0_ref.shape[0]
    w, log_total = w_ref[...], total_ref[...]
    hard_out[...] = (w * jnp.exp(hard_total(parts) - log_total)).astype(BF16).astype(F32)
    scores = [INV_TEMP * s0_ref[...], INV_TEMP * s1_ref[...], INV_TEMP * s2_ref[...]]
    for s, block in enumerate(scores + [whole3_ref[...]]):
        coef = (w * jnp.exp(block - log_total)).astype(BF16)
        coef_ref[:, s * rows : (s + 1) * rows] = coef
        if s in (1, 2):
            swap_ref[:, (s - 1) * rows : s * rows] = coef
    eye = lax.broadcasted_iota(jnp.int32, (rows, rows), 0) == lax.broadcasted_iota(
        jnp.int32, (rows, rows), 1
    )
    loss_ref[...] = log_total - jnp.sum(jnp.where(eye, scores[0], 0.0), axis=0, keepdims=True)


def sums_body(q_ref, pair_ref, coef_ref, swap_ref, sent3, partial1, token):
    signal(token)
    rows, width = q_ref.shape
    odd = lax.axis_index("blk") % 2 == 1
    mine = jnp.where(odd, coef_ref[:, rows : 2 * rows], coef_ref[:, 3 * rows :])
    coef = jnp.concatenate([mine, swap_ref[:, rows:]], axis=1)
    for c in range(0, width, CHUNK):
        at = slice(c, c + CHUNK)
        held = jnp.concatenate([q_ref[:, at], pair_ref[:, width + c : width + c + CHUNK]], axis=0)
        total = dot(coef, held, ((1,), (0,)))
        sent3[:, at] = total.astype(BF16)
        partial1[:, at] = total


def relay_body(partial1, got3_ref, out, done):
    signal(done)
    out[...] = (partial1[...] + got3_ref[...].astype(F32)).astype(BF16)


def base_body(
    q_ref, pair_ref, p_ref, n1_ref, e3_ref, o3_ref, coef_ref, swap_ref, w_ref, own3_ref,
    token, got3_ref, pulled, base, coef_t,
):
    rows, width = q_ref.shape
    w = jnp.broadcast_to(w_ref[...], (rows, rows)).T[:, :1]
    odd = lax.axis_index("blk") % 2 == 1
    blocks = (p_ref, n1_ref, pair_ref, e3_ref, o3_ref)
    for s in range(5):
        k = min(s, 3) * rows
        coef_t[:, s * rows : (s + 1) * rows] = coef_ref[:, k : k + rows].astype(F32).T.astype(BF16)
    coef = [coef_ref[:, :rows], jnp.where(odd, swap_ref[:, :rows], jnp.zeros((rows, rows), BF16))]
    coef = jnp.concatenate(coef, axis=1)
    for c in range(0, width, CHUNK):
        at = slice(c, c + CHUNK)
        held = jnp.concatenate([block[:, at] for block in blocks], axis=0)
        pulled[:, at] = dot(coef_t[...], held, ((1,), (0,))) - w * p_ref[:, at].astype(F32)
        held = jnp.concatenate([q_ref[:, at], pair_ref[:, width + c : width + c + CHUNK]], axis=0)
        came = jnp.where(odd, 0.0, got3_ref[:, at].astype(F32)) + own3_ref[:, at].astype(F32)
        own = dot(coef, held, ((1,), (0,))) + came
        base[:, at] = own - w * q_ref[:, at].astype(F32)


def gather_body(groups, pulled, base, *refs):
    backs, (out, almost, held, sems) = refs[:groups][::-1], refs[groups:]
    rows, cols = pulled.shape[0], backs[0].shape[1]
    g = lax.axis_index("grp")
    copies = []
    for r, back in enumerate(backs):
        at = pl.ds(pl.multiple_of((g ^ r) * cols, 128), cols)
        held[:, at] = (INV_TEMP * (pulled[:, at] + back[:rows].astype(F32))).astype(BF16)
        copies.append(pltpu.make_async_copy(held.at[:, at], out.at[:, at], sems.at[r]))
        copies[-1].start()
        almost[:, at] = base[:, at] + back[rows:].astype(F32)
    for copy in copies:
        copy.wait()


def finish_body(almost, own1, out, held, sems):
    width = almost.shape[1]
    copies = []
    for n, c in enumerate(range(0, width, CHUNK)):
        at = slice(c, c + CHUNK)
        held[:, at] = (INV_TEMP * (almost[:, at] + own1[:, at].astype(F32))).astype(BF16)
        copies.append(pltpu.make_async_copy(held.at[:, at], out.at[:, at], sems.at[n]))
        copies[-1].start()
    for copy in copies:
        copy.wait()


def per_device(queries, passages, hard_index, weights):
    rows, width = queries.shape
    groups = lax.axis_size("grp")
    loop = lax.axis_size("blk")
    cols = width // groups

    def pairs_of(by, which=(0, 1)):
        return [(i, (i + by) % loop) for i in range(loop) if i % 2 in which]

    def shift(array, by, which=(0, 1)):
        return lax.ppermute(array, "blk", pairs_of(by, which))

    def swap(array):
        return lax.ppermute(array, "blk", [(i, i ^ 1) for i in range(loop)])

    def over_groups(array, r):
        return lax.ppermute(array, "grp", [(i, i ^ r) for i in range(groups)])

    def exchange(arrays):
        out = list(arrays)
        for r in reversed(range(1, groups)):
            out[r] = over_groups(arrays[r], r)
        return out

    def like(*shape, dtype=BF16):
        return jax.ShapeDtypeStruct(shape, dtype)

    block, block32 = like(rows, width), like(rows, width, dtype=F32)
    square, triple = like(rows, rows, dtype=F32), like(3, rows, dtype=F32)
    piece, back = like(2 * rows + TAIL, cols), like(2 * rows, cols)

    next1 = shift(passages, -1)

    *pieces, token = local_call(
        functools.partial(load_body, groups, loop * rows), [piece] * groups + [TOKEN],
        queries, passages, hard_index.T, in_specs=[HBM, HBM, HBM],
        scratch=[pltpu.VMEM((3, rows), jnp.int32), pltpu.SemaphoreType.DMA((2 * groups + 1,))],
        limit=51,
    )
    pieces = exchange(pieces)

    (later_p,) = local_call(pass_body, [block], passages, token)
    next3_even = shift(later_p, -3, (1,))
    (next1,) = local_call(pass_body, [block], next1, token, flops=LONG)
    next3_odd = shift(next1, -2, (1,))
    pair = swap(
        local_call(choose_body, [like(rows, 2 * width)], next1, next3_even, queries, flops=LONG)[0]
    )

    s0, s1, s3 = local_call(scores_body, [square] * 3, queries, passages, next1, next3_even)
    parts = local_call(
        functools.partial(hard_scores_body, groups), [triple] * groups, *pieces[::-1], s0, flops=LONG
    )
    (s2,) = local_call(last_score_body, [square], queries, pair)
    parts = exchange(parts)
    one_row = like(1, rows, dtype=F32)
    log_total, whole3, term3 = local_call(
        functools.partial(first_sum_body, groups), [one_row, square, block],
        *parts[::-1], queries, s0, s1, s2, s3, next3_odd, weights[None, :],
    )
    loss_rows, coef, hard_coef, to_core = local_call(
        functools.partial(weigh_body, groups),
        [one_row, like(rows, 4 * rows), triple, like(rows, 2 * rows)],
        *parts[::-1], s0, s1, s2, whole3, log_total, weights[None, :],
    )

    got3 = lax.ppermute(term3, "blk", pairs_of(2, (1,))[:-1] + [(loop - 1, 2)])
    from_core = swap(to_core)
    sent3, partial1, token = local_call(
        sums_body, [block, block32, TOKEN], queries, pair, coef, from_core
    )
    own3 = shift(sent3, 3, (0,))

    hard_coefs = exchange([hard_coef] * groups)
    square_all = pltpu.VMEM((groups * rows, groups * rows), BF16)
    *backs, token = local_call(
        functools.partial(hard_grads_body, groups), [back] * groups + [TOKEN],
        *hard_coefs, *pieces[::-1], token, scratch=[square_all, square_all],
    )
    backs = exchange(backs)

    sent1, token = local_call(relay_body, [block, TOKEN], partial1, got3, flops=SOME)
    own1 = shift(sent1, 1, (1,))

    pulled, base = local_call(
        base_body, [block32, block32],
        queries, pair, passages, next1, next3_even, next3_odd, coef, from_core,
        weights[None, :], own3, token, got3, flops=LONG, scratch=[pltpu.VMEM((rows, 5 * rows), BF16)],
    )
    held = pltpu.VMEM((rows, width), BF16)
    grad_queries, almost = local_call(
        functools.partial(gather_body, groups), [block, block32], pulled, base, *backs[::-1],
        out_specs=[HBM, VMEM], scratch=[held, pltpu.SemaphoreType.DMA((groups,))],
    )
    (grad_passages,) = local_call(
        finish_body, [block], almost, own1, out_specs=[HBM],
        scratch=[held, pltpu.SemaphoreType.DMA((width // CHUNK,))],
    )
    return loss_rows.reshape(rows), grad_queries, grad_passages


def solution(mesh):
    rows = P(("grp", "blk"))
    matrix = P(("grp", "blk"), None)
    return jax.shard_map(
        per_device,
        mesh=mesh,
        in_specs=(matrix, matrix, matrix, rows),
        out_specs=(rows, matrix, matrix),
        check_vma=False,
    )
```

```python
import functools
import math

import jax
import jax.numpy as jnp
from jax import lax
from jax.experimental import pallas as pl
from jax.experimental.pallas import tpu as pltpu
from jax.sharding import PartitionSpec as P

INV_TEMP = 50.0
BF16 = jnp.bfloat16
F32 = jnp.float32
CHUNK = 512
TAIL = 16
LONG, SOME = 5 * 10**10, 16 * 10**9
VMEM = pl.BlockSpec(memory_space=pltpu.VMEM)
HBM = pl.BlockSpec(memory_space=pltpu.HBM)
TOKEN = jax.ShapeDtypeStruct((8, 128), F32)


def dot(left, right, dims):
    return lax.dot_general(left, right, (dims, ((), ())), preferred_element_type=F32)


def size_of(arrays):
    return sum(math.prod(a.shape) * jnp.dtype(a.dtype).itemsize for a in arrays)


def local_call(body, out_shape, *args, flops=0, in_specs=None, out_specs=None, scratch=(), limit=20):
    return pl.pallas_call(
        body,
        out_shape=out_shape,
        in_specs=in_specs or [VMEM] * len(args),
        out_specs=out_specs or [VMEM] * len(out_shape),
        scratch_shapes=list(scratch),
        cost_estimate=pl.CostEstimate(
            flops=flops, bytes_accessed=size_of(args) + size_of(out_shape), transcendentals=0
        ),
        compiler_params=pltpu.CompilerParams(vmem_limit_bytes=limit * 2**20),
    )(*args)


def signal(token):
    token[...] = jnp.zeros(token.shape, token.dtype)


def split_index(index, rows, group_rows):
    if group_rows & (group_rows - 1) or rows & (rows - 1):
        return index // group_rows, index % rows
    return index >> (group_rows.bit_length() - 1), index & (rows - 1)


def load_body(groups, group_rows, q_hbm, p_hbm, index_hbm, *refs):
    pieces, (token, index_ref, sems) = refs[:groups], refs[groups:]
    rows = q_hbm.shape[0]
    cols = pieces[0].shape[1]
    g = lax.axis_index("grp")
    index_copy = pltpu.make_async_copy(index_hbm, index_ref, sems.at[2 * groups])
    index_copy.start()
    copies = []
    for r, piece in enumerate(pieces):
        at = pl.ds(pl.multiple_of((g ^ r) * cols, 128), cols)
        for n, source in enumerate((q_hbm, p_hbm)):
            target = piece.at[pl.ds(n * rows, rows)]
            copies.append(pltpu.make_async_copy(source.at[:, at], target, sems.at[2 * r + n]))
            copies[-1].start()
    signal(token)
    index_copy.wait()
    index = jnp.concatenate([index_ref[...], jnp.zeros((TAIL - 3, rows), jnp.int32)], axis=0)
    named_group, named_row = split_index(index, rows, group_rows)
    named_group = named_group.astype(F32).astype(BF16)
    named_row = named_row.astype(F32).astype(BF16)
    for piece in pieces:
        piece[2 * rows :, :rows] = named_group
        piece[2 * rows :, rows : 2 * rows] = named_row
        if cols > 2 * rows:
            piece[2 * rows :, 2 * rows :] = jnp.zeros((TAIL, cols - 2 * rows), BF16)
    for copy in copies:
        copy.wait()


def places_of(piece_ref, rows):
    tail = piece_ref[2 * rows :, : 2 * rows].astype(F32).astype(jnp.int32)
    g = lax.axis_index("grp")
    return [(tail[k : k + 1, :rows] ^ g) * rows + tail[k : k + 1, rows:] for k in range(3)]


def hard_scores_body(groups, *refs):
    pieces, outs = [*refs[2 : groups + 1][::-1], refs[0]], refs[groups + 1 :]
    rows = outs[0].shape[1]
    ids = lax.broadcasted_iota(jnp.int32, (rows, rows), 0)
    for r in range(groups):
        others = [other for other in range(groups) if other != r]
        places = places_of(pieces[r], rows)
        held = jnp.concatenate([pieces[other][rows : 2 * rows] for other in others], axis=0)
        dots = dot(held, pieces[r][:rows], ((1,), (1,)))
        sums = [jnp.zeros((1, rows), F32) for _ in places]
        for n, other in enumerate(others):
            block = dots[n * rows : (n + 1) * rows]
            for k, place in enumerate(places):
                hit = jnp.where(ids == place - other * rows, block, 0.0)
                sums[k] += jnp.sum(hit, axis=0, keepdims=True)
        outs[r][...] = jnp.concatenate(sums, axis=0)


def hard_grads_body(groups, *refs):
    coefs, pieces, outs = refs[:groups][::-1], refs[groups : 2 * groups][::-1], refs[2 * groups + 1 : 3 * groups + 1]
    token, matrix, matrix_t = refs[3 * groups + 1 :]
    rows = coefs[0].shape[1]
    cols = outs[0].shape[1]
    signal(token)
    ids = lax.broadcasted_iota(jnp.int32, (groups * rows, rows), 0)
    for r in range(groups):
        places = places_of(pieces[r], rows)
        total = jnp.zeros(ids.shape, F32)
        for k in range(3):
            total += jnp.where(ids == places[k], coefs[r][k : k + 1], 0.0)
        mine = slice(r * rows, (r + 1) * rows)
        matrix[:, mine] = total.astype(BF16)
        matrix_t[mine] = total.T.astype(BF16)
    step = min(cols, 256)
    for c in range(0, cols, step):
        at = slice(c, c + step)
        q_all = jnp.concatenate([piece[:rows, at] for piece in pieces], axis=0)
        p_all = jnp.concatenate([piece[rows : 2 * rows, at] for piece in pieces], axis=0)
        grad_q = dot(matrix_t[...], p_all, ((1,), (0,))).astype(BF16)
        grad_p = dot(matrix[...], q_all, ((1,), (0,))).astype(BF16)
        for r in range(groups):
            mine = slice(r * rows, (r + 1) * rows)
            outs[r][:rows, at] = grad_q[mine]
            outs[r][rows:, at] = grad_p[mine]


def pass_body(source, token, out):
    out[...] = source[...]


def choose_body(n1_ref, e3_ref, q_ref, out):
    width = q_ref.shape[1]
    odd = lax.axis_index("blk") % 2 == 1
    out[:, width:] = q_ref[...]

    @pl.when(odd)
    def _():
        out[:, :width] = n1_ref[...]

    @pl.when(jnp.logical_not(odd))
    def _():
        out[:, :width] = e3_ref[...]


def scores_body(q_ref, *refs):
    half = len(refs) // 2
    for block, out in zip(refs[:half], refs[half:]):
        out[...] = dot(block[...], q_ref[...], ((1,), (1,)))


def last_score_body(q_ref, pair_ref, out):
    out[...] = dot(pair_ref[:, : q_ref.shape[1]], q_ref[...], ((1,), (1,)))


def hard_total(parts):
    total = parts[-1][...]
    for other in parts[-2::-1]:
        total = total + other[...]
    return INV_TEMP * total


def first_sum_body(groups, *refs):
    parts, refs = refs[:groups], refs[groups:]
    q_ref, s0_ref, s1_ref, s2_ref, s3_ref, last_ref, w_ref, total_ref, whole3_ref, term3_ref = refs
    width = q_ref.shape[1]
    s3 = INV_TEMP * (s3_ref[...] + dot(last_ref[...], q_ref[...], ((1,), (1,))))
    scores = [INV_TEMP * s0_ref[...], INV_TEMP * s1_ref[...], INV_TEMP * s2_ref[...], s3]
    hard = hard_total(parts)
    largest = jnp.max(hard, axis=0, keepdims=True)
    for block in scores:
        largest = jnp.maximum(largest, jnp.max(block, axis=0, keepdims=True))
    summed = jnp.sum(jnp.exp(hard - largest), axis=0, keepdims=True)
    for block in scores:
        summed = summed + jnp.sum(jnp.exp(block - largest), axis=0, keepdims=True)
    log_total = largest + jnp.log(summed)
    total_ref[...] = log_total
    whole3_ref[...] = s3
    coef3 = (w_ref[...] * jnp.exp(s3 - log_total)).astype(BF16)
    for c in range(0, width, CHUNK):
        at = slice(c, c + CHUNK)
        term3_ref[:, at] = dot(coef3, q_ref[:, at], ((1,), (0,))).astype(BF16)


def weigh_body(groups, *refs):
    parts, refs = refs[:groups], refs[groups:]
    s0_ref, s1_ref, s2_ref, whole3_ref, total_ref, w_ref, *refs = refs
    loss_ref, coef_ref, hard_out, swap_ref = refs
    rows = s0_ref.shape[0]
    w, log_total = w_ref[...], total_ref[...]
    hard_out[...] = (w * jnp.exp(hard_total(parts) - log_total)).astype(BF16).astype(F32)
    scores = [INV_TEMP * s0_ref[...], INV_TEMP * s1_ref[...], INV_TEMP * s2_ref[...]]
    for s, block in enumerate(scores + [whole3_ref[...]]):
        coef = (w * jnp.exp(block - log_total)).astype(BF16)
        coef_ref[:, s * rows : (s + 1) * rows] = coef
        if s in (1, 2):
            swap_ref[:, (s - 1) * rows : s * rows] = coef
    eye = lax.broadcasted_iota(jnp.int32, (rows, rows), 0) == lax.broadcasted_iota(
        jnp.int32, (rows, rows), 1
    )
    loss_ref[...] = log_total - jnp.sum(jnp.where(eye, scores[0], 0.0), axis=0, keepdims=True)


def sums_body(q_ref, pair_ref, coef_ref, swap_ref, sent3, partial1, token):
    signal(token)
    rows, width = q_ref.shape
    odd = lax.axis_index("blk") % 2 == 1
    mine = jnp.where(odd, coef_ref[:, rows : 2 * rows], coef_ref[:, 3 * rows :])
    coef = jnp.concatenate([mine, swap_ref[:, rows:]], axis=1)
    for c in range(0, width, CHUNK):
        at = slice(c, c + CHUNK)
        held = jnp.concatenate([q_ref[:, at], pair_ref[:, width + c : width + c + CHUNK]], axis=0)
        total = dot(coef, held, ((1,), (0,)))
        sent3[:, at] = total.astype(BF16)
        partial1[:, at] = total


def relay_body(partial1, got3_ref, out, done):
    signal(done)
    out[...] = (partial1[...] + got3_ref[...].astype(F32)).astype(BF16)


def base_body(
    q_ref, pair_ref, p_ref, n1_ref, e3_ref, o3_ref, coef_ref, swap_ref, w_ref, own3_ref,
    token, pulled, base, coef_t,
):
    rows, width = q_ref.shape
    w = jnp.broadcast_to(w_ref[...], (rows, rows)).T[:, :1]
    odd = lax.axis_index("blk") % 2 == 1
    blocks = (p_ref, n1_ref, pair_ref, e3_ref, o3_ref)
    for s in range(5):
        k = min(s, 3) * rows
        coef_t[:, s * rows : (s + 1) * rows] = coef_ref[:, k : k + rows].astype(F32).T.astype(BF16)
    coef = [coef_ref[:, :rows], jnp.where(odd, swap_ref[:, :rows], jnp.zeros((rows, rows), BF16))]
    coef = jnp.concatenate(coef, axis=1)
    for c in range(0, width, CHUNK):
        at = slice(c, c + CHUNK)
        held = jnp.concatenate([block[:, at] for block in blocks], axis=0)
        pulled[:, at] = dot(coef_t[...], held, ((1,), (0,))) - w * p_ref[:, at].astype(F32)
        held = jnp.concatenate([q_ref[:, at], pair_ref[:, width + c : width + c + CHUNK]], axis=0)
        own = dot(coef, held, ((1,), (0,))) + own3_ref[:, at].astype(F32)
        base[:, at] = own - w * q_ref[:, at].astype(F32)


def gather_body(groups, pulled, base, *refs):
    backs, (out, almost, held, sems) = refs[:groups][::-1], refs[groups:]
    rows, cols = pulled.shape[0], backs[0].shape[1]
    g = lax.axis_index("grp")
    copies = []
    for r, back in enumerate(backs):
        at = pl.ds(pl.multiple_of((g ^ r) * cols, 128), cols)
        held[:, at] = (INV_TEMP * (pulled[:, at] + back[:rows].astype(F32))).astype(BF16)
        copies.append(pltpu.make_async_copy(held.at[:, at], out.at[:, at], sems.at[r]))
        copies[-1].start()
        almost[:, at] = base[:, at] + back[rows:].astype(F32)
    for copy in copies:
        copy.wait()


def finish_body(almost, own1, out, held, sems):
    width = almost.shape[1]
    copies = []
    for n, c in enumerate(range(0, width, CHUNK)):
        at = slice(c, c + CHUNK)
        held[:, at] = (INV_TEMP * (almost[:, at] + own1[:, at].astype(F32))).astype(BF16)
        copies.append(pltpu.make_async_copy(held.at[:, at], out.at[:, at], sems.at[n]))
        copies[-1].start()
    for copy in copies:
        copy.wait()


def per_device(queries, passages, hard_index, weights):
    rows, width = queries.shape
    groups = lax.axis_size("grp")
    loop = lax.axis_size("blk")
    cols = width // groups

    def shift(array, by, which=(0, 1)):
        pairs = [(i, (i + by) % loop) for i in range(loop) if i % 2 in which]
        return lax.ppermute(array, "blk", pairs)

    def swap(array):
        return lax.ppermute(array, "blk", [(i, i ^ 1) for i in range(loop)])

    def over_groups(array, r):
        return lax.ppermute(array, "grp", [(i, i ^ r) for i in range(groups)])

    def exchange(arrays):
        out = list(arrays)
        for r in reversed(range(1, groups)):
            out[r] = over_groups(arrays[r], r)
        return out

    def like(*shape, dtype=BF16):
        return jax.ShapeDtypeStruct(shape, dtype)

    block, block32 = like(rows, width), like(rows, width, dtype=F32)
    square, triple = like(rows, rows, dtype=F32), like(3, rows, dtype=F32)
    piece, back = like(2 * rows + TAIL, cols), like(2 * rows, cols)

    next1 = shift(passages, -1)

    *pieces, token = local_call(
        functools.partial(load_body, groups, loop * rows), [piece] * groups + [TOKEN],
        queries, passages, hard_index.T, in_specs=[HBM, HBM, HBM],
        scratch=[pltpu.VMEM((3, rows), jnp.int32), pltpu.SemaphoreType.DMA((2 * groups + 1,))],
        limit=51,
    )
    pieces = exchange(pieces)

    (later_p,) = local_call(pass_body, [block], passages, token)
    next3_even = shift(later_p, -3, (1,))
    (next1,) = local_call(pass_body, [block], next1, token, flops=LONG)
    next3_odd = shift(next1, -2, (1,))
    pair = swap(
        local_call(choose_body, [like(rows, 2 * width)], next1, next3_even, queries, flops=LONG)[0]
    )

    s0, s1, s3 = local_call(scores_body, [square] * 3, queries, passages, next1, next3_even)
    parts = local_call(
        functools.partial(hard_scores_body, groups), [triple] * groups, pieces[-1], s0, *pieces[-2::-1], flops=LONG
    )
    (s2,) = local_call(last_score_body, [square], queries, pair)
    parts = exchange(parts)
    one_row = like(1, rows, dtype=F32)
    log_total, whole3, term3 = local_call(
        functools.partial(first_sum_body, groups), [one_row, square, block],
        *parts[::-1], queries, s0, s1, s2, s3, next3_odd, weights[None, :],
    )
    loss_rows, coef, hard_coef, to_core = local_call(
        functools.partial(weigh_body, groups),
        [one_row, like(rows, 4 * rows), triple, like(rows, 2 * rows)],
        *parts[::-1], s0, s1, s2, whole3, log_total, weights[None, :],
    )

    got3 = shift(term3, 2, (1,))
    from_core = swap(to_core)
    sent3, partial1, token = local_call(
        sums_body, [block, block32, TOKEN], queries, pair, coef, from_core
    )
    own3 = shift(sent3, 3, (0,))

    hard_coefs = exchange([hard_coef] * groups)
    square_all = pltpu.VMEM((groups * rows, groups * rows), BF16)
    *backs, token = local_call(
        functools.partial(hard_grads_body, groups), [back] * groups + [TOKEN],
        *hard_coefs[::-1], *pieces[::-1], token, scratch=[square_all, square_all],
    )
    backs = exchange(backs)

    sent1, token = local_call(relay_body, [block, TOKEN], partial1, got3, flops=SOME)
    own1 = shift(sent1, 1, (1,))

    pulled, base = local_call(
        base_body, [block32, block32],
        queries, pair, passages, next1, next3_even, next3_odd, coef, from_core,
        weights[None, :], own3, token, flops=LONG, scratch=[pltpu.VMEM((rows, 5 * rows), BF16)],
    )
    held = pltpu.VMEM((rows, width), BF16)
    grad_queries, almost = local_call(
        functools.partial(gather_body, groups), [block, block32], pulled, base, *backs[::-1],
        out_specs=[HBM, VMEM], scratch=[held, pltpu.SemaphoreType.DMA((groups,))],
    )
    (grad_passages,) = local_call(
        finish_body, [block], almost, own1, out_specs=[HBM],
        scratch=[held, pltpu.SemaphoreType.DMA((width // CHUNK,))],
    )
    return loss_rows.reshape(rows), grad_queries, grad_passages


def solution(mesh):
    rows = P(("grp", "blk"))
    matrix = P(("grp", "blk"), None)
    return jax.shard_map(
        per_device,
        mesh=mesh,
        in_specs=(matrix, matrix, matrix, rows),
        out_specs=(rows, matrix, matrix),
        check_vma=False,
    )
```
